32 devices in a mesh: seq: 16 (over z, x, core), grp: 2 (over y).
Axes of the slice: x: 2, y: 2, z: 4, core: 2. Of those that a mesh axis runs over, the one named last changes fastest.
Arguments:
- tokens: bfloat16 [4, 4096, 768], P('grp', 'seq'), may hold values from -6 to 6
- weight_qkv: bfloat16 [768, 2304], replicated, may hold values from -0.21875 to 0.21875
- bias_query: float32 [768], replicated, may hold values from -1.75 to 1.75
- bias_value: float32 [768], replicated, may hold values from -1.75 to 1.75
- weight_score: bfloat16 [768, 12], replicated, may hold values from -0.21875 to 0.21875
- weight_out: bfloat16 [768, 768], replicated, may hold values from -0.625 to 0.625
- bias_out: float32 [768], replicated, may hold values from -1.75 to 1.75
- gain_one: float32 [768], replicated, may hold values from 0.5 to 1.5
- shift_one: float32 [768], replicated, may hold values from -1.75 to 1.75
- gain_two: float32 [768], replicated, may hold values from 0.5 to 1.5
- shift_two: float32 [768], replicated, may hold values from -1.75 to 1.75
- weight_up: bfloat16 [768, 3072], replicated, may hold values from -0.21875 to 0.21875
- bias_up: float32 [3072], replicated, may hold values from -1.75 to 1.75
- weight_down: bfloat16 [3072, 768], replicated, may hold values from -0.109375 to 0.109375
- bias_down: float32 [768], replicated, may hold values from -1.75 to 1.75
- cotangent: bfloat16 [4, 4096, 768], P('grp', 'seq'), may hold values from -6 to 6
- lengths: int32 [4], P('grp'), may hold values from 512 to 4096, as said below
- candidates: int32 [4, 16, 32], P('grp'), may hold values from 0 to 255, as said below
- selected: int32 [4, 64, 64], P('grp', 'seq'), may hold values from 0 to 511, as said below
Outputs:
- mixed: bfloat16 [4, 4096, 768], P('grp', 'seq')
- grad_tokens: float32 [4, 4096, 768], P('grp', 'seq')
- grad_qkv: float32 [768, 2304], P('seq')
- grad_bias_query: float32 [768], P('seq')
- grad_bias_value: float32 [768], P('seq')
- grad_score: float32 [768, 12], P('seq')
- grad_out: float32 [768, 768], P('seq')
- grad_bias_out: float32 [768], P('seq')
- grad_gain_one: float32 [768], P('seq')
- grad_shift_one: float32 [768], P('seq')
- grad_gain_two: float32 [768], P('seq')
- grad_shift_two: float32 [768], P('seq')
- grad_up: float32 [768, 3072], P('seq')
- grad_bias_up: float32 [3072], P('seq')
- grad_down: float32 [3072, 768], P('seq')
- grad_bias_down: float32 [768], P('seq')
The draws below stay inside these ranges and needn't reach their ends.
Inputs may be any that keep to these rules, and one draw needn't show every extreme that they name: `lengths`: in each group of 2 consecutive sequences one, chosen at random, has length 4096. `candidates`: distinct within each sequence and device block. `selected`: the 64 entries of a query block are distinct candidates of its sequence.
All inputs are finite; a program needn't handle non-finite values.
Results may differ from the reference program's by a relative error of at most 0.012.
Values may be sent and summed in bfloat16 or wider, within the bound.
A program may use at most 256 MiB of HBM per device.

```python
import jax
import jax.numpy as jnp
from jax import lax

D = 768
HEADS = 12
HEAD = 64
FF = 3072
WIN = 64
KSEL = 64
KC = 32
TOK = 256
SEQS_GRP = 2
SEQ_LEN = 4096
SEQS = 4
BLOCKS = 64
CANDS = 512
N_SEQ = 16


def draw_lengths(key, part):
    key = jax.random.fold_in(key, 11)
    first_key, second_key = jax.random.split(key)
    drawn = jax.random.randint(first_key, (SEQS,), SEQ_LEN // 8, SEQ_LEN + 1)
    chosen = jax.random.randint(second_key, (SEQS // SEQS_GRP,), 0, SEQS_GRP)
    full_one = jnp.arange(SEQS) % SEQS_GRP == jnp.repeat(chosen, SEQS_GRP)
    return jnp.where(full_one, SEQ_LEN, drawn).astype(jnp.int32)


def draw_candidates(key, part):
    key = jax.random.fold_in(key, 23)
    raw = jax.random.randint(key, (SEQS, N_SEQ, TOK), 0, 2 ** 20)
    keyed = raw * TOK + jnp.arange(TOK)
    return lax.top_k(keyed, KC)[1].astype(jnp.int32)


def draw_selected(key, part):
    key = jax.random.fold_in(key, 37)
    raw = jax.random.randint(key, (SEQS, BLOCKS, CANDS), 0, 2 ** 20)
    keyed = raw * CANDS + jnp.arange(CANDS)
    return lax.top_k(keyed, KSEL)[1].astype(jnp.int32)


def block_scale(key, extent, pieces, low, high):
    loudness = 1.0
    for position, parts in pieces:
        draws = jax.random.uniform(jax.random.fold_in(jax.random.fold_in(key, 6), position), (parts,), jnp.float32, low / len(pieces), high / len(pieces))
        loudness = loudness * jnp.repeat(jnp.exp(draws), extent[position] // parts).reshape((-1,) + (1,) * (len(extent) - 1 - position))
    return loudness


def gaussian(stream_key, shape, scale, reach, pieces=(), held_as=jnp.bfloat16):
    values = scale * jax.random.normal(stream_key, shape, jnp.float32)
    if pieces:
        values = values * block_scale(stream_key, shape, pieces, -0.22, 0.18)
    return jnp.clip(values, -reach, reach).astype(held_as)


def setup_inputs(seed: int = 0) -> dict:
    seeds = jax.random.split(jax.random.key(seed), 20)
    tokens = gaussian(seeds[0], (SEQS, SEQ_LEN, D), 1.0, 6.0, ((0, 2), (1, 16)))
    weight_qkv = gaussian(seeds[1], (D, 3 * D), D ** -0.5, 0.21875)
    bias_query = gaussian(seeds[2], (D,), 0.3, 1.75, (), jnp.float32)
    bias_value = gaussian(seeds[3], (D,), 0.3, 1.75, (), jnp.float32)
    weight_score = gaussian(seeds[4], (D, HEADS), D ** -0.5, 0.21875)
    weight_out = gaussian(seeds[5], (D, D), (D // 8) ** -0.5, 0.625)
    bias_out = gaussian(seeds[6], (D,), 0.3, 1.75, (), jnp.float32)
    gain_one = jnp.clip(1.0 + 0.1 * jax.random.normal(seeds[7], (D,), jnp.float32), 0.5, 1.5)
    shift_one = gaussian(seeds[8], (D,), 0.3, 1.75, (), jnp.float32)
    gain_two = jnp.clip(1.0 + 0.1 * jax.random.normal(seeds[9], (D,), jnp.float32), 0.5, 1.5)
    shift_two = gaussian(seeds[10], (D,), 0.3, 1.75, (), jnp.float32)
    weight_up = gaussian(seeds[11], (D, FF), D ** -0.5, 0.21875)
    bias_up = gaussian(seeds[12], (FF,), 0.3, 1.75, (), jnp.float32)
    weight_down = gaussian(seeds[13], (FF, D), FF ** -0.5, 0.109375)
    bias_down = gaussian(seeds[14], (D,), 0.3, 1.75, (), jnp.float32)
    cotangent = gaussian(seeds[15], (SEQS, SEQ_LEN, D), 1.0, 6.0, ((0, 2), (1, 16)))
    lengths = draw_lengths(jax.random.fold_in(seeds[19], 71), 0)
    candidates = draw_candidates(jax.random.fold_in(seeds[19], 71), 0)
    selected = draw_selected(jax.random.fold_in(seeds[19], 71), 0)
    return dict(tokens=tokens, weight_qkv=weight_qkv, bias_query=bias_query, bias_value=bias_value, weight_score=weight_score, weight_out=weight_out, bias_out=bias_out, gain_one=gain_one, shift_one=shift_one, gain_two=gain_two, shift_two=shift_two, weight_up=weight_up, bias_up=bias_up, weight_down=weight_down, bias_down=bias_down, cotangent=cotangent, lengths=lengths, candidates=candidates, selected=selected)


@jax.custom_vjp
def low(v):
    return lax.optimization_barrier(v.astype(jnp.bfloat16)).astype(jnp.float32)

@jax.custom_vjp
def low_back(v):
    return v

def low_keep(v):
    return (low(v), None)

def low_pass(kept, grad):
    return (grad,)

def back_keep(v):
    return (v, None)

def back_low(kept, grad):
    return (low(grad),)
low.defvjp(low_keep, low_pass)
low_back.defvjp(back_keep, back_low)
HIGHEST = lax.Precision.HIGHEST
NEG_FILL = -1e+30

def layer_norm(values, gain, shift):
    center = values - lax.optimization_barrier(jnp.mean(values, axis=-1, keepdims=True))
    spread = lax.optimization_barrier(jnp.mean(center * center, axis=-1, keepdims=True))
    return center * lax.rsqrt(spread + 1e-05) * gain + shift

def forward(inputs, weight_qkv, bias_query, bias_value, weight_score, weight_out, bias_out, gain_one, shift_one, gain_two, shift_two, weight_up, bias_up, weight_down, bias_down, length, cand_rows, select_rows):
    blocks = SEQ_LEN // WIN
    score_scale = HEAD ** (-0.5)
    normed = low(layer_norm(inputs, gain_one, shift_one))
    packed = jnp.dot(normed, weight_qkv, precision=HIGHEST)
    queries = low_back(low(packed[:, :D] + bias_query))
    key_rows = low_back(low(packed[:, D:2 * D]))
    value_rows = low_back(low(packed[:, 2 * D:] + bias_value))
    scores = low_back(low(jnp.dot(normed, weight_score, precision=HIGHEST)))
    gates = -jax.nn.softplus(-scores)
    query_blocks = queries.reshape(blocks, WIN, HEADS, HEAD)
    filler = jnp.zeros((WIN, D), jnp.float32)
    key_pad = jnp.concatenate([filler, key_rows], 0)
    value_pad = jnp.concatenate([filler, value_rows], 0)
    key_win = jnp.concatenate([key_pad[:SEQ_LEN].reshape(blocks, WIN, HEADS, HEAD), key_pad[WIN:].reshape(blocks, WIN, HEADS, HEAD)], 1)
    value_win = jnp.concatenate([value_pad[:SEQ_LEN].reshape(blocks, WIN, HEADS, HEAD), value_pad[WIN:].reshape(blocks, WIN, HEADS, HEAD)], 1)
    block_first = jnp.arange(blocks, dtype=jnp.int32) * WIN
    query_off = jnp.arange(WIN, dtype=jnp.int32)
    key_off = jnp.arange(2 * WIN, dtype=jnp.int32)
    key_pos = block_first[:, None, None] - WIN + key_off[None, None, :]
    query_pos = block_first[:, None, None] + query_off[None, :, None]
    in_window = (key_off[None, None, :] > query_off[None, :, None]) & (key_off[None, None, :] <= query_off[None, :, None] + WIN) & (key_pos >= 0)
    win_mask = in_window & ((key_pos < length) | (key_pos == query_pos))
    cand_pos = ((jnp.arange(N_SEQ, dtype=jnp.int32) * TOK)[:, None] + cand_rows).reshape(-1)
    sel_pos = cand_pos[select_rows]
    sel_mask = (sel_pos <= block_first[:, None] - WIN) & (sel_pos < length)
    key_sel = key_rows[sel_pos].reshape(blocks, KSEL, HEADS, HEAD)
    value_sel = value_rows[sel_pos].reshape(blocks, KSEL, HEADS, HEAD)
    gate_sel = gates[sel_pos]
    logit_win = jnp.einsum('bqhd,bkhd->bhqk', query_blocks, key_win, precision=HIGHEST) * score_scale
    logit_sel = jnp.einsum('bqhd,bkhd->bhqk', query_blocks, key_sel, precision=HIGHEST) * score_scale
    logit_sel = logit_sel + jnp.transpose(gate_sel, (0, 2, 1))[:, :, None, :]
    logit_win = low_back(logit_win)
    logit_sel = low_back(logit_sel)
    logit_win = jnp.where(win_mask[:, None], logit_win, NEG_FILL)
    logit_sel = jnp.where(sel_mask[:, None, None, :], logit_sel, NEG_FILL)
    row_max = jnp.maximum(lax.optimization_barrier(jnp.max(logit_win, axis=-1, keepdims=True)), lax.optimization_barrier(jnp.max(logit_sel, axis=-1, keepdims=True)))
    exp_win = jnp.exp(logit_win - row_max)
    exp_sel = jnp.exp(logit_sel - row_max)
    row_total = lax.optimization_barrier(jnp.sum(exp_win, axis=-1, keepdims=True)) + lax.optimization_barrier(jnp.sum(exp_sel, axis=-1, keepdims=True))
    prob_win = low(exp_win / row_total)
    prob_sel = low(exp_sel / row_total)
    attended = jnp.einsum('bhqk,bkhd->bqhd', prob_win, value_win, precision=HIGHEST)
    attended = attended + jnp.einsum('bhqk,bkhd->bqhd', prob_sel, value_sel, precision=HIGHEST)
    attended = low_back(low(attended.reshape(SEQ_LEN, D)))
    branch = low_back(jnp.dot(attended, weight_out, precision=HIGHEST) + bias_out)
    middle = inputs + branch
    normed_two = low(layer_norm(middle, gain_two, shift_two))
    hidden_pre = low_back(jnp.dot(normed_two, weight_up, precision=HIGHEST) + bias_up)
    hidden = low(jax.nn.gelu(hidden_pre, approximate=True))
    return middle + jnp.dot(hidden, weight_down, precision=HIGHEST) + bias_down

def reference(tokens, weight_qkv, bias_query, bias_value, weight_score, weight_out, bias_out, gain_one, shift_one, gain_two, shift_two, weight_up, bias_up, weight_down, bias_down, cotangent, lengths, candidates, selected):
    weights = tuple((member.astype(jnp.float32) for member in (weight_qkv, bias_query, bias_value, weight_score, weight_out, bias_out, gain_one, shift_one, gain_two, shift_two, weight_up, bias_up, weight_down, bias_down)))

    def one_sequence(totals, member):
        inputs, grad_in, length, cand_rows, select_rows = member

        def apply(values, *params):
            return forward(values, *params, length, cand_rows, select_rows)
        output, pullback = jax.vjp(apply, inputs.astype(jnp.float32), *weights)
        gradients = pullback(grad_in.astype(jnp.float32))
        totals = tuple((summed + addend for summed, addend in zip(totals, gradients[1:])))
        return (totals, (output.astype(jnp.bfloat16), gradients[0]))
    initial = tuple((jnp.zeros(member.shape, jnp.float32) for member in weights))
    totals, (mixed, grad_tokens) = lax.scan(one_sequence, initial, (tokens, cotangent, lengths, candidates, selected))
    return (mixed, grad_tokens, totals[0], totals[1], totals[2], totals[3], totals[4], totals[5], totals[6], totals[7], totals[8], totals[9], totals[10], totals[11], totals[12], totals[13])
```

```python
import jax
import jax.numpy as jnp
from jax import lax
from jax.experimental import pallas as pl
from jax.experimental.pallas import tpu as pltpu
from jax.sharding import PartitionSpec as P

WIN = 64
MESH_ID = pl.DeviceIdType.MESH
BF16 = jnp.bfloat16
F32 = jnp.float32


class Place:
    def __init__(self, seq_count, grp_count):
        self.nc = 2
        self.nz = 4 if seq_count % 8 == 0 else 1
        self.nx = seq_count // (self.nc * self.nz)
        self.ng = grp_count
        self.counts = {"z": self.nz, "x": self.nx, "c": self.nc, "g": self.ng}

    def locate(self):
        rank = lax.axis_index("seq")
        self.at = {
            "c": lax.rem(rank, self.nc),
            "x": lax.rem(lax.div(rank, self.nc), self.nx),
            "z": lax.div(rank, self.nc * self.nx),
            "g": lax.axis_index("grp"),
        }
        return self

    def device(self, axis, where):
        at = dict(self.at)
        at[axis] = where
        return ((at["z"] * self.nx + at["x"]) * self.nc + at["c"], at["g"])

    def others(self, axis):
        count = self.counts[axis]
        return [lax.rem(self.at[axis] + step, count) for step in range(1, count)]

    def greet(self, more):
        barrier = pltpu.get_barrier_semaphore()
        devices = list(more)
        for axis in "czxg":
            devices += [self.device(axis, where) for where in self.others(axis)]
        for device in devices:
            pl.semaphore_signal(barrier, inc=1, device_id=device, device_id_type=MESH_ID)
        pl.semaphore_wait(barrier, len(devices))


class Mail:
    def __init__(self, send_sems, recv_sems):
        self.send_sems, self.recv_sems, self.count, self.sent = send_sems, recv_sems, 0, []

    def send(self, src, dst, device):
        copy = pltpu.make_async_remote_copy(
            src_ref=src,
            dst_ref=dst,
            send_sem=self.send_sems.at[self.count],
            recv_sem=self.recv_sems.at[self.count],
            device_id=device,
            device_id_type=MESH_ID,
        )
        copy.start()
        self.count += 1
        self.sent.append(copy)
        return copy

    def settle(self, copies):
        for copy in copies:
            copy.wait_send()
        gone = {id(copy) for copy in copies}
        self.sent = [copy for copy in self.sent if id(copy) not in gone]

    def finish(self):
        self.settle(list(self.sent))


class Reduction:
    def __init__(self, place, rows, wide, split, dtype=BF16, groups=True):
        self.place, self.rows, self.wide, self.split = place, rows, wide, split
        self.dtype, self.groups = dtype, groups
        nz, nx, ng = place.nz, place.nx, place.ng
        if split:
            part = wide // ng
            self.part = part
            self.order = "gxz"
            self.boxes = [
                (ng, nz, nx, rows, part),
                (max(ng - 1, 1), nz, nx, rows, part),
                (max(nx - 1, 1), nz, rows, part),
                (max(nz - 1, 1), rows, part),
                (ng, rows, part),
            ]
            self.copies = ng + (ng - 1) + (nx - 1) + (nz - 1) + (ng - 1)
        else:
            self.boxes = [
                (nz, nx, rows, wide),
                (max(nx - 1, 1), nz, rows, wide),
                (max(nz - 1, 1), rows, wide),
            ]
            self.copies = 1 + (nx - 1) + (nz - 1)
            if groups:
                self.boxes.append((ng, rows, wide))
                self.copies += ng - 1

    def scratch(self):
        return [pltpu.VMEM(box, self.dtype) for box in self.boxes]

    def bind(self, mail, refs, src, first, out):
        self.mail, self.refs, self.src, self.first, self.out = mail, refs, src, first, out
        self.stages = self.split_stages() if self.split else self.whole_stages()
        return self

    def pause(self, copies):
        for copy in copies:
            copy.wait_recv()

    def whole_stages(self):
        place, mail, wide = self.place, self.mail, self.wide
        c, x, z, g = (place.at[axis] for axis in "cxzg")
        nz, nx, ng = place.nz, place.nx, place.ng
        cols = pl.ds(self.first, wide)
        r0, r1, r2 = self.refs[:3]
        pending = {}

        def start():
            far = place.others("c")[0]
            pending[0] = [
                mail.send(self.src.at[:, :, far, :, cols], r0, place.device("c", far))
            ]

        def after_core():
            self.pause(pending[0])

            def add(i, _):
                zi, xi = lax.div(i, nx), lax.rem(i, nx)
                mine = self.src[zi, xi, c, :, cols].astype(F32)
                r0[zi, xi] = (mine + r0[zi, xi].astype(F32)).astype(self.dtype)
                return 0

            lax.fori_loop(0, nz * nx, add, 0)
            mail.settle(pending[0])
            pending[1] = [
                mail.send(r0.at[:, far], r1.at[i], place.device("x", far))
                for i, far in enumerate(place.others("x"))
            ]

        def after_x():
            self.pause(pending[1])

            def add(zi, _):
                total = r0[zi, x].astype(F32)
                for i in range(nx - 1):
                    total = total + r1[i, zi].astype(F32)
                r1[0, zi] = total.astype(self.dtype)
                return 0

            lax.fori_loop(0, nz, add, 0)
            pending[2] = [
                mail.send(r1.at[0, far], r2.at[i], place.device("z", far))
                for i, far in enumerate(place.others("z"))
            ]

        def after_z():
            self.pause(pending[2])
            total = r1[0, z].astype(F32)
            for i in range(nz - 1):
                total = total + r2[i].astype(F32)
            if not self.groups:
                self.out(0, total)
                return
            r3 = self.refs[3]
            r3[g] = total.astype(self.dtype)
            pending[3] = [
                mail.send(r3.at[g], r3.at[g], place.device("g", far)) for far in place.others("g")
            ]

        def after_groups():
            self.pause(pending[3])
            r3 = self.refs[3]
            total = r3[0].astype(F32)
            for i in range(1, ng):
                total = total + r3[i].astype(F32)
            self.out(0, total)

        return [start, after_core, after_x, after_z] + ([after_groups] if self.groups else [])

    def split_stages(self):
        place, mail, part = self.place, self.mail, self.part
        c, x, z, g = (place.at[axis] for axis in "cxzg")
        nz, nx, ng = place.nz, place.nx, place.ng
        r0, r1, r2, r3, r4 = self.refs
        pending = {}

        def start():
            far = place.others("c")[0]
            pending[0] = [
                mail.send(
                    self.src.at[:, :, far, :, pl.ds(self.first + i * part, part)],
                    r0.at[i],
                    place.device("c", far),
                )
                for i in range(ng)
            ]

        def after_core():
            self.pause(pending[0])

            def add(j, _):
                zi, xi = lax.div(j, nx), lax.rem(j, nx)
                for i in range(ng):
                    mine = self.src[zi, xi, c, :, pl.ds(self.first + i * part, part)].astype(F32)
                    r0[i, zi, xi] = (mine + r0[i, zi, xi].astype(F32)).astype(self.dtype)
                return 0

            lax.fori_loop(0, nz * nx, add, 0)
            mail.settle(pending[0])
            pending[1] = [
                mail.send(r0.at[far], r1.at[i], place.device("g", far))
                for i, far in enumerate(place.others("g"))
            ]

        def after_groups():
            self.pause(pending[1])

            def add(j, _):
                zi, xi = lax.div(j, nx), lax.rem(j, nx)
                total = r0[g, zi, xi].astype(F32)
                for i in range(ng - 1):
                    total = total + r1[i, zi, xi].astype(F32)
                r1[0, zi, xi] = total.astype(self.dtype)
                return 0

            lax.fori_loop(0, nz * nx, add, 0)
            pending[2] = [
                mail.send(r1.at[0, :, far], r2.at[i], place.device("x", far))
                for i, far in enumerate(place.others("x"))
            ]

        def after_x():
            self.pause(pending[2])

            def add(zi, _):
                total = r1[0, zi, x].astype(F32)
                for i in range(nx - 1):
                    total = total + r2[i, zi].astype(F32)
                r2[0, zi] = total.astype(self.dtype)
                return 0

            lax.fori_loop(0, nz, add, 0)
            pending[3] = [
                mail.send(r2.at[0, far], r3.at[i], place.device("z", far))
                for i, far in enumerate(place.others("z"))
            ]

        def after_z():
            self.pause(pending[3])
            total = r2[0, z].astype(F32)
            for i in range(nz - 1):
                total = total + r3[i].astype(F32)
            r4[g] = total.astype(self.dtype)
            pending[4] = [
                mail.send(r4.at[g], r4.at[g], place.device("g", far)) for far in place.others("g")
            ]

        def after_gather():
            self.pause(pending[4])
            for i in range(ng):
                self.out(i * part, r4[i].astype(F32))

        return [start, after_core, after_groups, after_x, after_z, after_gather]


class Total:
    def __init__(self, place, shape):
        self.place, self.shape = place, shape
        self.counts = [place.nc, place.nx, place.nz, place.ng]
        self.copies = sum(count - 1 for count in self.counts)

    def scratch(self):
        return [pltpu.VMEM((count,) + self.shape, F32) for count in self.counts]

    def bind(self, mail, refs, src, out):
        self.mail, self.refs, self.src, self.out = mail, refs, src, out
        axes = "cxzg"
        pending = {}

        def stage(level):
            def run():
                if level == 0:
                    value = self.src()
                else:
                    for copy in pending[level - 1]:
                        copy.wait_recv()
                    box = refs[level - 1]
                    value = box[0]
                    for i in range(1, self.counts[level - 1]):
                        value = value + box[i]
                if level == 4:
                    self.out(value)
                    return
                box, axis = refs[level], axes[level]
                here = self.place.at[axis]
                box[here] = value
                pending[level] = [
                    mail.send(box.at[here], box.at[here], self.place.device(axis, far))
                    for far in self.place.others(axis)
                ]

            return run

        self.stages = [stage(level) for level in range(5)]
        return self

NT = (((1,), (1,)), ((), ()))
TN = (((0,), (0,)), ((), ()))
NEG_FILL = -1e30
QUAD = 4
WHOLE = pl.BlockSpec(memory_space=pltpu.VMEM)
CURVE = 0.7978845608028654
CUBE = 0.044715


def dot(a, b, dims=(((1,), (0,)), ((), ()))):
    return lax.dot_general(a, b, dims, preferred_element_type=F32)


def row(ref):
    return ref[...].reshape(1, ref.shape[0])


def norm_parts(values):
    center = values - jnp.mean(values, axis=-1, keepdims=True)
    root = lax.rsqrt(jnp.mean(center * center, axis=-1, keepdims=True) + 1e-05)
    return center * root, root


def norm_back(grad, hat, root, gain):
    gx = grad * gain
    return root * (
        gx - jnp.mean(gx, axis=-1, keepdims=True) - hat * jnp.mean(gx * hat, axis=-1, keepdims=True)
    )


def hot_columns(index_row, count):
    rows = lax.broadcasted_iota(jnp.int32, (count, index_row.shape[1]), 0)
    return jnp.where(rows == index_row, 1.0, 0.0).astype(BF16)


def selected_row(sel_ref, seq):
    return jnp.concatenate([sel_ref[seq, b : b + 1, :] for b in range(sel_ref.shape[1])], axis=1)


def spread_heads(rows, size):
    lane_head = lax.broadcasted_iota(jnp.int32, rows.shape, 1) // size
    zero = jnp.zeros_like(rows)
    return jnp.concatenate([jnp.where(lane_head == h, rows, zero) for h in range(QUAD)], axis=0)


def merge_heads(wide, size):
    count = wide.shape[0] // QUAD
    lane_head = lax.broadcasted_iota(jnp.int32, (count, wide.shape[1]), 1) // size
    result = wide[:count]
    for h in range(1, QUAD):
        result = jnp.where(lane_head == h, wide[h * count : (h + 1) * count], result)
    return result


def window_bias(base, length):
    shape = (2 * WIN, QUAD * WIN)
    key = lax.broadcasted_iota(jnp.int32, shape, 0)
    query = lax.broadcasted_iota(jnp.int32, shape, 1) % WIN
    key_pos = key + (base - WIN)
    keep = (
        (key > query)
        & (key <= query + WIN)
        & (key_pos >= 0)
        & ((key_pos < length) | (key == query + WIN))
    )
    return jnp.where(keep, 0.0, NEG_FILL).astype(F32)


def keys_of(ext_ref, sel_ref, seq, start, rows_at, cols):
    return jnp.concatenate(
        [ext_ref[seq, pl.ds(start, 2 * WIN), cols], sel_ref[pl.ds(rows_at, WIN), cols]], axis=0
    )


def opening(place, tokens, candidates, selected, lengths, gain, shift, weight_qkv, bias_query, bias_value, weight_score):
    rows, width = tokens.shape
    seq_count, ranks, cands = candidates.shape
    tok = rows // seq_count
    blocks = tok // WIN
    every = ranks * cands
    heads = weight_score.shape[1]
    head_size = width // heads
    nz, nx, nc = place.nz, place.nx, place.nc
    copies = 1 + (nz - 1) + (nx - 1) * nz + nz * nx
    scale = head_size ** (-0.5)
    picks = blocks * WIN

    def kernel(
        len_ref, tok_ref, cand_ref, sel_ref, gain_ref, shift_ref, w_ref, bq_ref, bv_ref, ws_ref,
        normed_ref, q_ref, ext_ref, halo_ref, nsel_ref, ksel_ref, bias_ref, score_ref,
        gat, halo_out, halo_in, send_sems, recv_sems,
    ):
        place.locate()
        mail = Mail(send_sems, recv_sems)
        z, x, c, g = (place.at[axis] for axis in "zxcg")
        rank = lax.axis_index("seq")
        after = (lax.rem(rank + 1, ranks), g)
        before = (lax.rem(rank + ranks - 1, ranks), g)
        barrier = pltpu.get_barrier_semaphore()
        greeted = [after, before]
        for axis in "czx":
            greeted += [place.device(axis, where) for where in place.others(axis)]
        for device in greeted:
            pl.semaphore_signal(barrier, inc=1, device_id=device, device_id_type=MESH_ID)
        gain_row, shift_row = row(gain_ref), row(shift_ref)

        def norm(values):
            return (norm_parts(values.astype(F32))[0] * gain_row + shift_row).astype(BF16)

        for seq in range(seq_count):
            hot = hot_columns(cand_ref[seq, pl.ds(rank, 1), :], tok)
            gat[seq, z, x, c] = norm(dot(hot, tok_ref[pl.ds(seq * tok, tok), :], TN))
            halo_out[seq] = norm(tok_ref[pl.ds((seq + 1) * tok - WIN, WIN), :])
        pl.semaphore_wait(barrier, len(greeted))

        def slot(zi, xi, ci):
            return gat.at[:, zi, xi, ci]

        by_z = [
            mail.send(slot(z, x, c), slot(z, x, c), place.device("z", far))
            for far in place.others("z")
        ]
        halo_copy = mail.send(halo_out, halo_in, after)
        core = place.device("c", place.others("c")[0])
        by_x, by_c = [], []

        def forward_x(zi):
            by_x.append(
                [
                    mail.send(slot(zi, x, c), slot(zi, x, c), place.device("x", far))
                    for far in place.others("x")
                ]
            )
            by_c.append(mail.send(slot(zi, x, c), slot(zi, x, c), core))

        def forward_c(zi, step):
            for i, copy in enumerate(by_x[step]):
                copy.wait_recv()
                come = lax.rem(x + nx - 1 - i, nx)
                by_c.append(mail.send(slot(zi, come, c), slot(zi, come, c), core))

        forward_x(z)
        for seq in range(seq_count):
            normed_ref[pl.ds(seq * tok, tok), :] = norm(tok_ref[pl.ds(seq * tok, tok), :])
        sources = [z] + [lax.rem(z + nz - 1 - i, nz) for i in range(nz - 1)]
        queries = dot(normed_ref[...], w_ref[:, :width]) + row(bq_ref)
        q_ref[...] = (queries.astype(BF16).astype(F32) * scale).astype(BF16)
        value_bias = row(bv_ref)
        for i in range(nz - 1):
            by_z[i].wait_recv()
            forward_x(sources[i + 1])
        forward_c(sources[0], 0)

        def project(values, half):
            part = dot(values, w_ref[:, pl.ds((1 + half) * width, width)])
            if half == 1:
                part = part + value_bias
            return part.astype(BF16)

        for half in range(2):
            cols = pl.ds(half * width, width)
            for seq in range(seq_count):
                ext_ref[seq, pl.ds(WIN, tok), cols] = project(
                    normed_ref[pl.ds(seq * tok, tok), :], half
                )
        halo_copy.wait_recv()
        for seq in range(seq_count):
            halo_ref[pl.ds(seq * WIN, WIN), :] = halo_in[seq]
        for half in range(2):
            part = project(halo_ref[...], half)
            for seq in range(seq_count):
                ext_ref[seq, pl.ds(0, WIN), pl.ds(half * width, width)] = part[
                    seq * WIN : (seq + 1) * WIN
                ]
        counted = []
        for seq in range(seq_count):
            index = selected_row(sel_ref, seq)
            inner = hot_columns(index % cands, cands)
            table = cand_ref[seq].astype(F32).astype(BF16)
            offset = dot(table, inner)
            block_of = lax.broadcasted_iota(jnp.int32, (ranks, picks), 0)
            chosen = jnp.where(block_of == index // cands, offset, 0.0)
            position = jnp.sum(chosen, axis=0, keepdims=True)
            position = position + ((index // cands) * tok).astype(F32)
            lane_block = lax.broadcasted_iota(jnp.int32, (1, picks), 1) // WIN
            limit = jnp.minimum((rank * blocks + lane_block) * WIN - WIN + 1, len_ref[seq])
            flag = jnp.where(position < limit.astype(F32), 1.0, 0.0)
            across = lax.broadcasted_iota(jnp.int32, (picks, picks), 0)
            down = lax.broadcasted_iota(jnp.int32, (picks, picks), 1)
            diagonal = jnp.where(across == down, flag, 0.0).astype(BF16)
            counted.append(dot(diagonal, jnp.ones((picks, width), BF16)))
        head_of = lax.broadcasted_iota(jnp.int32, (heads, width), 1) // WIN
        widen = jnp.where(head_of == lax.broadcasted_iota(jnp.int32, (heads, width), 0), 1.0, 0.0)
        score_ref[...] = jnp.zeros_like(score_ref)
        for i in range(1, nz):
            forward_c(sources[i], i)
        for copy in by_c:
            copy.wait_recv()
        for seq in range(seq_count):
            here = pl.ds(seq * picks, picks)
            hot = hot_columns(selected_row(sel_ref, seq), every)
            picked = dot(hot, gat[seq].reshape(every, width), TN).astype(BF16)
            nsel_ref[here, :] = picked
            for half in range(2):
                ksel_ref[here, pl.ds(half * width, width)] = project(picked, half)
            score = dot(picked, ws_ref[...]).astype(BF16)
            score_ref[here, pl.ds(0, heads)] = score
            wide = dot(score, widen.astype(BF16))
            gate = jnp.minimum(wide, 0.0) - jnp.log1p(jnp.exp(-jnp.abs(wide)))
            bias_ref[here, :] = jnp.where(counted[seq] > 0.5, gate, NEG_FILL)
        mail.finish()

    shapes = [
        ((rows, width), BF16),
        ((rows, width), BF16),
        ((seq_count, tok + WIN, 2 * width), BF16),
        ((seq_count * WIN, width), BF16),
        ((seq_count * picks, width), BF16),
        ((seq_count * picks, 2 * width), BF16),
        ((seq_count * picks, width), F32),
        ((seq_count * picks, 128), BF16),
    ]
    return pl.pallas_call(
        kernel,
        out_shape=[jax.ShapeDtypeStruct(*shape) for shape in shapes],
        in_specs=[pl.BlockSpec(memory_space=pltpu.SMEM)] + [WHOLE] * 9,
        out_specs=[WHOLE] * len(shapes),
        scratch_shapes=[
            pltpu.VMEM((seq_count, nz, nx, nc, cands, width), BF16),
            pltpu.VMEM((seq_count, WIN, width), BF16),
            pltpu.VMEM((seq_count, WIN, width), BF16),
            pltpu.SemaphoreType.DMA((copies,)),
            pltpu.SemaphoreType.DMA((copies,)),
        ],
        compiler_params=pltpu.CompilerParams(
            collective_id=2, has_side_effects=True, vmem_limit_bytes=48 * 2**20
        ),
    )(lengths, tokens, candidates, selected, gain, shift, weight_qkv, bias_query, bias_value, weight_score)


def middle_part(lengths, queries, ext, ksel, bias_sel, tokens, dy, weight_out, bias_out, gain, shift, weight_up, bias_up, weight_down, bias_down, head_size):
    rows, width = tokens.shape
    seq_count, ext_rows, _ = ext.shape
    tok = ext_rows - WIN
    blocks = tok // WIN
    lanes = QUAD * head_size
    quads = width // lanes
    hidden_size = bias_up.shape[0]
    parts = hidden_size // width

    def kernel(
        len_ref, q_ref, ext_ref, sel_ref, bias_ref, tok_ref, dy_ref, wo_ref, bo_ref, gain_ref, shift_ref,
        wu_ref, bu_ref, wd_ref, bd_ref,
        att_ref, prob_ref, mixed_ref, hidden_ref, gpre_ref, n2_ref, branch_ref, gmid_ref, gatt_ref, vec_ref,
    ):
        base = lax.axis_index("seq") * tok

        def attend(i, _):
            seq, block = lax.div(i, blocks), lax.rem(i, blocks)
            at = pl.multiple_of(i * WIN, WIN)
            start = pl.multiple_of(block * WIN, WIN)
            mask = window_bias(base + block * WIN, len_ref[seq])
            for quad in range(quads):
                cols = pl.ds(quad * lanes, lanes)
                vals = pl.ds(width + quad * lanes, lanes)
                keys = keys_of(ext_ref, sel_ref, seq, start, at, cols)
                values = keys_of(ext_ref, sel_ref, seq, start, at, vals)
                wide = spread_heads(q_ref[pl.ds(at, WIN), cols], head_size)
                logits = dot(keys, wide, NT)
                logits = logits + jnp.concatenate([mask, bias_ref[pl.ds(at, WIN), cols]], axis=0)
                grown = jnp.exp(logits - jnp.max(logits, axis=0, keepdims=True))
                probs = (grown / jnp.sum(grown, axis=0, keepdims=True)).astype(BF16)
                prob_ref[i, quad] = probs
                att_ref[pl.ds(at, WIN), cols] = merge_heads(
                    dot(probs, values, TN), head_size
                ).astype(BF16)
            return 0

        lax.fori_loop(0, seq_count * blocks, attend, 0)
        gain_row = row(gain_ref)
        middle = tok_ref[...].astype(F32) + dot(att_ref[...], wo_ref[...]) + row(bo_ref)
        gmid_ref[...] = middle
        hat, _ = norm_parts(middle)
        n2_ref[...] = (hat * gain_row + row(shift_ref)).astype(BF16)
        bias_row = row(bu_ref)
        mixed = middle + row(bd_ref)
        grad_normed = jnp.zeros((rows, width), F32)
        for part in range(parts):
            cols = pl.ds(part * width, width)
            pre = dot(n2_ref[...], wu_ref[:, cols]) + bias_row[:, part * width : (part + 1) * width]
            square = pre * pre
            tanh = jnp.tanh(CURVE * pre * (1.0 + CUBE * square))
            half = 0.5 + 0.5 * tanh
            hidden_ref[:, cols] = (pre * half).astype(BF16)
            slope = half + 0.5 * pre * (1.0 - tanh * tanh) * (CURVE + 3 * CUBE * CURVE * square)
            gpre = (dot(dy_ref[...], wd_ref[cols, :], NT) * slope).astype(BF16)
            gpre_ref[:, cols] = gpre
            vec_ref[pl.ds(8 + part, 1), :] = jnp.sum(gpre.astype(F32), axis=0, keepdims=True)
            mixed = mixed + dot(hidden_ref[:, cols], wd_ref[cols, :])
            grad_normed = grad_normed + dot(gpre, wu_ref[:, cols], NT)
        mixed_ref[...] = mixed.astype(BF16)
        hat, root = norm_parts(gmid_ref[...])
        dy_wide = dy_ref[...].astype(F32)
        vec_ref[0:4, :] = jnp.zeros((4, width), F32)
        vec_ref[5:6, :] = jnp.sum(grad_normed * hat, axis=0, keepdims=True)
        vec_ref[6:7, :] = jnp.sum(grad_normed, axis=0, keepdims=True)
        vec_ref[7:8, :] = jnp.sum(dy_wide, axis=0, keepdims=True)
        grad_middle = dy_wide + norm_back(grad_normed, hat, root, gain_row)
        gmid_ref[...] = grad_middle
        branch = grad_middle.astype(BF16)
        branch_ref[...] = branch
        vec_ref[4:5, :] = jnp.sum(branch.astype(F32), axis=0, keepdims=True)
        gatt_ref[...] = dot(branch, wo_ref[...], NT).astype(BF16)

    shapes = [
        ((rows, width), BF16),
        ((seq_count * blocks, quads, 3 * WIN, QUAD * WIN), BF16),
        ((rows, width), BF16),
        ((rows, hidden_size), BF16),
        ((rows, hidden_size), BF16),
        ((rows, width), BF16),
        ((rows, width), BF16),
        ((rows, width), F32),
        ((rows, width), BF16),
        ((8 + parts, width), F32),
    ]
    return pl.pallas_call(
        kernel,
        out_shape=[jax.ShapeDtypeStruct(*shape) for shape in shapes],
        in_specs=[pl.BlockSpec(memory_space=pltpu.SMEM)] + [WHOLE] * 14,
        out_specs=[WHOLE] * len(shapes),
        compiler_params=pltpu.CompilerParams(vmem_limit_bytes=60 * 2**20),
    )(lengths, queries, ext, ksel, bias_sel, tokens, dy, weight_out, bias_out, gain, shift, weight_up, bias_up, weight_down, bias_down)

class Shift:
    copies = 1

    def __init__(self, shape):
        self.shape = shape

    def scratch(self):
        return [pltpu.VMEM(self.shape, BF16)]

    def bind(self, mail, refs, src, device, out):
        held = []

        def start():
            held.append(mail.send(src, refs[0], device))

        def finish():
            held[0].wait_recv()
            out(refs[0][...])

        self.stages = [start, finish]
        return self


class Flow:
    def __init__(self):
        self.active = []

    def begin(self, tasks):
        for task in tasks:
            task.stages.pop(0)()
        self.advance()
        self.active.extend(tasks)

    def advance(self):
        for task in self.active:
            task.stages.pop(0)()
        self.active = [task for task in self.active if task.stages]

    def drain(self):
        while self.active:
            self.advance()


def closing(place, gradients, attention, weight_qkv, weight_score, selected, gain, shift, tokens, vec, head_size):
    hidden, dy, gpre, n2, branch, attended = gradients
    queries, ext, ksel, probs, score, gatt, normed, halo, nsel = attention
    rows, width = dy.shape
    seq_count, ext_rows, _ = ext.shape
    tok = ext_rows - WIN
    blocks = tok // WIN
    steps = seq_count * blocks
    lanes = QUAD * head_size
    quads = width // lanes
    heads = weight_score.shape[1]
    hidden_size = hidden.shape[1]
    parts = hidden_size // width
    nz, nx, nc, ng = place.nz, place.nx, place.nc, place.ng
    ranks = nz * nx * nc
    lead = (nz, nx, nc)
    share = width // ranks
    down_share = hidden_size // ranks
    down_wide = 256
    every_row = vec.shape[0] + heads
    picks = blocks * WIN
    cands = 32
    scale = head_size ** (-0.5)
    can_split = width % (128 * ng) == 0
    downs = [Reduction(place, down_share, down_wide, False) for _ in range(width // down_wide)]
    ups = [Reduction(place, share, width, can_split) for _ in range(parts)]
    out_task = Reduction(place, share, width, False)
    qkvs = [Reduction(place, share, width, can_split and i < quads - 1) for i in range(quads)]
    back_wide = width // 2
    backs = [Reduction(place, seq_count * cands, back_wide, False, groups=False) for _ in range(2)]
    total = Total(place, (every_row, width))
    shift_task = Shift((seq_count, WIN, width))
    tasks = downs + ups + [out_task] + qkvs + backs + [total, shift_task]
    boxes, counts = [], []
    for task in tasks:
        mine = task.scratch()
        boxes.extend(mine)
        counts.append(len(mine))
    copies = sum(task.copies for task in tasks)
    slots, down_slots = 3, 2
    work = [
        pltpu.VMEM((slots,) + lead + (share, width), BF16),
        pltpu.VMEM((down_slots,) + lead + (down_share, down_wide), BF16),
        pltpu.VMEM(lead + (seq_count * cands, width), BF16),
        pltpu.VMEM((seq_count, WIN, width), BF16),
        pltpu.VMEM((rows, lanes), BF16),
        pltpu.VMEM((seq_count, ext_rows, 2 * lanes), F32),
        pltpu.VMEM((seq_count * picks, 2 * lanes), BF16),
        pltpu.VMEM((seq_count * picks, 128), F32),
        pltpu.VMEM((seq_count * picks, width), F32),
        pltpu.VMEM((seq_count * WIN, width), F32),
        pltpu.VMEM((every_row, width), F32),
    ]

    def kernel(*refs):
        (
            hid_ref, dy_ref, gpre_ref, n2_ref, branch_ref, att_ref,
            q_ref, ext_ref, sel_ref, prob_ref, score_ref, gatt_ref, normed_ref, halo_ref, nsel_ref,
            w_ref, ws_ref, pick_ref, gain_ref, shift_ref, tok_ref, vec_ref,
        ) = refs[:22]
        gqkv_ref, gout_ref, gup_ref, gdown_ref, total_ref, gn_ref, cand_ref, back_ref = refs[22:30]
        rest = list(refs[30:])
        recv_sems, send_sems = rest.pop(), rest.pop()
        stage, down_stage, back_src, halo_src, gq_ref, acc, gsel_ref, gates, gn_sel, gn_halo, own_vec = rest[-11:]
        room = rest[:-11]
        place.locate()
        mail = Mail(send_sems, recv_sems)
        rank, g = lax.axis_index("seq"), lax.axis_index("grp")
        after = (lax.rem(rank + 1, ranks), g)
        before = (lax.rem(rank + ranks - 1, ranks), g)
        place.greet([after, before])
        taken = {}
        for task, count in zip(tasks, counts):
            taken[id(task)] = room[:count]
            del room[:count]

        def column_writer(out, first):
            def write(offset, value):
                out[:, pl.ds(first + offset, value.shape[1])] = value

            return write

        def quad_writer(quad):
            def write(offset, value):
                wide = value.shape[1]
                low = offset
                while low < offset + wide:
                    kind = low // lanes
                    high = min(offset + wide, (kind + 1) * lanes)
                    at = kind * width + quad * lanes + low - kind * lanes
                    gqkv_ref[:, pl.ds(at, high - low)] = value[:, low - offset : high - offset]
                    low = high

            return write

        used = [0, 0]

        def bind(task, which, out):
            if which == 0:
                src = stage.at[used[0] % slots]
                used[0] += 1
            else:
                src = down_stage.at[used[1] % down_slots]
                used[1] += 1
            task.bind(mail, taken[id(task)], src, 0, out)
            return src

        def fill(src, left, right):
            shares, share_rows = src.shape[0] * src.shape[1] * src.shape[2], src.shape[3]
            value = dot(left, right, TN).astype(BF16)
            src[...] = value.reshape(src.shape)

        def down(i):
            src = bind(downs[i], 1, column_writer(gdown_ref, i * down_wide))
            fill(src, hid_ref[...], dy_ref[:, i * down_wide : (i + 1) * down_wide])
            return downs[i]

        def up(i):
            src = bind(ups[i], 0, column_writer(gup_ref, i * width))
            fill(src, n2_ref[...], gpre_ref[:, i * width : (i + 1) * width])
            return ups[i]

        def out():
            src = bind(out_task, 0, column_writer(gout_ref, 0))
            fill(src, att_ref[...], branch_ref[...])
            return out_task

        def attend_back(quad, first, last):
            cols = pl.ds(quad * lanes, lanes)
            vals = pl.ds(width + quad * lanes, lanes)

            def step(i, _):
                seq, block = lax.div(i, blocks), lax.rem(i, blocks)
                at = pl.multiple_of(i * WIN, WIN)
                start = pl.multiple_of(block * WIN, WIN)
                keys = keys_of(ext_ref, sel_ref, seq, start, at, cols)
                values = keys_of(ext_ref, sel_ref, seq, start, at, vals)
                wide_q = spread_heads(q_ref[pl.ds(at, WIN), cols], head_size)
                wide_g = spread_heads(gatt_ref[pl.ds(at, WIN), cols], head_size)
                low_probs = prob_ref[i, quad]
                full = low_probs.astype(F32)
                weighed = full * dot(values, wide_g, NT)
                delta = jnp.sum(weighed, axis=0, keepdims=True)
                low = (weighed - full * delta).astype(BF16)
                grad_values = dot(low_probs, wide_g)
                grad_keys = dot(low, wide_q)
                gq = merge_heads(dot(low, keys, TN), head_size) * scale
                gq_ref[pl.ds(at, WIN), :] = gq.astype(BF16)
                acc[seq, pl.ds(start, 2 * WIN), :lanes] += grad_keys[: 2 * WIN]
                acc[seq, pl.ds(start, 2 * WIN), lanes:] += grad_values[: 2 * WIN]
                gsel_ref[pl.ds(at, WIN), :lanes] = grad_keys[2 * WIN :].astype(BF16)
                gsel_ref[pl.ds(at, WIN), lanes:] = grad_values[2 * WIN :].astype(BF16)
                head = lax.broadcasted_iota(jnp.int32, (lanes, 128), 0) // head_size + quad * QUAD
                pick = jnp.where(head == lax.broadcasted_iota(jnp.int32, (lanes, 128), 1), 1.0, 0.0)
                gates[pl.ds(at, WIN), :] += dot(low[2 * WIN :], pick.astype(BF16))
                return 0

            if first == 0:
                acc[...] = jnp.zeros_like(acc)
            lax.fori_loop(first, last, step, 0)

        def finish_quad(quad):
            src = bind(qkvs[quad], 0, quad_writer(quad))
            gq = gq_ref[...]
            gown = jnp.concatenate([acc[seq, WIN:, :] for seq in range(seq_count)], axis=0).astype(BF16)
            ghalo = jnp.concatenate([acc[seq, :WIN, :] for seq in range(seq_count)], axis=0).astype(BF16)
            gsel = gsel_ref[...]
            src[:, :, :, :, :lanes] = (
                dot(normed_ref[...], gq, TN).astype(BF16).reshape(lead + (share, lanes))
            )
            both = dot(normed_ref[...], gown, TN) + dot(halo_ref[...], ghalo, TN) + dot(nsel_ref[...], gsel, TN)
            src[:, :, :, :, lanes:] = both.astype(BF16).reshape(lead + (share, 2 * lanes))
            spots = [pl.ds(kind * width + quad * lanes, lanes) for kind in range(3)]
            own = dot(gq, w_ref[:, spots[0]], NT)
            own = own + dot(gown[:, :lanes], w_ref[:, spots[1]], NT)
            own = own + dot(gown[:, lanes:], w_ref[:, spots[2]], NT)
            near = dot(ghalo[:, :lanes], w_ref[:, spots[1]], NT) + dot(ghalo[:, lanes:], w_ref[:, spots[2]], NT)
            chosen = dot(gsel[:, :lanes], w_ref[:, spots[1]], NT) + dot(gsel[:, lanes:], w_ref[:, spots[2]], NT)
            if quad == 0:
                gn_ref[...], gn_halo[...], gn_sel[...] = own, near, chosen
            else:
                gn_ref[...] += own
                gn_halo[...] += near
                gn_sel[...] += chosen
            cols = pl.ds(quad * lanes, lanes)
            own_vec[0:1, cols] = jnp.sum(gq.astype(F32), axis=0, keepdims=True)
            own_vec[1:2, cols] = (
                jnp.sum(gown[:, lanes:].astype(F32), axis=0, keepdims=True)
                + jnp.sum(ghalo[:, lanes:].astype(F32), axis=0, keepdims=True)
                + jnp.sum(gsel[:, lanes:].astype(F32), axis=0, keepdims=True)
            )
            return qkvs[quad]

        def give_back():
            score_now = score_ref[...].astype(F32)
            gscore = (gates[...] / (1.0 + jnp.exp(score_now))).astype(BF16)
            chosen = gn_sel[...] + dot(gscore[:, :heads], ws_ref[...], NT)
            low = chosen.astype(BF16)
            for seq in range(seq_count):
                hot = hot_columns(selected_row(pick_ref, seq), ranks * cands)
                terms = dot(hot, low[seq * picks : (seq + 1) * picks]).astype(BF16)
                back_src[:, :, :, pl.ds(seq * cands, cands), :] = terms.reshape(lead + (cands, width))
                halo_src[seq] = gn_halo[pl.ds(seq * WIN, WIN), :].astype(BF16)
            for i, task in enumerate(backs):
                task.bind(mail, taken[id(task)], back_src, i * back_wide, column_writer(cand_ref, i * back_wide))

            def halo_write(value):
                back_ref[...] = value

            shift_task.bind(mail, taken[id(shift_task)], halo_src, before, halo_write)
            gain_row, shift_row = row(gain_ref), row(shift_ref)
            hat, _ = norm_parts(tok_ref[...].astype(F32))

            def hat_of(ref):
                return (ref[...].astype(F32) - shift_row) / gain_row

            own, near = gn_ref[...], gn_halo[...]
            own_vec[2:3, :] = (
                jnp.sum(own * hat, axis=0, keepdims=True)
                + jnp.sum(near * hat_of(halo_ref), axis=0, keepdims=True)
                + jnp.sum(chosen * hat_of(nsel_ref), axis=0, keepdims=True)
            )
            own_vec[3:4, :] = (
                jnp.sum(own, axis=0, keepdims=True)
                + jnp.sum(near, axis=0, keepdims=True)
                + jnp.sum(chosen, axis=0, keepdims=True)
            )
            own_vec[4 : vec_ref.shape[0], :] = vec_ref[4:, :]
            own_vec[vec_ref.shape[0] :, :] = dot(gscore, nsel_ref[...], TN)[:heads]

            def vec_write(value):
                total_ref[...] = value

            total.bind(mail, taken[id(total)], lambda: own_vec[...], vec_write)
            return [shift_task] + backs + [total]

        gates[...] = jnp.zeros_like(gates)
        flow = Flow()
        half = steps // 2
        flow.begin([down(0)])
        attend_back(0, 0, half)
        flow.begin([up(0)])
        attend_back(0, half, steps)
        flow.begin([down(1)])
        flow.begin([up(1)])
        attend_back_done = finish_quad(0)
        flow.begin([attend_back_done])
        attend_back(1, 0, half)
        flow.begin([down(2)])
        attend_back(1, half, steps)
        flow.begin([up(2)])
        flow.begin([finish_quad(1)])
        attend_back(2, 0, half)
        flow.begin([out()])
        attend_back(2, half, steps)
        flow.begin([up(3)])
        flow.begin([finish_quad(2)])
        flow.begin(give_back())
        flow.drain()
        mail.finish()

    shapes = [
        ((share, 3 * width), F32),
        ((share, width), F32),
        ((share, hidden_size), F32),
        ((down_share, width), F32),
        ((every_row, width), F32),
        ((rows, width), F32),
        ((seq_count * cands, width), F32),
        ((seq_count, WIN, width), BF16),
    ]
    return pl.pallas_call(
        kernel,
        out_shape=[jax.ShapeDtypeStruct(*shape) for shape in shapes],
        in_specs=[WHOLE] * 22,
        out_specs=[WHOLE] * len(shapes),
        scratch_shapes=boxes
        + work
        + [pltpu.SemaphoreType.DMA((copies,)), pltpu.SemaphoreType.DMA((copies,))],
        compiler_params=pltpu.CompilerParams(
            collective_id=3, has_side_effects=True, vmem_limit_bytes=63 * 2**20
        ),
    )(
        hidden, dy, gpre, n2, branch, attended,
        queries, ext, ksel, probs, score, gatt, normed, halo, nsel,
        weight_qkv, weight_score, selected, gain, shift, tokens, vec,
    )


def ending(tokens, candidates, gain, grad_middle, gn, cand_back, halo_back, total, parts, heads, ranks):
    rows, width = tokens.shape
    seq_count, _, cands = candidates.shape
    tok = rows // seq_count
    share = width // ranks
    up_share = parts * share
    vec_rows = total.shape[0]

    def kernel(
        tok_ref, cand_ref, gain_ref, gmid_ref, gn_ref, back_ref, halo_ref, total_ref,
        grad_ref, small_ref, up_ref, score_ref,
    ):
        rank = lax.axis_index("seq")
        gain_row = row(gain_ref)
        for seq in range(seq_count):
            here = pl.ds(seq * tok, tok)
            hot = hot_columns(cand_ref[seq, pl.ds(rank, 1), :], tok)
            came = back_ref[pl.ds(seq * cands, cands), :].astype(BF16)
            grad = gn_ref[here, :] + dot(hot, came)
            near = halo_ref[seq].astype(F32)
            grad = grad + jnp.concatenate([jnp.zeros((tok - WIN, width), F32), near], axis=0)
            hat, root = norm_parts(tok_ref[here, :].astype(F32))
            grad_ref[here, :] = gmid_ref[here, :] + norm_back(grad, hat, root, gain_row)
        from_row = lax.broadcasted_iota(jnp.int32, (width, share), 0)
        to_col = lax.broadcasted_iota(jnp.int32, (width, share), 1)
        pick = jnp.where(from_row == to_col + rank * share, 1.0, 0.0)
        values = total_ref[...]
        small = lax.dot_general(
            values, pick, (((1,), (0,)), ((), ())),
            precision=lax.Precision.HIGHEST, preferred_element_type=F32,
        )
        small_ref[...] = small[:8]
        score_ref[...] = small[8 + parts :].T
        per_row = width // up_share
        from_row = lax.broadcasted_iota(jnp.int32, (width, up_share), 0)
        to_col = lax.broadcasted_iota(jnp.int32, (width, up_share), 1)
        pick = jnp.where(from_row == to_col + lax.rem(rank, per_row) * up_share, 1.0, 0.0)
        ups = lax.dot_general(
            values[8 : 8 + parts], pick, (((1,), (0,)), ((), ())),
            precision=lax.Precision.HIGHEST, preferred_element_type=F32,
        )
        which = lax.broadcasted_iota(jnp.int32, ups.shape, 0)
        up_ref[...] = jnp.sum(
            jnp.where(which == lax.div(rank, per_row), ups, 0.0), axis=0, keepdims=True
        )

    return pl.pallas_call(
        kernel,
        out_shape=[
            jax.ShapeDtypeStruct((rows, width), F32),
            jax.ShapeDtypeStruct((8, share), F32),
            jax.ShapeDtypeStruct((1, up_share), F32),
            jax.ShapeDtypeStruct((share, heads), F32),
        ],
        in_specs=[WHOLE] * 8,
        out_specs=[WHOLE] * 4,
        compiler_params=pltpu.CompilerParams(vmem_limit_bytes=40 * 2**20),
    )(tokens, candidates, gain, grad_middle, gn, cand_back, halo_back, total)


def per_device(
    tokens,
    weight_qkv,
    bias_query,
    bias_value,
    weight_score,
    weight_out,
    bias_out,
    gain_one,
    shift_one,
    gain_two,
    shift_two,
    weight_up,
    bias_up,
    weight_down,
    bias_down,
    cotangent,
    lengths,
    candidates,
    selected,
):
    seq_count, tok, width = tokens.shape
    heads = weight_score.shape[1]
    head_size = width // heads
    rows = seq_count * tok
    ranks = lax.axis_size("seq")
    place = Place(ranks, lax.axis_size("grp"))
    parts = bias_up.shape[0] // width
    flat = tokens.reshape(rows, width)
    dy = cotangent.reshape(rows, width)
    normed, queries, ext, halo, nsel, ksel, bias_sel, score = opening(
        place, flat, candidates, selected, lengths, gain_one, shift_one,
        weight_qkv, bias_query, bias_value, weight_score,
    )
    attended, probs, mixed, hidden, gpre, n2, branch, grad_middle, gatt, vec = middle_part(
        lengths, queries, ext, ksel, bias_sel, flat, dy, weight_out, bias_out, gain_two, shift_two,
        weight_up, bias_up, weight_down, bias_down, head_size,
    )
    grad_qkv, grad_out, grad_up, grad_down, total, gn, cand_back, halo_back = closing(
        place,
        (hidden, dy, gpre, n2, branch, attended),
        (queries, ext, ksel, probs, score, gatt, normed, halo, nsel),
        weight_qkv, weight_score, selected, gain_one, shift_one, flat, vec, head_size,
    )
    grad_tokens, small, up_row, score_rows = ending(
        flat, candidates, gain_one, grad_middle, gn, cand_back, halo_back, total, parts, heads, ranks
    )
    return (
        mixed.reshape(tokens.shape),
        grad_tokens.reshape(tokens.shape),
        grad_qkv,
        small[0],
        small[1],
        score_rows,
        grad_out,
        small[4],
        small[2],
        small[3],
        small[5],
        small[6],
        grad_up,
        up_row[0],
        grad_down,
        small[7],
    )


def solution(mesh):
    return jax.shard_map(
        per_device,
        mesh=mesh,
        in_specs=(
            P("grp", "seq", None),
            P(),
            P(),
            P(),
            P(),
            P(),
            P(),
            P(),
            P(),
            P(),
            P(),
            P(),
            P(),
            P(),
            P(),
            P("grp", "seq", None),
            P("grp"),
            P("grp", None, None),
            P("grp", "seq", None),
        ),
        out_specs=(
            P("grp", "seq", None),
            P("grp", "seq", None),
            P("seq", None),
            P("seq"),
            P("seq"),
            P("seq", None),
            P("seq", None),
            P("seq"),
            P("seq"),
            P("seq"),
            P("seq"),
            P("seq"),
            P("seq", None),
            P("seq"),
            P("seq", None),
            P("seq"),
        ),
        check_vma=False,
    )
```

```python
import jax
import jax.numpy as jnp
from jax import lax
from jax.experimental import pallas as pl
from jax.experimental.pallas import tpu as pltpu
from jax.sharding import PartitionSpec as P

WIN = 64
MESH_ID = pl.DeviceIdType.MESH
BF16 = jnp.bfloat16
F32 = jnp.float32


class Place:
    def __init__(self, seq_count, grp_count):
        self.nc = 2
        self.np = 2 if seq_count % 8 == 0 else 1
        self.nq = self.np
        self.nz = self.nq * self.np
        self.nx = seq_count // (self.nc * self.nz)
        self.ng = grp_count
        self.lead = (self.nq, self.np, self.nx, self.nc)
        self.counts = {
            "q": self.nq, "p": self.np, "z": self.nz, "x": self.nx, "c": self.nc, "g": self.ng,
        }

    def locate(self):
        rank = lax.axis_index("seq")
        z = lax.div(rank, self.nc * self.nx)
        self.at = {
            "c": lax.rem(rank, self.nc),
            "x": lax.rem(lax.div(rank, self.nc), self.nx),
            "z": z,
            "p": lax.rem(z, self.np),
            "q": lax.div(z, self.np),
            "g": lax.axis_index("grp"),
        }
        return self

    def device(self, axis, where):
        at = dict(self.at)
        at[axis] = where
        z = at["z"] if axis == "z" else at["q"] * self.np + at["p"]
        return ((z * self.nx + at["x"]) * self.nc + at["c"], at["g"])

    def others(self, axis):
        count = self.counts[axis]
        return [lax.rem(self.at[axis] + step, count) for step in range(1, count)]

    def greet(self, axes, more):
        barrier = pltpu.get_barrier_semaphore()
        devices = list(more)
        for axis in axes:
            devices += [self.device(axis, where) for where in self.others(axis)]
        for device in devices:
            pl.semaphore_signal(barrier, inc=1, device_id=device, device_id_type=MESH_ID)
        return barrier, len(devices)


class Mail:
    def __init__(self, send_sems, recv_sems):
        self.send_sems, self.recv_sems, self.count, self.sent = send_sems, recv_sems, 0, []

    def send(self, src, dst, device):
        copy = pltpu.make_async_remote_copy(
            src_ref=src,
            dst_ref=dst,
            send_sem=self.send_sems.at[self.count],
            recv_sem=self.recv_sems.at[self.count],
            device_id=device,
            device_id_type=MESH_ID,
        )
        copy.start()
        self.count += 1
        self.sent.append(copy)
        return copy

    def settle(self, copies):
        for copy in copies:
            copy.wait_send()
        gone = {id(copy) for copy in copies}
        self.sent = [copy for copy in self.sent if id(copy) not in gone]

    def finish(self):
        self.settle(list(self.sent))


def each(dims, body):
    count = 1
    for dim in dims:
        count *= dim
    if count == 1:
        body((0,) * len(dims))
        return

    def turn(flat, _):
        index, rest = [], flat
        for dim in reversed(dims):
            index.insert(0, lax.rem(rest, dim))
            rest = lax.div(rest, dim)
        body(tuple(index))
        return 0

    lax.fori_loop(0, count, turn, 0)


class Reduction:
    def __init__(self, place, rows, wide, order, groups=True):
        self.place, self.rows, self.wide, self.order, self.groups = place, rows, wide, order, groups
        self.split = "g" in order
        axes = ["q", "p", "x"]
        self.part = wide
        if self.split:
            axes.insert(0, "g")
            self.part = wide // place.ng
        self.axes = axes
        lead = tuple(place.counts[axis] for axis in axes)
        self.boxes = [lead + (rows, self.part)]
        self.copies = place.ng if self.split else 1
        left = list(axes)
        for axis in order:
            left.remove(axis)
            others = place.counts[axis] - 1
            self.copies += others
            lead = tuple(place.counts[one] for one in left)
            self.boxes.append((max(others, 1),) + lead + (rows, self.part))
        if groups:
            self.boxes.append((place.ng, rows, self.part))
            self.copies += place.ng - 1

    def scratch(self):
        return [pltpu.VMEM(box, BF16) for box in self.boxes]

    def bind(self, mail, refs, src, first, out):
        place, part = self.place, self.part
        here = place.at
        pieces = place.ng if self.split else 1
        state = {}
        self.freed = False

        def start():
            far = place.others("c")[0]
            device = place.device("c", far)
            state["wait"] = []
            for i in range(pieces):
                view = src.at[:, :, :, far, :, pl.ds(first + i * part, part)]
                target = refs[0].at[i] if self.split else refs[0]
                state["wait"].append(mail.send(view, target, device))

        def send(level):
            axis = self.order[level]
            current, axes = state["current"], state["axes"]
            spot = axes.index(axis)
            state["spot"] = spot
            state["wait"] = [
                mail.send(
                    current.at[(slice(None),) * spot + (far,)],
                    refs[level + 1].at[i],
                    place.device(axis, far),
                )
                for i, far in enumerate(place.others(axis))
            ]

        def after_core():
            for copy in state["wait"]:
                copy.wait_recv()
            box = refs[0]

            def add(index):
                for i in range(pieces):
                    at = (i,) + index if self.split else index
                    mine = src[index + (here["c"], slice(None), pl.ds(first + i * part, part))]
                    box[at] = (mine.astype(F32) + box[at].astype(F32)).astype(BF16)

            each(place.lead[:3], add)
            mail.settle(state["wait"])
            self.freed = True
            state["current"], state["axes"] = box, list(self.axes)
            send(0)

        def after(level):
            def run():
                for copy in state["wait"]:
                    copy.wait_recv()
                axis, spot, current = self.order[level], state["spot"], state["current"]
                axes = [one for one in state["axes"] if one != axis]
                box = refs[level + 1]

                def total(index):
                    at = index[:spot] + (here[axis],) + index[spot:]
                    value = current[at].astype(F32)
                    for i in range(place.counts[axis] - 1):
                        value = value + box[(i,) + index].astype(F32)
                    return value

                if level + 1 < len(self.order):

                    def add(index):
                        box[(0,) + index] = total(index).astype(BF16)

                    each(tuple(place.counts[one] for one in axes), add)
                    state["current"], state["axes"] = box.at[0], axes
                    send(level + 1)
                    return
                value = total(())
                if not self.groups:
                    out(0, value)
                    return
                last = refs[-1]
                mine = here["g"]
                last[mine] = value.astype(BF16)
                state["wait"] = [
                    mail.send(last.at[mine], last.at[mine], place.device("g", far))
                    for far in place.others("g")
                ]

            return run

        def end():
            for copy in state["wait"]:
                copy.wait_recv()
            last = refs[-1]
            if self.split:
                for i in range(place.ng):
                    out(i * part, last[i].astype(F32))
                return
            value = last[0].astype(F32)
            for i in range(1, place.ng):
                value = value + last[i].astype(F32)
            out(0, value)

        self.stages = [start, after_core] + [after(level) for level in range(len(self.order))]
        if self.groups:
            self.stages.append(end)
        return self


class Total:
    axes = "cxpqg"

    def __init__(self, place, shape):
        self.place, self.shape = place, shape
        self.counts = [place.counts[axis] for axis in self.axes]
        self.copies = sum(count - 1 for count in self.counts)

    def scratch(self):
        return [
            pltpu.VMEM((count,) + self.shape, BF16 if level else F32)
            for level, count in enumerate(self.counts)
        ]

    def bind(self, mail, refs, src, out):
        pending = {}
        place = self.place

        def stage(level):
            def run():
                if level == 0:
                    value = src()
                else:
                    for copy in pending[level - 1]:
                        copy.wait_recv()
                    box = refs[level - 1]
                    value = box[0].astype(F32)
                    for i in range(1, self.counts[level - 1]):
                        value = value + box[i].astype(F32)
                if level == len(self.axes):
                    out(value)
                    return
                box, axis = refs[level], self.axes[level]
                here = place.at[axis]
                box[here] = value.astype(box.dtype)
                pending[level] = [
                    mail.send(box.at[here], box.at[here], place.device(axis, far))
                    for far in place.others(axis)
                ]

            return run

        self.stages = [stage(level) for level in range(len(self.axes) + 1)]
        return self

NT = (((1,), (1,)), ((), ()))
TN = (((0,), (0,)), ((), ()))
NEG_FILL = -1e30
QUAD = 4
WHOLE = pl.BlockSpec(memory_space=pltpu.VMEM)
FAR = pl.BlockSpec(memory_space=pl.ANY)
LIMIT = 63 * 2**20
CURVE = 0.7978845608028654
CUBE = 0.044715


def dot(a, b, dims=(((1,), (0,)), ((), ()))):
    return lax.dot_general(a, b, dims, preferred_element_type=F32)


class Porter:
    def __init__(self, sems, sources, places):
        self.sems, self.count, self.out = sems, 0, []
        self.coming = {}
        for source, place in zip(sources, places):
            copy = pltpu.make_async_copy(source, place, self.sems.at[self.count])
            copy.start()
            self.count += 1
            self.coming[id(place)] = copy

    def need(self, *places):
        for place in places:
            copy = self.coming.pop(id(place), None)
            if copy is not None:
                copy.wait()

    def ship(self, place, target):
        copy = pltpu.make_async_copy(place, target, self.sems.at[self.count])
        copy.start()
        self.count += 1
        self.out.append(copy)

    def finish(self):
        for copy in list(self.coming.values()) + self.out:
            copy.wait()


def like(arrays):
    return [pltpu.VMEM(array.shape, array.dtype) for array in arrays]


def row(ref):
    return ref[...].reshape(1, ref.shape[0])


def norm_parts(values):
    center = values - jnp.mean(values, axis=-1, keepdims=True)
    root = lax.rsqrt(jnp.mean(center * center, axis=-1, keepdims=True) + 1e-05)
    return center * root, root


def norm_back(grad, hat, root, gain):
    gx = grad * gain
    return root * (
        gx - jnp.mean(gx, axis=-1, keepdims=True) - hat * jnp.mean(gx * hat, axis=-1, keepdims=True)
    )


def hot_columns(index_row, count):
    rows = lax.broadcasted_iota(jnp.int32, (count, index_row.shape[1]), 0)
    return jnp.where(rows == index_row, 1.0, 0.0).astype(BF16)


def selected_row(sel_ref, seq):
    return jnp.concatenate([sel_ref[seq, b : b + 1, :] for b in range(sel_ref.shape[1])], axis=1)


def spread_heads(rows, size):
    lane_head = lax.broadcasted_iota(jnp.int32, rows.shape, 1) // size
    zero = jnp.zeros_like(rows)
    return jnp.concatenate([jnp.where(lane_head == h, rows, zero) for h in range(QUAD)], axis=0)


def merge_heads(wide, size):
    count = wide.shape[0] // QUAD
    lane_head = lax.broadcasted_iota(jnp.int32, (count, wide.shape[1]), 1) // size
    result = wide[:count]
    for h in range(1, QUAD):
        result = jnp.where(lane_head == h, wide[h * count : (h + 1) * count], result)
    return result


def window_bias(base, length):
    shape = (2 * WIN, QUAD * WIN)
    key = lax.broadcasted_iota(jnp.int32, shape, 0)
    query = lax.broadcasted_iota(jnp.int32, shape, 1) % WIN
    key_pos = key + (base - WIN)
    keep = (
        (key > query)
        & (key <= query + WIN)
        & (key_pos >= 0)
        & ((key_pos < length) | (key == query + WIN))
    )
    return jnp.where(keep, 0.0, NEG_FILL).astype(F32)


def keys_of(ext_ref, sel_ref, seq, start, rows_at, cols):
    return jnp.concatenate(
        [ext_ref[seq, pl.ds(start, 2 * WIN), cols], sel_ref[pl.ds(rows_at, WIN), cols]], axis=0
    )


def opening(place, tokens, candidates, selected, lengths, gain, shift, weight_qkv, bias_query, bias_value, score_rows):
    rows, width = tokens.shape
    seq_count, ranks, cands = candidates.shape
    tok = rows // seq_count
    blocks = tok // WIN
    every = ranks * cands
    heads = score_rows.shape[0]
    head_size = width // heads
    nz, nx, nc = place.nz, place.nx, place.nc
    copies = 1 + (nz - 1) + (nx - 1) * nz + nz * nx
    scale = head_size ** (-0.5)
    picks = blocks * WIN

    def kernel(
        len_ref, tok_ref, cand_ref, sel_ref, gain_ref, shift_ref, w_far, bq_ref, bv_ref, ws_ref,
        normed_far, q_far, ext_far, halo_far, nsel_far, ksel_far, bias_far, score_far,
        w_ref, normed_ref, q_ref, ext_ref, halo_ref, nsel_ref, ksel_ref, bias_ref, score_ref,
        gat, halo_out, halo_in, move_sems, send_sems, recv_sems,
    ):
        porter = Porter(move_sems, [w_far], [w_ref])
        place.locate()
        mail = Mail(send_sems, recv_sems)
        z, x, c, g = (place.at[axis] for axis in "zxcg")
        rank = lax.axis_index("seq")
        after = (lax.rem(rank + 1, ranks), g)
        before = (lax.rem(rank + ranks - 1, ranks), g)
        barrier = pltpu.get_barrier_semaphore()
        greeted = [after, before]
        for axis in "czx":
            greeted += [place.device(axis, where) for where in place.others(axis)]
        for device in greeted:
            pl.semaphore_signal(barrier, inc=1, device_id=device, device_id_type=MESH_ID)
        gain_row, shift_row = row(gain_ref), row(shift_ref)

        def norm(values):
            return (norm_parts(values.astype(F32))[0] * gain_row + shift_row).astype(BF16)

        for seq in range(seq_count):
            hot = hot_columns(cand_ref[seq, pl.ds(rank, 1), :], tok)
            gat[seq, z, x, c] = norm(dot(hot, tok_ref[pl.ds(seq * tok, tok), :], TN))
            halo_out[seq] = norm(tok_ref[pl.ds((seq + 1) * tok - WIN, WIN), :])
        pl.semaphore_wait(barrier, len(greeted))

        def slot(zi, xi, ci):
            return gat.at[:, zi, xi, ci]

        by_z = [
            mail.send(slot(z, x, c), slot(z, x, c), place.device("z", far))
            for far in place.others("z")
        ]
        halo_copy = mail.send(halo_out, halo_in, after)
        core = place.device("c", place.others("c")[0])
        by_x, by_c = [], []

        def forward_x(zi):
            by_x.append(
                [
                    mail.send(slot(zi, x, c), slot(zi, x, c), place.device("x", far))
                    for far in place.others("x")
                ]
            )
            by_c.append(mail.send(slot(zi, x, c), slot(zi, x, c), core))

        def forward_c(zi, step):
            for i, copy in enumerate(by_x[step]):
                copy.wait_recv()
                come = lax.rem(x + nx - 1 - i, nx)
                by_c.append(mail.send(slot(zi, come, c), slot(zi, come, c), core))

        forward_x(z)
        for seq in range(seq_count):
            normed_ref[pl.ds(seq * tok, tok), :] = norm(tok_ref[pl.ds(seq * tok, tok), :])
        sources = [z] + [lax.rem(z + nz - 1 - i, nz) for i in range(nz - 1)]
        porter.ship(normed_ref, normed_far)
        porter.need(w_ref)
        queries = dot(normed_ref[...], w_ref[:, :width]) + row(bq_ref)
        q_ref[...] = (queries.astype(BF16).astype(F32) * scale).astype(BF16)
        porter.ship(q_ref, q_far)
        value_bias = row(bv_ref)
        for i in range(nz - 1):
            by_z[i].wait_recv()
            forward_x(sources[i + 1])
        forward_c(sources[0], 0)

        def project(values, half):
            part = dot(values, w_ref[:, pl.ds((1 + half) * width, width)])
            if half == 1:
                part = part + value_bias
            return part.astype(BF16)

        for half in range(2):
            cols = pl.ds(half * width, width)
            for seq in range(seq_count):
                ext_ref[seq, pl.ds(WIN, tok), cols] = project(
                    normed_ref[pl.ds(seq * tok, tok), :], half
                )
        halo_copy.wait_recv()
        for seq in range(seq_count):
            halo_ref[pl.ds(seq * WIN, WIN), :] = halo_in[seq]
        for half in range(2):
            part = project(halo_ref[...], half)
            for seq in range(seq_count):
                ext_ref[seq, pl.ds(0, WIN), pl.ds(half * width, width)] = part[
                    seq * WIN : (seq + 1) * WIN
                ]
        porter.ship(halo_ref, halo_far)
        porter.ship(ext_ref, ext_far)
        counted = []
        for seq in range(seq_count):
            index = selected_row(sel_ref, seq)
            inner = hot_columns(index % cands, cands)
            table = cand_ref[seq].astype(F32).astype(BF16)
            offset = dot(table, inner)
            block_of = lax.broadcasted_iota(jnp.int32, (ranks, picks), 0)
            chosen = jnp.where(block_of == index // cands, offset, 0.0)
            position = jnp.sum(chosen, axis=0, keepdims=True)
            position = position + ((index // cands) * tok).astype(F32)
            lane_block = lax.broadcasted_iota(jnp.int32, (1, picks), 1) // WIN
            limit = jnp.minimum((rank * blocks + lane_block) * WIN - WIN + 1, len_ref[seq])
            flag = jnp.where(position < limit.astype(F32), 1.0, 0.0)
            across = lax.broadcasted_iota(jnp.int32, (picks, picks), 0)
            down = lax.broadcasted_iota(jnp.int32, (picks, picks), 1)
            diagonal = jnp.where(across == down, flag, 0.0).astype(BF16)
            counted.append(dot(diagonal, jnp.ones((picks, width), BF16)))
        head_of = lax.broadcasted_iota(jnp.int32, (heads, width), 1) // head_size
        widen = jnp.where(head_of == lax.broadcasted_iota(jnp.int32, (heads, width), 0), 1.0, 0.0)
        score_ref[...] = jnp.zeros_like(score_ref)
        for i in range(1, nz):
            forward_c(sources[i], i)
        for copy in by_c:
            copy.wait_recv()
        for seq in range(seq_count):
            here = pl.ds(seq * picks, picks)
            hot = hot_columns(selected_row(sel_ref, seq), every)
            picked = dot(hot, gat[seq].reshape(every, width), TN).astype(BF16)
            nsel_ref[here, :] = picked
            for half in range(2):
                ksel_ref[here, pl.ds(half * width, width)] = project(picked, half)
            score = dot(picked, ws_ref[...], NT).astype(BF16)
            score_ref[here, pl.ds(0, heads)] = score
            wide = dot(score, widen.astype(BF16))
            gate = jnp.minimum(wide, 0.0) - jnp.log1p(jnp.exp(-jnp.abs(wide)))
            bias_ref[here, :] = jnp.where(counted[seq] > 0.5, gate, NEG_FILL)
        porter.ship(nsel_ref, nsel_far)
        porter.ship(ksel_ref, ksel_far)
        porter.ship(bias_ref, bias_far)
        porter.ship(score_ref, score_far)
        mail.finish()
        porter.finish()

    shapes = [
        ((rows, width), BF16),
        ((rows, width), BF16),
        ((seq_count, tok + WIN, 2 * width), BF16),
        ((seq_count * WIN, width), BF16),
        ((seq_count * picks, width), BF16),
        ((seq_count * picks, 2 * width), BF16),
        ((seq_count * picks, width), F32),
        ((seq_count * picks, 128), BF16),
    ]
    return pl.pallas_call(
        kernel,
        out_shape=[jax.ShapeDtypeStruct(*shape) for shape in shapes],
        in_specs=[pl.BlockSpec(memory_space=pltpu.SMEM)] + [WHOLE] * 5 + [FAR] + [WHOLE] * 3,
        out_specs=[FAR] * len(shapes),
        scratch_shapes=like([weight_qkv])
        + [pltpu.VMEM(*shape) for shape in shapes]
        + [
            pltpu.VMEM((seq_count, nz, nx, nc, cands, width), BF16),
            pltpu.VMEM((seq_count, WIN, width), BF16),
            pltpu.VMEM((seq_count, WIN, width), BF16),
            pltpu.SemaphoreType.DMA((1 + len(shapes),)),
            pltpu.SemaphoreType.DMA((copies,)),
            pltpu.SemaphoreType.DMA((copies,)),
        ],
        compiler_params=pltpu.CompilerParams(
            collective_id=2, has_side_effects=True, vmem_limit_bytes=LIMIT
        ),
    )(lengths, tokens, candidates, selected, gain, shift, weight_qkv, bias_query, bias_value, score_rows)


def middle_part(lengths, queries, ext, ksel, bias_sel, tokens, dy, weight_out, bias_out, gain, shift, weight_up, bias_up, weight_down, bias_down, head_size):
    rows, width = tokens.shape
    seq_count, ext_rows, _ = ext.shape
    tok = ext_rows - WIN
    blocks = tok // WIN
    lanes = QUAD * head_size
    quads = width // lanes
    hidden_size = bias_up.shape[0]
    parts = hidden_size // width

    def kernel(
        len_ref, bo_ref, gain_ref, shift_ref, bu_ref, bd_ref, *refs
    ):
        far_in, far_out = refs[:9], refs[9:19]
        near_in, near_out, move_sems = refs[19:28], refs[28:38], refs[38]
        q_ref, ext_ref, sel_ref, bias_ref, tok_ref, wo_ref, dy_ref, wu_ref, wd_ref = near_in
        att_ref, prob_ref, mixed_ref, hidden_ref, gpre_ref, n2_ref, branch_ref, gmid_ref, gatt_ref, vec_ref = near_out
        porter = Porter(move_sems, far_in, near_in)
        porter.need(q_ref, ext_ref, sel_ref, bias_ref)

        def ship(ref):
            porter.ship(ref, far_out[[one is ref for one in near_out].index(True)])

        base = lax.axis_index("seq") * tok

        def attend(i, _):
            seq, block = lax.div(i, blocks), lax.rem(i, blocks)
            at = pl.multiple_of(i * WIN, WIN)
            start = pl.multiple_of(block * WIN, WIN)
            mask = window_bias(base + block * WIN, len_ref[seq])
            for quad in range(quads):
                cols = pl.ds(quad * lanes, lanes)
                vals = pl.ds(width + quad * lanes, lanes)
                keys = keys_of(ext_ref, sel_ref, seq, start, at, cols)
                values = keys_of(ext_ref, sel_ref, seq, start, at, vals)
                wide = spread_heads(q_ref[pl.ds(at, WIN), cols], head_size)
                logits = dot(keys, wide, NT)
                logits = logits + jnp.concatenate([mask, bias_ref[pl.ds(at, WIN), cols]], axis=0)
                grown = jnp.exp(logits - jnp.max(logits, axis=0, keepdims=True))
                probs = (grown / jnp.sum(grown, axis=0, keepdims=True)).astype(BF16)
                prob_ref[i, quad] = probs
                att_ref[pl.ds(at, WIN), cols] = merge_heads(
                    dot(probs, values, TN), head_size
                ).astype(BF16)
            return 0

        lax.fori_loop(0, seq_count * blocks, attend, 0)
        ship(att_ref)
        ship(prob_ref)
        porter.need(tok_ref, wo_ref)
        gain_row = row(gain_ref)
        middle = tok_ref[...].astype(F32) + dot(att_ref[...], wo_ref[...]) + row(bo_ref)
        gmid_ref[...] = middle
        hat, _ = norm_parts(middle)
        n2_ref[...] = (hat * gain_row + row(shift_ref)).astype(BF16)
        ship(n2_ref)
        porter.need(dy_ref, wu_ref, wd_ref)
        bias_row = row(bu_ref)
        mixed = middle + row(bd_ref)
        grad_normed = jnp.zeros((rows, width), F32)
        for part in range(parts):
            cols = pl.ds(part * width, width)
            pre = dot(n2_ref[...], wu_ref[:, cols]) + bias_row[:, part * width : (part + 1) * width]
            square = pre * pre
            tanh = jnp.tanh(CURVE * pre * (1.0 + CUBE * square))
            half = 0.5 + 0.5 * tanh
            hidden_ref[:, cols] = (pre * half).astype(BF16)
            slope = half + 0.5 * pre * (1.0 - tanh * tanh) * (CURVE + 3 * CUBE * CURVE * square)
            gpre = (dot(dy_ref[...], wd_ref[cols, :], NT) * slope).astype(BF16)
            gpre_ref[:, cols] = gpre
            vec_ref[pl.ds(8 + part, 1), :] = jnp.sum(gpre.astype(F32), axis=0, keepdims=True)
            mixed = mixed + dot(hidden_ref[:, cols], wd_ref[cols, :])
            grad_normed = grad_normed + dot(gpre, wu_ref[:, cols], NT)
        ship(hidden_ref)
        ship(gpre_ref)
        mixed_ref[...] = mixed.astype(BF16)
        ship(mixed_ref)
        hat, root = norm_parts(gmid_ref[...])
        dy_wide = dy_ref[...].astype(F32)
        vec_ref[0:4, :] = jnp.zeros((4, width), F32)
        vec_ref[5:6, :] = jnp.sum(grad_normed * hat, axis=0, keepdims=True)
        vec_ref[6:7, :] = jnp.sum(grad_normed, axis=0, keepdims=True)
        vec_ref[7:8, :] = jnp.sum(dy_wide, axis=0, keepdims=True)
        grad_middle = dy_wide + norm_back(grad_normed, hat, root, gain_row)
        gmid_ref[...] = grad_middle
        ship(gmid_ref)
        branch = grad_middle.astype(BF16)
        branch_ref[...] = branch
        ship(branch_ref)
        vec_ref[4:5, :] = jnp.sum(branch.astype(F32), axis=0, keepdims=True)
        ship(vec_ref)
        gatt_ref[...] = dot(branch, wo_ref[...], NT).astype(BF16)
        ship(gatt_ref)
        porter.finish()

    large = (queries, ext, ksel, bias_sel, tokens, weight_out, dy, weight_up, weight_down)
    shapes = [
        ((rows, width), BF16),
        ((seq_count * blocks, quads, 3 * WIN, QUAD * WIN), BF16),
        ((rows, width), BF16),
        ((rows, hidden_size), BF16),
        ((rows, hidden_size), BF16),
        ((rows, width), BF16),
        ((rows, width), BF16),
        ((rows, width), F32),
        ((rows, width), BF16),
        ((8 + parts, width), F32),
    ]
    return pl.pallas_call(
        kernel,
        out_shape=[jax.ShapeDtypeStruct(*shape) for shape in shapes],
        in_specs=[pl.BlockSpec(memory_space=pltpu.SMEM)] + [WHOLE] * 5 + [FAR] * len(large),
        out_specs=[FAR] * len(shapes),
        scratch_shapes=like(large)
        + [pltpu.VMEM(*shape) for shape in shapes]
        + [pltpu.SemaphoreType.DMA((len(large) + len(shapes),))],
        compiler_params=pltpu.CompilerParams(vmem_limit_bytes=LIMIT),
    )(lengths, bias_out, gain, shift, bias_up, bias_down, *large)

SCHEDULE = (
    "cd2", "bd2", "cq0a", "cq0b", "ad2", "cd0", "bd0", "cfin0", "ad0", "bq0", "cq1a", "aq0",
    "cu0", "bu0", "co", "bo", "cu1", "ad2", "au0", "ao", "bu1", "cd1", "bd1", "cu3",
    "au1", "aq0", "ad1", "bu3", "cq1b", "au3", "ad0", "cfin1", "ad2", "au1", "ao", "bq1",
    "cu2", "aq0", "bu2", "cq2a", "au2", "aq1", "ad0", "ao", "au0", "cq2b", "ad1", "ad2",
    "aq0", "cfin2", "au1", "ad2", "ao", "bq2", "au3", "aq1", "ad0", "aq0", "au0", "aq2",
    "au2", "ad2", "cgive", "au3", "ad1", "aq1", "au1", "ao", "aq0", "ad0", "bs", "bb0",
    "bb1", "bt", "at", "au0", "aq2", "ab1", "au2", "ab0", "au3", "au1", "ad1", "at",
    "aq1", "ad0", "ao", "au0", "au3", "au1", "au2", "aq2", "as", "at", "au3", "ad1",
    "aq1", "au0", "ab1", "ab0", "au2", "ad1", "aq2", "at", "aq1", "ab1", "au2", "ab0",
    "at", "aq2", "aq2", "ab1", "ab0",
)
ORDERS = {
    "b0": "xpq",
    "b1": "pxq",
    "d0": "xgpq",
    "d1": "xpgq",
    "d2": "xqpg",
    "o": "pgxq",
    "q0": "gxpq",
    "q1": "xgqp",
    "q2": "xgpq",
    "u0": "xgqp",
    "u1": "gpqx",
    "u2": "gpxq",
    "u3": "qxpg",
}

class Shift:
    copies = 1

    def __init__(self, shape):
        self.shape = shape

    def scratch(self):
        return [pltpu.VMEM(self.shape, BF16)]

    def bind(self, mail, refs, src, device, out):
        held = []

        def start():
            held.append(mail.send(src, refs[0], device))

        def finish():
            held[0].wait_recv()
            out(refs[0][...])

        self.stages = [start, finish]
        return self


def closing(place, gradients, attention, weight_qkv, score_rows, selected, gain, shift, tokens, vec, head_size):
    hidden, dy, gpre, n2, branch, attended = gradients
    queries, ext, ksel, probs, score, gatt, normed, halo, nsel = attention
    rows, width = dy.shape
    seq_count, ext_rows, _ = ext.shape
    tok = ext_rows - WIN
    blocks = tok // WIN
    steps = seq_count * blocks
    lanes = QUAD * head_size
    quads = width // lanes
    heads = score_rows.shape[0]
    hidden_size = hidden.shape[1]
    parts = hidden_size // width
    large = tuple(gradients) + tuple(attention) + (weight_qkv, tokens)
    ng = place.ng
    lead = place.lead
    ranks = place.nz * place.nx * place.nc
    share = width // ranks
    down_share = hidden_size // ranks
    down_wide = 256
    every_row = vec.shape[0] + heads
    picks = blocks * WIN
    cands = 32
    scale = head_size ** (-0.5)
    can_split = width % (128 * ng) == 0 and down_wide % (128 * ng) == 0
    def order(name):
        given = ORDERS[name]
        return given if can_split else given.replace("g", "")

    def reduction(name, piece_rows, wide, groups=True):
        return Reduction(place, piece_rows, wide, order(name), groups)

    downs = [reduction(f"d{i}", down_share, down_wide) for i in range(width // down_wide)]
    ups = [reduction(f"u{i}", share, width) for i in range(parts)]
    out_task = reduction("o", share, width)
    qkvs = [reduction(f"q{i}", share, width) for i in range(quads)]
    back_wide = width // 2
    backs = [reduction(f"b{i}", seq_count * cands, back_wide, False) for i in range(2)]
    total = Total(place, (every_row, width))
    shift_task = Shift((seq_count, WIN, width))
    tasks = downs + ups + [out_task] + qkvs + backs + [total, shift_task]
    boxes, counts = [], []
    for task in tasks:
        mine = task.scratch()
        boxes.extend(mine)
        counts.append(len(mine))
    copies = sum(task.copies for task in tasks)
    slots, down_slots = 3, 2
    work = [
        pltpu.VMEM((slots,) + lead + (share, width), BF16),
        pltpu.VMEM((down_slots,) + lead + (down_share, down_wide), BF16),
        pltpu.VMEM(lead + (seq_count * cands, width), BF16),
        pltpu.VMEM((seq_count, WIN, width), BF16),
        pltpu.VMEM((rows, lanes), BF16),
        pltpu.VMEM((seq_count, ext_rows, 2 * lanes), F32),
        pltpu.VMEM((seq_count * picks, 2 * lanes), BF16),
        pltpu.VMEM((seq_count * picks, 128), F32),
        pltpu.VMEM((seq_count * picks, width), F32),
        pltpu.VMEM((seq_count * WIN, width), F32),
        pltpu.VMEM((every_row, width), F32),
    ]

    def kernel(*refs):
        ws_ref, pick_ref, gain_ref, shift_ref, vec_ref = refs[:5]
        far = refs[5 : 5 + len(large)]
        refs = refs[5 + len(large) :]
        gqkv_ref, gout_ref, gup_ref, gdown_ref, total_ref, gn_ref, cand_ref, back_ref = refs[:8]
        near = refs[8 : 8 + len(large)]
        (
            hid_ref, dy_ref, gpre_ref, n2_ref, branch_ref, att_ref,
            q_ref, ext_ref, sel_ref, prob_ref, score_ref, gatt_ref, normed_ref, halo_ref, nsel_ref,
            w_ref, tok_ref,
        ) = near
        porter = Porter(refs[8 + len(large)], far, near)
        rest = list(refs[9 + len(large) :])
        recv_sems, send_sems = rest.pop(), rest.pop()
        stage, down_stage, back_src, halo_src, gq_ref, acc, gsel_ref, gates, gn_sel, gn_halo, own_vec = rest[-11:]
        room = rest[:-11]
        place.locate()
        mail = Mail(send_sems, recv_sems)
        rank, g = lax.axis_index("seq"), lax.axis_index("grp")
        after = (lax.rem(rank + 1, ranks), g)
        before = (lax.rem(rank + ranks - 1, ranks), g)
        barrier, answers = place.greet("cxpqg", [after, before])
        pl.semaphore_wait(barrier, answers)
        taken = {}
        for task, count in zip(tasks, counts):
            taken[id(task)] = room[:count]
            del room[:count]

        def column_writer(out, first):
            def write(offset, value):
                out[:, pl.ds(first + offset, value.shape[1])] = value

            return write

        def quad_writer(quad):
            def write(offset, value):
                wide = value.shape[1]
                low = offset
                while low < offset + wide:
                    kind = low // lanes
                    high = min(offset + wide, (kind + 1) * lanes)
                    at = kind * width + quad * lanes + low - kind * lanes
                    gqkv_ref[:, pl.ds(at, high - low)] = value[:, low - offset : high - offset]
                    low = high

            return write

        used = [0, 0]

        holders = [[None] * slots, [None] * down_slots]

        def bind(task, which, out):
            count = (slots, down_slots)[which]
            spot = used[which] % count
            used[which] += 1
            held = holders[which][spot]
            while held is not None and not held.freed:
                held.stages.pop(0)()
            holders[which][spot] = task
            src = (stage, down_stage)[which].at[spot]
            task.bind(mail, taken[id(task)], src, 0, out)
            return src

        def fill(src, left, right):
            value = dot(left, right, TN).astype(BF16)
            src[...] = value.reshape(src.shape)

        def down(i):
            porter.need(hid_ref, dy_ref)
            src = bind(downs[i], 1, column_writer(gdown_ref, i * down_wide))
            fill(src, hid_ref[...], dy_ref[:, i * down_wide : (i + 1) * down_wide])
            return downs[i]

        def up(i):
            porter.need(n2_ref, gpre_ref)
            src = bind(ups[i], 0, column_writer(gup_ref, i * width))
            fill(src, n2_ref[...], gpre_ref[:, i * width : (i + 1) * width])
            return ups[i]

        def out():
            porter.need(att_ref, branch_ref)
            src = bind(out_task, 0, column_writer(gout_ref, 0))
            fill(src, att_ref[...], branch_ref[...])
            return out_task

        def attend_back(quad, first, last):
            cols = pl.ds(quad * lanes, lanes)
            vals = pl.ds(width + quad * lanes, lanes)

            def step(i, _):
                seq, block = lax.div(i, blocks), lax.rem(i, blocks)
                at = pl.multiple_of(i * WIN, WIN)
                start = pl.multiple_of(block * WIN, WIN)
                keys = keys_of(ext_ref, sel_ref, seq, start, at, cols)
                values = keys_of(ext_ref, sel_ref, seq, start, at, vals)
                wide_q = spread_heads(q_ref[pl.ds(at, WIN), cols], head_size)
                wide_g = spread_heads(gatt_ref[pl.ds(at, WIN), cols], head_size)
                low_probs = prob_ref[i, quad]
                full = low_probs.astype(F32)
                weighed = full * dot(values, wide_g, NT)
                delta = jnp.sum(weighed, axis=0, keepdims=True)
                low = (weighed - full * delta).astype(BF16)
                grad_values = dot(low_probs, wide_g)
                grad_keys = dot(low, wide_q)
                gq = merge_heads(dot(low, keys, TN), head_size) * scale
                gq_ref[pl.ds(at, WIN), :] = gq.astype(BF16)
                acc[seq, pl.ds(start, 2 * WIN), :lanes] += grad_keys[: 2 * WIN]
                acc[seq, pl.ds(start, 2 * WIN), lanes:] += grad_values[: 2 * WIN]
                gsel_ref[pl.ds(at, WIN), :lanes] = grad_keys[2 * WIN :].astype(BF16)
                gsel_ref[pl.ds(at, WIN), lanes:] = grad_values[2 * WIN :].astype(BF16)
                head = lax.broadcasted_iota(jnp.int32, (lanes, 128), 0) // head_size + quad * QUAD
                pick = jnp.where(head == lax.broadcasted_iota(jnp.int32, (lanes, 128), 1), 1.0, 0.0)
                gates[pl.ds(at, WIN), :] += dot(low[2 * WIN :], pick.astype(BF16))
                return 0

            porter.need(q_ref, ext_ref, sel_ref, prob_ref, gatt_ref)
            if first == 0:
                acc[...] = jnp.zeros_like(acc)
            lax.fori_loop(first, last, step, 0)

        def finish_quad(quad):
            porter.need(normed_ref, halo_ref, nsel_ref, w_ref)
            src = bind(qkvs[quad], 0, quad_writer(quad))
            gq = gq_ref[...]
            gown = jnp.concatenate([acc[seq, WIN:, :] for seq in range(seq_count)], axis=0).astype(BF16)
            ghalo = jnp.concatenate([acc[seq, :WIN, :] for seq in range(seq_count)], axis=0).astype(BF16)
            gsel = gsel_ref[...]
            src[:, :, :, :, :, :lanes] = (
                dot(normed_ref[...], gq, TN).astype(BF16).reshape(lead + (share, lanes))
            )
            both = dot(normed_ref[...], gown, TN) + dot(halo_ref[...], ghalo, TN) + dot(nsel_ref[...], gsel, TN)
            src[:, :, :, :, :, lanes:] = both.astype(BF16).reshape(lead + (share, 2 * lanes))
            spots = [pl.ds(kind * width + quad * lanes, lanes) for kind in range(3)]
            own = dot(gq, w_ref[:, spots[0]], NT)
            own = own + dot(gown[:, :lanes], w_ref[:, spots[1]], NT)
            own = own + dot(gown[:, lanes:], w_ref[:, spots[2]], NT)
            near = dot(ghalo[:, :lanes], w_ref[:, spots[1]], NT) + dot(ghalo[:, lanes:], w_ref[:, spots[2]], NT)
            chosen = dot(gsel[:, :lanes], w_ref[:, spots[1]], NT) + dot(gsel[:, lanes:], w_ref[:, spots[2]], NT)
            if quad == 0:
                gn_ref[...], gn_halo[...], gn_sel[...] = own, near, chosen
            else:
                gn_ref[...] += own
                gn_halo[...] += near
                gn_sel[...] += chosen
            cols = pl.ds(quad * lanes, lanes)
            own_vec[0:1, cols] = jnp.sum(gq.astype(F32), axis=0, keepdims=True)
            own_vec[1:2, cols] = (
                jnp.sum(gown[:, lanes:].astype(F32), axis=0, keepdims=True)
                + jnp.sum(ghalo[:, lanes:].astype(F32), axis=0, keepdims=True)
                + jnp.sum(gsel[:, lanes:].astype(F32), axis=0, keepdims=True)
            )
            return qkvs[quad]

        def give_back():
            porter.need(score_ref, tok_ref)
            score_now = score_ref[...].astype(F32)
            gscore = (gates[...] / (1.0 + jnp.exp(score_now))).astype(BF16)
            chosen = gn_sel[...] + dot(gscore[:, :heads], ws_ref[...])
            low = chosen.astype(BF16)
            for seq in range(seq_count):
                hot = hot_columns(selected_row(pick_ref, seq), ranks * cands)
                terms = dot(hot, low[seq * picks : (seq + 1) * picks]).astype(BF16)
                back_src[:, :, :, :, pl.ds(seq * cands, cands), :] = terms.reshape(lead + (cands, width))
                halo_src[seq] = gn_halo[pl.ds(seq * WIN, WIN), :].astype(BF16)
            for i, task in enumerate(backs):
                task.bind(mail, taken[id(task)], back_src, i * back_wide, column_writer(cand_ref, i * back_wide))

            def halo_write(value):
                back_ref[...] = value

            shift_task.bind(mail, taken[id(shift_task)], halo_src, before, halo_write)
            gain_row, shift_row = row(gain_ref), row(shift_ref)
            hat, _ = norm_parts(tok_ref[...].astype(F32))

            def hat_of(ref):
                return (ref[...].astype(F32) - shift_row) / gain_row

            own, near = gn_ref[...], gn_halo[...]
            own_vec[2:3, :] = (
                jnp.sum(own * hat, axis=0, keepdims=True)
                + jnp.sum(near * hat_of(halo_ref), axis=0, keepdims=True)
                + jnp.sum(chosen * hat_of(nsel_ref), axis=0, keepdims=True)
            )
            own_vec[3:4, :] = (
                jnp.sum(own, axis=0, keepdims=True)
                + jnp.sum(near, axis=0, keepdims=True)
                + jnp.sum(chosen, axis=0, keepdims=True)
            )
            own_vec[4 : vec_ref.shape[0], :] = vec_ref[4:, :]
            own_vec[vec_ref.shape[0] :, :] = dot(gscore, nsel_ref[...], TN)[:heads]

            def vec_write(value):
                total_ref[...] = value

            total.bind(mail, taken[id(total)], lambda: own_vec[...], vec_write)
            return [shift_task] + backs + [total]

        gates[...] = jnp.zeros_like(gates)
        half = steps // 2
        begun = {"s": shift_task, "t": total, "o": out_task}
        work_of = {"o": out, "give": give_back}
        for i, task in enumerate(downs):
            begun[f"d{i}"], work_of[f"d{i}"] = task, lambda i=i: down(i)
        for i, task in enumerate(ups):
            begun[f"u{i}"], work_of[f"u{i}"] = task, lambda i=i: up(i)
        for i, task in enumerate(qkvs):
            begun[f"q{i}"], work_of[f"fin{i}"] = task, lambda i=i: finish_quad(i)
            work_of[f"q{i}a"] = lambda i=i: attend_back(i, 0, half)
            work_of[f"q{i}b"] = lambda i=i: attend_back(i, half, steps)
        for i, task in enumerate(backs):
            begun[f"b{i}"] = task
        for entry in SCHEDULE:
            what, name = entry[0], entry[1:]
            if what == "c":
                work_of[name]()
            elif begun[name].stages:
                begun[name].stages.pop(0)()
        for task in tasks:
            while task.stages:
                task.stages.pop(0)()
        mail.finish()
        porter.finish()

    shapes = [
        ((share, 3 * width), F32),
        ((share, width), F32),
        ((share, hidden_size), F32),
        ((down_share, width), F32),
        ((every_row, width), F32),
        ((rows, width), F32),
        ((seq_count * cands, width), F32),
        ((seq_count, WIN, width), BF16),
    ]
    return pl.pallas_call(
        kernel,
        out_shape=[jax.ShapeDtypeStruct(*shape) for shape in shapes],
        in_specs=[WHOLE] * 5 + [FAR] * len(large),
        out_specs=[WHOLE] * len(shapes),
        scratch_shapes=like(large)
        + [pltpu.SemaphoreType.DMA((len(large),))]
        + boxes
        + work
        + [pltpu.SemaphoreType.DMA((copies,)), pltpu.SemaphoreType.DMA((copies,))],
        compiler_params=pltpu.CompilerParams(
            collective_id=3, has_side_effects=True, vmem_limit_bytes=LIMIT
        ),
    )(score_rows, selected, gain, shift, vec, *large)


def ending(tokens, candidates, gain, grad_middle, gn, cand_back, halo_back, total, sums, parts, heads, ranks):
    rows, width = tokens.shape
    seq_count, _, cands = candidates.shape
    tok = rows // seq_count
    share = width // ranks
    up_share = parts * share
    vec_rows = total.shape[0]

    def kernel(
        tok_ref, cand_ref, gain_ref, gmid_ref, gn_ref, back_ref, halo_ref, total_ref, *refs
    ):
        grad_ref, small_ref, up_ref, score_ref = refs[len(sums) : len(sums) + 4]
        for came, result in zip(refs[: len(sums)], refs[len(sums) + 4 :]):
            result[...] = came[...]
        rank = lax.axis_index("seq")
        gain_row = row(gain_ref)
        for seq in range(seq_count):
            here = pl.ds(seq * tok, tok)
            hot = hot_columns(cand_ref[seq, pl.ds(rank, 1), :], tok)
            came = back_ref[pl.ds(seq * cands, cands), :].astype(BF16)
            grad = gn_ref[here, :] + dot(hot, came)
            near = halo_ref[seq].astype(F32)
            grad = grad + jnp.concatenate([jnp.zeros((tok - WIN, width), F32), near], axis=0)
            hat, root = norm_parts(tok_ref[here, :].astype(F32))
            grad_ref[here, :] = gmid_ref[here, :] + norm_back(grad, hat, root, gain_row)
        from_row = lax.broadcasted_iota(jnp.int32, (width, share), 0)
        to_col = lax.broadcasted_iota(jnp.int32, (width, share), 1)
        pick = jnp.where(from_row == to_col + rank * share, 1.0, 0.0)
        values = total_ref[...]
        small = lax.dot_general(
            values, pick, (((1,), (0,)), ((), ())),
            precision=lax.Precision.HIGHEST, preferred_element_type=F32,
        )
        small_ref[...] = small[:8]
        score_ref[...] = small[8 + parts :]
        per_row = width // up_share
        from_row = lax.broadcasted_iota(jnp.int32, (width, up_share), 0)
        to_col = lax.broadcasted_iota(jnp.int32, (width, up_share), 1)
        pick = jnp.where(from_row == to_col + lax.rem(rank, per_row) * up_share, 1.0, 0.0)
        ups = lax.dot_general(
            values[8 : 8 + parts], pick, (((1,), (0,)), ((), ())),
            precision=lax.Precision.HIGHEST, preferred_element_type=F32,
        )
        which = lax.broadcasted_iota(jnp.int32, ups.shape, 0)
        up_ref[...] = jnp.sum(
            jnp.where(which == lax.div(rank, per_row), ups, 0.0), axis=0, keepdims=True
        )

    return pl.pallas_call(
        kernel,
        out_shape=[
            jax.ShapeDtypeStruct((rows, width), F32),
            jax.ShapeDtypeStruct((8, share), F32),
            jax.ShapeDtypeStruct((1, up_share), F32),
            jax.ShapeDtypeStruct((heads, share), F32),
        ]
        + [jax.ShapeDtypeStruct(array.shape, array.dtype) for array in sums],
        in_specs=[WHOLE] * (8 + len(sums)),
        out_specs=[WHOLE] * (4 + len(sums)),
        compiler_params=pltpu.CompilerParams(vmem_limit_bytes=LIMIT),
    )(tokens, candidates, gain, grad_middle, gn, cand_back, halo_back, total, *sums)


def per_device(
    tokens,
    weight_qkv,
    bias_query,
    bias_value,
    weight_score,
    weight_out,
    bias_out,
    gain_one,
    shift_one,
    gain_two,
    shift_two,
    weight_up,
    bias_up,
    weight_down,
    bias_down,
    cotangent,
    lengths,
    candidates,
    selected,
):
    seq_count, tok, width = tokens.shape
    heads = weight_score.shape[1]
    head_size = width // heads
    rows = seq_count * tok
    ranks = lax.axis_size("seq")
    place = Place(ranks, lax.axis_size("grp"))
    parts = bias_up.shape[0] // width
    flat = tokens.reshape(rows, width)
    dy = cotangent.reshape(rows, width)
    normed, queries, ext, halo, nsel, ksel, bias_sel, score = opening(
        place, flat, candidates, selected, lengths, gain_one, shift_one,
        weight_qkv, bias_query, bias_value, weight_score.T,
    )
    attended, probs, mixed, hidden, gpre, n2, branch, grad_middle, gatt, vec = middle_part(
        lengths, queries, ext, ksel, bias_sel, flat, dy, weight_out, bias_out, gain_two, shift_two,
        weight_up, bias_up, weight_down, bias_down, head_size,
    )
    grad_qkv, grad_out, grad_up, grad_down, total, gn, cand_back, halo_back = closing(
        place,
        (hidden, dy, gpre, n2, branch, attended),
        (queries, ext, ksel, probs, score, gatt, normed, halo, nsel),
        weight_qkv, weight_score.T, selected, gain_one, shift_one, flat, vec, head_size,
    )
    grad_tokens, small, up_row, score_rows, *sums = ending(
        flat, candidates, gain_one, grad_middle, gn, cand_back, halo_back, total,
        (grad_qkv, grad_out, grad_up, grad_down), parts, heads, ranks,
    )
    grad_qkv, grad_out, grad_up, grad_down = sums
    return (
        mixed.reshape(tokens.shape),
        grad_tokens.reshape(tokens.shape),
        grad_qkv,
        small[0],
        small[1],
        score_rows.T,
        grad_out,
        small[4],
        small[2],
        small[3],
        small[5],
        small[6],
        grad_up,
        up_row[0],
        grad_down,
        small[7],
    )


def solution(mesh):
    return jax.shard_map(
        per_device,
        mesh=mesh,
        in_specs=(
            P("grp", "seq", None),
            P(),
            P(),
            P(),
            P(),
            P(),
            P(),
            P(),
            P(),
            P(),
            P(),
            P(),
            P(),
            P(),
            P(),
            P("grp", "seq", None),
            P("grp"),
            P("grp", None, None),
            P("grp", "seq", None),
        ),
        out_specs=(
            P("grp", "seq", None),
            P("grp", "seq", None),
            P("seq", None),
            P("seq"),
            P("seq"),
            P("seq", None),
            P("seq", None),
            P("seq"),
            P("seq"),
            P("seq"),
            P("seq"),
            P("seq"),
            P("seq", None),
            P("seq"),
            P("seq", None),
            P("seq"),
        ),
        check_vma=False,
    )
```

```python
import jax
import jax.numpy as jnp
from jax import lax
from jax.experimental import pallas as pl
from jax.experimental.pallas import tpu as pltpu
from jax.sharding import PartitionSpec as P

WIN = 64
MESH_ID = pl.DeviceIdType.MESH
BF16 = jnp.bfloat16
F32 = jnp.float32


class Place:
    def __init__(self, seq_count, grp_count):
        self.nc = 2
        self.np = 2 if seq_count % 8 == 0 else 1
        self.nq = self.np
        self.nz = self.nq * self.np
        self.nx = seq_count // (self.nc * self.nz)
        self.ng = grp_count
        self.lead = (self.nq, self.np, self.nx, self.nc)
        self.counts = {
            "q": self.nq, "p": self.np, "z": self.nz, "x": self.nx, "c": self.nc, "g": self.ng,
        }

    def locate(self):
        rank = lax.axis_index("seq")
        z = lax.div(rank, self.nc * self.nx)
        self.at = {
            "c": lax.rem(rank, self.nc),
            "x": lax.rem(lax.div(rank, self.nc), self.nx),
            "z": z,
            "p": lax.rem(z, self.np),
            "q": lax.div(z, self.np),
            "g": lax.axis_index("grp"),
        }
        return self

    def device(self, axis, where):
        at = dict(self.at)
        at[axis] = where
        z = at["z"] if axis == "z" else at["q"] * self.np + at["p"]
        return ((z * self.nx + at["x"]) * self.nc + at["c"], at["g"])

    def others(self, axis):
        count = self.counts[axis]
        return [lax.rem(self.at[axis] + step, count) for step in range(1, count)]

    def greet(self, axes, more):
        barrier = pltpu.get_barrier_semaphore()
        devices = list(more)
        for axis in axes:
            devices += [self.device(axis, where) for where in self.others(axis)]
        for device in devices:
            pl.semaphore_signal(barrier, inc=1, device_id=device, device_id_type=MESH_ID)
        return barrier, len(devices)


class Mail:
    def __init__(self, send_sems, recv_sems):
        self.send_sems, self.recv_sems, self.count, self.sent = send_sems, recv_sems, 0, []

    def send(self, src, dst, device):
        copy = pltpu.make_async_remote_copy(
            src_ref=src,
            dst_ref=dst,
            send_sem=self.send_sems.at[self.count],
            recv_sem=self.recv_sems.at[self.count],
            device_id=device,
            device_id_type=MESH_ID,
        )
        copy.start()
        self.count += 1
        self.sent.append(copy)
        return copy

    def settle(self, copies):
        for copy in copies:
            copy.wait_send()
        gone = {id(copy) for copy in copies}
        self.sent = [copy for copy in self.sent if id(copy) not in gone]

    def finish(self):
        self.settle(list(self.sent))


def each(dims, body):
    count = 1
    for dim in dims:
        count *= dim
    if count == 1:
        body((0,) * len(dims))
        return

    def turn(flat, _):
        index, rest = [], flat
        for dim in reversed(dims):
            index.insert(0, lax.rem(rest, dim))
            rest = lax.div(rest, dim)
        body(tuple(index))
        return 0

    lax.fori_loop(0, count, turn, 0)


class Reduction:
    def __init__(self, place, rows, wide, order, groups=True):
        self.place, self.rows, self.wide, self.order, self.groups = place, rows, wide, order, groups
        self.split = "g" in order
        axes = ["q", "p", "x"]
        self.part = wide
        if self.split:
            axes.insert(0, "g")
            self.part = wide // place.ng
        self.axes = axes
        lead = tuple(place.counts[axis] for axis in axes)
        self.boxes = [lead + (rows, self.part)]
        self.copies = place.ng if self.split else 1
        left = list(axes)
        for axis in order:
            left.remove(axis)
            others = place.counts[axis] - 1
            self.copies += others
            lead = tuple(place.counts[one] for one in left)
            self.boxes.append((max(others, 1),) + lead + (rows, self.part))
        if groups:
            self.boxes.append((place.ng, rows, self.part))
            self.copies += place.ng - 1

    def scratch(self):
        return [pltpu.VMEM(box, BF16) for box in self.boxes]

    def bind(self, mail, refs, src, first, out):
        place, part = self.place, self.part
        here = place.at
        pieces = place.ng if self.split else 1
        state = {}
        self.freed = False

        def start():
            far = place.others("c")[0]
            device = place.device("c", far)
            state["wait"] = []
            for i in range(pieces):
                view = src.at[:, :, :, far, :, pl.ds(first + i * part, part)]
                target = refs[0].at[i] if self.split else refs[0]
                state["wait"].append(mail.send(view, target, device))

        def send(level):
            axis = self.order[level]
            current, axes = state["current"], state["axes"]
            spot = axes.index(axis)
            state["spot"] = spot
            state["wait"] = [
                mail.send(
                    current.at[(slice(None),) * spot + (far,)],
                    refs[level + 1].at[i],
                    place.device(axis, far),
                )
                for i, far in enumerate(place.others(axis))
            ]

        def after_core():
            for copy in state["wait"]:
                copy.wait_recv()
            box = refs[0]

            def add(index):
                for i in range(pieces):
                    at = (i,) + index if self.split else index
                    mine = src[index + (here["c"], slice(None), pl.ds(first + i * part, part))]
                    box[at] = (mine.astype(F32) + box[at].astype(F32)).astype(BF16)

            each(place.lead[:3], add)
            mail.settle(state["wait"])
            self.freed = True
            state["current"], state["axes"] = box, list(self.axes)
            send(0)

        def after(level):
            def run():
                for copy in state["wait"]:
                    copy.wait_recv()
                axis, spot, current = self.order[level], state["spot"], state["current"]
                axes = [one for one in state["axes"] if one != axis]
                box = refs[level + 1]

                def total(index):
                    at = index[:spot] + (here[axis],) + index[spot:]
                    value = current[at].astype(F32)
                    for i in range(place.counts[axis] - 1):
                        value = value + box[(i,) + index].astype(F32)
                    return value

                if level + 1 < len(self.order):

                    def add(index):
                        box[(0,) + index] = total(index).astype(BF16)

                    each(tuple(place.counts[one] for one in axes), add)
                    state["current"], state["axes"] = box.at[0], axes
                    send(level + 1)
                    return
                value = total(())
                if not self.groups:
                    out(0, value)
                    return
                last = refs[-1]
                mine = here["g"]
                last[mine] = value.astype(BF16)
                state["wait"] = [
                    mail.send(last.at[mine], last.at[mine], place.device("g", far))
                    for far in place.others("g")
                ]

            return run

        def end():
            for copy in state["wait"]:
                copy.wait_recv()
            last = refs[-1]
            if self.split:
                for i in range(place.ng):
                    out(i * part, last[i].astype(F32))
                return
            value = last[0].astype(F32)
            for i in range(1, place.ng):
                value = value + last[i].astype(F32)
            out(0, value)

        self.stages = [start, after_core] + [after(level) for level in range(len(self.order))]
        if self.groups:
            self.stages.append(end)
        return self


class Total:
    axes = "cxpqg"

    def __init__(self, place, shape):
        self.place, self.shape = place, shape
        self.counts = [place.counts[axis] for axis in self.axes]
        self.copies = sum(count - 1 for count in self.counts)

    def scratch(self):
        return [
            pltpu.VMEM((count,) + self.shape, BF16 if level else F32)
            for level, count in enumerate(self.counts)
        ]

    def bind(self, mail, refs, src, out):
        pending = {}
        place = self.place

        def stage(level):
            def run():
                if level == 0:
                    value = src()
                else:
                    for copy in pending[level - 1]:
                        copy.wait_recv()
                    box = refs[level - 1]
                    value = box[0].astype(F32)
                    for i in range(1, self.counts[level - 1]):
                        value = value + box[i].astype(F32)
                if level == len(self.axes):
                    out(value)
                    return
                box, axis = refs[level], self.axes[level]
                here = place.at[axis]
                box[here] = value.astype(box.dtype)
                pending[level] = [
                    mail.send(box.at[here], box.at[here], place.device(axis, far))
                    for far in place.others(axis)
                ]

            return run

        self.stages = [stage(level) for level in range(len(self.axes) + 1)]
        return self

NT = (((1,), (1,)), ((), ()))
TN = (((0,), (0,)), ((), ()))
NEG_FILL = -1e30
QUAD = 4
WHOLE = pl.BlockSpec(memory_space=pltpu.VMEM)
FAR = pl.BlockSpec(memory_space=pl.ANY)
LIMIT = 63 * 2**20
CURVE = 0.7978845608028654
CUBE = 0.044715


def dot(a, b, dims=(((1,), (0,)), ((), ()))):
    return lax.dot_general(a, b, dims, preferred_element_type=F32)


class Porter:
    def __init__(self, sems, sources, places):
        self.sems, self.count, self.out = sems, 0, []
        self.coming = {}
        for source, place in zip(sources, places):
            copy = pltpu.make_async_copy(source, place, self.sems.at[self.count])
            copy.start()
            self.count += 1
            self.coming[id(place)] = copy

    def need(self, *places):
        for place in places:
            copy = self.coming.pop(id(place), None)
            if copy is not None:
                copy.wait()

    def ship(self, place, target):
        copy = pltpu.make_async_copy(place, target, self.sems.at[self.count])
        copy.start()
        self.count += 1
        self.out.append(copy)

    def finish(self):
        for copy in list(self.coming.values()) + self.out:
            copy.wait()


def like(arrays):
    return [pltpu.VMEM(array.shape, array.dtype) for array in arrays]


def row(ref):
    return ref[...].reshape(1, ref.shape[0])


def norm_parts(values):
    center = values - jnp.mean(values, axis=-1, keepdims=True)
    root = lax.rsqrt(jnp.mean(center * center, axis=-1, keepdims=True) + 1e-05)
    return center * root, root


def norm_back(grad, hat, root, gain):
    gx = grad * gain
    return root * (
        gx - jnp.mean(gx, axis=-1, keepdims=True) - hat * jnp.mean(gx * hat, axis=-1, keepdims=True)
    )


def hot_columns(index_row, count):
    rows = lax.broadcasted_iota(jnp.int32, (count, index_row.shape[1]), 0)
    return jnp.where(rows == index_row, 1.0, 0.0).astype(BF16)


def selected_row(sel_ref, seq):
    return jnp.concatenate([sel_ref[seq, b : b + 1, :] for b in range(sel_ref.shape[1])], axis=1)


def spread_heads(rows, size):
    lane_head = lax.broadcasted_iota(jnp.int32, rows.shape, 1) // size
    zero = jnp.zeros_like(rows)
    return jnp.concatenate([jnp.where(lane_head == h, rows, zero) for h in range(QUAD)], axis=0)


def merge_heads(wide, size):
    count = wide.shape[0] // QUAD
    lane_head = lax.broadcasted_iota(jnp.int32, (count, wide.shape[1]), 1) // size
    result = wide[:count]
    for h in range(1, QUAD):
        result = jnp.where(lane_head == h, wide[h * count : (h + 1) * count], result)
    return result


def window_bias(base, length):
    shape = (2 * WIN, QUAD * WIN)
    key = lax.broadcasted_iota(jnp.int32, shape, 0)
    query = lax.broadcasted_iota(jnp.int32, shape, 1) % WIN
    key_pos = key + (base - WIN)
    keep = (
        (key > query)
        & (key <= query + WIN)
        & (key_pos >= 0)
        & ((key_pos < length) | (key == query + WIN))
    )
    return jnp.where(keep, 0.0, NEG_FILL).astype(F32)


def keys_of(ext_ref, sel_ref, seq, start, rows_at, cols):
    return jnp.concatenate(
        [ext_ref[seq, pl.ds(start, 2 * WIN), cols], sel_ref[pl.ds(rows_at, WIN), cols]], axis=0
    )


def front(place, lengths, tokens, candidates, selected, norm_one, norm_two, biases, score_rows, weight_qkv, dy, weight_down, weight_out, weight_up):
    rows, width = tokens.shape
    seq_count, ranks, cands = candidates.shape
    tok = rows // seq_count
    blocks = tok // WIN
    every = ranks * cands
    heads = score_rows.shape[0]
    head_size = width // heads
    lanes = QUAD * head_size
    quads = width // lanes
    hidden_size = weight_up.shape[1]
    parts = hidden_size // width
    nz, nx, nc = place.nz, place.nx, place.nc
    copies = 1 + (nz - 1) + (nx - 1) * nz + nz * nx
    scale = head_size ** (-0.5)
    picks = blocks * WIN
    small = (tokens, candidates, selected, *norm_one, *norm_two, *biases, score_rows)
    large = (weight_qkv, dy, weight_down, weight_out, weight_up)
    shapes = [
        ((rows, width), BF16),
        ((rows, width), BF16),
        ((seq_count, tok + WIN, 2 * width), BF16),
        ((seq_count * WIN, width), BF16),
        ((seq_count * picks, width), BF16),
        ((seq_count * picks, 2 * width), BF16),
        ((seq_count * picks, 128), BF16),
        ((rows, width), BF16),
        ((seq_count * blocks, quads, 3 * WIN, QUAD * WIN), BF16),
        ((rows, width), BF16),
        ((rows, hidden_size), BF16),
        ((rows, hidden_size), BF16),
        ((rows, width), BF16),
        ((rows, width), BF16),
        ((rows, width), F32),
        ((rows, width), BF16),
        ((8 + parts, width), F32),
    ]

    def kernel(
        len_ref, tok_ref, cand_ref, pick_ref, gain_one, shift_one, gain_two, shift_two,
        bq_ref, bv_ref, bo_ref, bu_ref, bd_ref, ws_ref, *refs,
    ):
        far_in, refs = refs[: len(large)], refs[len(large) :]
        far_out, refs = refs[: len(shapes)], refs[len(shapes) :]
        near_in, refs = refs[: len(large)], refs[len(large) :]
        near_out, refs = refs[: len(shapes)], refs[len(shapes) :]
        bias_ref, gat, halo_out, halo_in, move_sems, send_sems, recv_sems = refs
        w_ref, dy_ref, wd_ref, wo_ref, wu_ref = near_in
        (
            normed_ref, q_ref, ext_ref, halo_ref, nsel_ref, ksel_ref, score_ref,
            att_ref, prob_ref, mixed_ref, hidden_ref, gpre_ref, n2_ref, branch_ref, gmid_ref, gatt_ref, vec_ref,
        ) = near_out
        porter = Porter(move_sems, far_in, near_in)

        def ship(ref):
            porter.ship(ref, far_out[[one is ref for one in near_out].index(True)])

        place.locate()
        mail = Mail(send_sems, recv_sems)
        z, x, c, g = (place.at[axis] for axis in "zxcg")
        rank = lax.axis_index("seq")
        after = (lax.rem(rank + 1, ranks), g)
        before = (lax.rem(rank + ranks - 1, ranks), g)
        barrier = pltpu.get_barrier_semaphore()
        greeted = [after, before]
        for axis in "czx":
            greeted += [place.device(axis, where) for where in place.others(axis)]
        for device in greeted:
            pl.semaphore_signal(barrier, inc=1, device_id=device, device_id_type=MESH_ID)
        gain_row, shift_row = row(gain_one), row(shift_one)

        def norm(values):
            return (norm_parts(values.astype(F32))[0] * gain_row + shift_row).astype(BF16)

        for seq in range(seq_count):
            hot = hot_columns(cand_ref[seq, pl.ds(rank, 1), :], tok)
            gat[seq, z, x, c] = norm(dot(hot, tok_ref[pl.ds(seq * tok, tok), :], TN))
            halo_out[seq] = norm(tok_ref[pl.ds((seq + 1) * tok - WIN, WIN), :])
        pl.semaphore_wait(barrier, len(greeted))

        def slot(zi, xi, ci):
            return gat.at[:, zi, xi, ci]

        by_z = [
            mail.send(slot(z, x, c), slot(z, x, c), place.device("z", far))
            for far in place.others("z")
        ]
        halo_copy = mail.send(halo_out, halo_in, after)
        core = place.device("c", place.others("c")[0])
        by_x, by_c = [], []

        def forward_x(zi):
            by_x.append(
                [
                    mail.send(slot(zi, x, c), slot(zi, x, c), place.device("x", far))
                    for far in place.others("x")
                ]
            )
            by_c.append(mail.send(slot(zi, x, c), slot(zi, x, c), core))

        def forward_c(zi, step):
            for i, copy in enumerate(by_x[step]):
                copy.wait_recv()
                come = lax.rem(x + nx - 1 - i, nx)
                by_c.append(mail.send(slot(zi, come, c), slot(zi, come, c), core))

        forward_x(z)
        for seq in range(seq_count):
            normed_ref[pl.ds(seq * tok, tok), :] = norm(tok_ref[pl.ds(seq * tok, tok), :])
        sources = [z] + [lax.rem(z + nz - 1 - i, nz) for i in range(nz - 1)]
        ship(normed_ref)
        porter.need(w_ref)
        queries = dot(normed_ref[...], w_ref[:, :width]) + row(bq_ref)
        q_ref[...] = (queries.astype(BF16).astype(F32) * scale).astype(BF16)
        ship(q_ref)
        value_bias = row(bv_ref)

        def project(values, half):
            part = dot(values, w_ref[:, pl.ds((1 + half) * width, width)])
            if half == 1:
                part = part + value_bias
            return part.astype(BF16)

        for half in range(2):
            cols = pl.ds(half * width, width)
            for seq in range(seq_count):
                ext_ref[seq, pl.ds(WIN, tok), cols] = project(
                    normed_ref[pl.ds(seq * tok, tok), :], half
                )
        halo_copy.wait_recv()
        for seq in range(seq_count):
            halo_ref[pl.ds(seq * WIN, WIN), :] = halo_in[seq]
        for half in range(2):
            part = project(halo_ref[...], half)
            for seq in range(seq_count):
                ext_ref[seq, pl.ds(0, WIN), pl.ds(half * width, width)] = part[
                    seq * WIN : (seq + 1) * WIN
                ]
        ship(halo_ref)
        ship(ext_ref)
        counted = []
        for seq in range(seq_count):
            index = selected_row(pick_ref, seq)
            inner = hot_columns(index % cands, cands)
            table = cand_ref[seq].astype(F32).astype(BF16)
            offset = dot(table, inner)
            block_of = lax.broadcasted_iota(jnp.int32, (ranks, picks), 0)
            chosen = jnp.where(block_of == index // cands, offset, 0.0)
            position = jnp.sum(chosen, axis=0, keepdims=True)
            position = position + ((index // cands) * tok).astype(F32)
            lane_block = lax.broadcasted_iota(jnp.int32, (1, picks), 1) // WIN
            limit = jnp.minimum((rank * blocks + lane_block) * WIN - WIN + 1, len_ref[seq])
            flag = jnp.where(position < limit.astype(F32), 1.0, 0.0)
            across = lax.broadcasted_iota(jnp.int32, (picks, picks), 0)
            down = lax.broadcasted_iota(jnp.int32, (picks, picks), 1)
            diagonal = jnp.where(across == down, flag, 0.0).astype(BF16)
            counted.append(dot(diagonal, jnp.ones((picks, width), BF16)))
        head_of = lax.broadcasted_iota(jnp.int32, (heads, width), 1) // head_size
        widen = jnp.where(head_of == lax.broadcasted_iota(jnp.int32, (heads, width), 0), 1.0, 0.0)
        score_ref[...] = jnp.zeros_like(score_ref)
        porter.need(dy_ref, wd_ref)
        for part in range(parts):
            cols = pl.ds(part * width, width)
            gpre_ref[:, cols] = dot(dy_ref[...], wd_ref[cols, :], NT).astype(BF16)
        for i in range(nz - 1):
            by_z[i].wait_recv()
            forward_x(sources[i + 1])
        forward_c(sources[0], 0)
        for i in range(1, nz):
            forward_c(sources[i], i)
        for copy in by_c:
            copy.wait_recv()
        for seq in range(seq_count):
            here = pl.ds(seq * picks, picks)
            hot = hot_columns(selected_row(pick_ref, seq), every)
            picked = dot(hot, gat[seq].reshape(every, width), TN).astype(BF16)
            nsel_ref[here, :] = picked
            for half in range(2):
                ksel_ref[here, pl.ds(half * width, width)] = project(picked, half)
            score = dot(picked, ws_ref[...], NT).astype(BF16)
            score_ref[here, pl.ds(0, heads)] = score
            wide = dot(score, widen.astype(BF16))
            gate = jnp.minimum(wide, 0.0) - jnp.log1p(jnp.exp(-jnp.abs(wide)))
            bias_ref[here, :] = jnp.where(counted[seq] > 0.5, gate, NEG_FILL)
        ship(nsel_ref)
        ship(ksel_ref)
        ship(score_ref)
        base = rank * tok

        def attend(i, _):
            seq, block = lax.div(i, blocks), lax.rem(i, blocks)
            at = pl.multiple_of(i * WIN, WIN)
            start = pl.multiple_of(block * WIN, WIN)
            mask = window_bias(base + block * WIN, len_ref[seq])
            for quad in range(quads):
                cols = pl.ds(quad * lanes, lanes)
                vals = pl.ds(width + quad * lanes, lanes)
                keys = keys_of(ext_ref, ksel_ref, seq, start, at, cols)
                values = keys_of(ext_ref, ksel_ref, seq, start, at, vals)
                wide = spread_heads(q_ref[pl.ds(at, WIN), cols], head_size)
                logits = dot(keys, wide, NT)
                logits = logits + jnp.concatenate([mask, bias_ref[pl.ds(at, WIN), cols]], axis=0)
                grown = jnp.exp(logits - jnp.max(logits, axis=0, keepdims=True))
                probs = (grown / jnp.sum(grown, axis=0, keepdims=True)).astype(BF16)
                prob_ref[i, quad] = probs
                att_ref[pl.ds(at, WIN), cols] = merge_heads(
                    dot(probs, values, TN), head_size
                ).astype(BF16)
            return 0

        lax.fori_loop(0, seq_count * blocks, attend, 0)
        ship(att_ref)
        ship(prob_ref)
        porter.need(wo_ref)
        gain_row = row(gain_two)
        middle = tok_ref[...].astype(F32) + dot(att_ref[...], wo_ref[...]) + row(bo_ref)
        gmid_ref[...] = middle
        hat, _ = norm_parts(middle)
        n2_ref[...] = (hat * gain_row + row(shift_two)).astype(BF16)
        ship(n2_ref)
        porter.need(wu_ref)
        bias_row = row(bu_ref)
        mixed = middle + row(bd_ref)
        grad_normed = jnp.zeros((rows, width), F32)
        for part in range(parts):
            cols = pl.ds(part * width, width)
            pre = dot(n2_ref[...], wu_ref[:, cols]) + bias_row[:, part * width : (part + 1) * width]
            square = pre * pre
            tanh = jnp.tanh(CURVE * pre * (1.0 + CUBE * square))
            half = 0.5 + 0.5 * tanh
            hidden_ref[:, cols] = (pre * half).astype(BF16)
            slope = half + 0.5 * pre * (1.0 - tanh * tanh) * (CURVE + 3 * CUBE * CURVE * square)
            gpre = (gpre_ref[:, cols].astype(F32) * slope).astype(BF16)
            gpre_ref[:, cols] = gpre
            vec_ref[pl.ds(8 + part, 1), :] = jnp.sum(gpre.astype(F32), axis=0, keepdims=True)
            mixed = mixed + dot(hidden_ref[:, cols], wd_ref[cols, :])
            grad_normed = grad_normed + dot(gpre, wu_ref[:, cols], NT)
        ship(hidden_ref)
        ship(gpre_ref)
        mixed_ref[...] = mixed.astype(BF16)
        ship(mixed_ref)
        hat, root = norm_parts(gmid_ref[...])
        dy_wide = dy_ref[...].astype(F32)
        vec_ref[0:4, :] = jnp.zeros((4, width), F32)
        vec_ref[5:6, :] = jnp.sum(grad_normed * hat, axis=0, keepdims=True)
        vec_ref[6:7, :] = jnp.sum(grad_normed, axis=0, keepdims=True)
        vec_ref[7:8, :] = jnp.sum(dy_wide, axis=0, keepdims=True)
        grad_middle = dy_wide + norm_back(grad_normed, hat, root, gain_row)
        gmid_ref[...] = grad_middle
        ship(gmid_ref)
        branch = grad_middle.astype(BF16)
        branch_ref[...] = branch
        ship(branch_ref)
        vec_ref[4:5, :] = jnp.sum(branch.astype(F32), axis=0, keepdims=True)
        ship(vec_ref)
        gatt_ref[...] = dot(branch, wo_ref[...], NT).astype(BF16)
        ship(gatt_ref)
        mail.finish()
        porter.finish()

    return pl.pallas_call(
        kernel,
        out_shape=[jax.ShapeDtypeStruct(*shape) for shape in shapes],
        in_specs=[pl.BlockSpec(memory_space=pltpu.SMEM)] + [WHOLE] * len(small) + [FAR] * len(large),
        out_specs=[FAR] * len(shapes),
        scratch_shapes=like(large)
        + [pltpu.VMEM(*shape) for shape in shapes]
        + [
            pltpu.VMEM((seq_count * picks, width), F32),
            pltpu.VMEM((seq_count, nz, nx, nc, cands, width), BF16),
            pltpu.VMEM((seq_count, WIN, width), BF16),
            pltpu.VMEM((seq_count, WIN, width), BF16),
            pltpu.SemaphoreType.DMA((len(large) + len(shapes),)),
            pltpu.SemaphoreType.DMA((copies,)),
            pltpu.SemaphoreType.DMA((copies,)),
        ],
        compiler_params=pltpu.CompilerParams(
            collective_id=2, has_side_effects=True, vmem_limit_bytes=LIMIT
        ),
    )(lengths, *small, *large)


SCHEDULE = (
    "cd2", "bd2", "cd0", "bd0", "cu2", "ad2", "bu2", "cu1", "ad0", "bu1", "cd1", "au2",
    "bd1", "cu3", "au1", "bu3", "cq0a", "au3", "ad1", "cq0b", "co", "ad2", "bo", "cfin0",
    "ao", "bq0", "cu0", "au2", "bu0", "cq1a", "au0", "aq0", "cq1b", "au1", "cfin1", "bq1",
    "cq2a", "au3", "au2", "aq1", "cq2b", "ad2", "ad0", "au1", "ao", "ad1", "cfin2", "au0",
    "au2", "aq0", "bq2", "cgive", "aq2", "ad2", "au3", "au1", "au2", "bs", "ao", "bb0",
    "bb1", "aq0", "bt", "at", "ab1", "ad1", "ab0", "au2", "ad2", "au1", "au3", "ao",
    "ad0", "aq2", "at", "au1", "ad2", "au0", "au3", "ab0", "aq0", "aq1", "ao", "ad0",
    "at", "au3", "ad1", "aq1", "aq0", "au0", "aq2", "as", "ad0", "ab0", "ab1", "at",
    "ad1", "aq0", "aq2", "au0", "ad0", "at", "aq1", "ad1", "ab0", "ab1", "au0", "aq2",
    "aq1", "aq2", "ab1", "aq1",
)
ORDERS = {
    "b0": "pxq",
    "b1": "xpq",
    "d0": "qxgp",
    "d1": "gqxp",
    "d2": "xqgp",
    "o": "xpq",
    "q0": "pgxq",
    "q1": "xgqp",
    "q2": "gpxq",
    "u0": "gxqp",
    "u1": "pxgq",
    "u2": "gxqp",
    "u3": "gxpq",
}

class Shift:
    copies = 1

    def __init__(self, shape):
        self.shape = shape

    def scratch(self):
        return [pltpu.VMEM(self.shape, BF16)]

    def bind(self, mail, refs, src, device, out):
        held = []

        def start():
            held.append(mail.send(src, refs[0], device))

        def finish():
            held[0].wait_recv()
            out(refs[0][...])

        self.stages = [start, finish]
        return self


def closing(place, gradients, attention, weight_qkv, score_rows, selected, gain, shift, tokens, vec, head_size):
    hidden, dy, gpre, n2, branch, attended = gradients
    queries, ext, ksel, probs, score, gatt, normed, halo, nsel = attention
    rows, width = dy.shape
    seq_count, ext_rows, _ = ext.shape
    tok = ext_rows - WIN
    blocks = tok // WIN
    steps = seq_count * blocks
    lanes = QUAD * head_size
    quads = width // lanes
    heads = score_rows.shape[0]
    hidden_size = hidden.shape[1]
    parts = hidden_size // width
    large = tuple(gradients) + tuple(attention) + (weight_qkv, tokens)
    ng = place.ng
    lead = place.lead
    ranks = place.nz * place.nx * place.nc
    share = width // ranks
    down_share = hidden_size // ranks
    down_wide = 256
    every_row = vec.shape[0] + heads
    picks = blocks * WIN
    cands = 32
    scale = head_size ** (-0.5)
    can_split = width % (128 * ng) == 0 and down_wide % (128 * ng) == 0
    def order(name):
        given = ORDERS[name]
        return given if can_split else given.replace("g", "")

    def reduction(name, piece_rows, wide, groups=True):
        return Reduction(place, piece_rows, wide, order(name), groups)

    downs = [reduction(f"d{i}", down_share, down_wide) for i in range(width // down_wide)]
    ups = [reduction(f"u{i}", share, width) for i in range(parts)]
    out_task = reduction("o", share, width)
    qkvs = [reduction(f"q{i}", share, width) for i in range(quads)]
    back_wide = width // 2
    backs = [reduction(f"b{i}", seq_count * cands, back_wide, False) for i in range(2)]
    total = Total(place, (every_row, width))
    shift_task = Shift((seq_count, WIN, width))
    tasks = downs + ups + [out_task] + qkvs + backs + [total, shift_task]
    boxes, counts = [], []
    for task in tasks:
        mine = task.scratch()
        boxes.extend(mine)
        counts.append(len(mine))
    copies = sum(task.copies for task in tasks)
    slots, down_slots = 3, 2
    work = [
        pltpu.VMEM((slots,) + lead + (share, width), BF16),
        pltpu.VMEM((down_slots,) + lead + (down_share, down_wide), BF16),
        pltpu.VMEM(lead + (seq_count * cands, width), BF16),
        pltpu.VMEM((seq_count, WIN, width), BF16),
        pltpu.VMEM((rows, lanes), BF16),
        pltpu.VMEM((seq_count, ext_rows, 2 * lanes), F32),
        pltpu.VMEM((seq_count * picks, 2 * lanes), BF16),
        pltpu.VMEM((seq_count * picks, 128), F32),
        pltpu.VMEM((seq_count * picks, width), F32),
        pltpu.VMEM((seq_count * WIN, width), F32),
        pltpu.VMEM((every_row, width), F32),
    ]

    def kernel(*refs):
        ws_ref, pick_ref, gain_ref, shift_ref, vec_ref = refs[:5]
        far = refs[5 : 5 + len(large)]
        refs = refs[5 + len(large) :]
        gqkv_ref, gout_ref, gup_ref, gdown_ref, total_ref, gn_ref, cand_ref, back_ref = refs[:8]
        near = refs[8 : 8 + len(large)]
        (
            hid_ref, dy_ref, gpre_ref, n2_ref, branch_ref, att_ref,
            q_ref, ext_ref, sel_ref, prob_ref, score_ref, gatt_ref, normed_ref, halo_ref, nsel_ref,
            w_ref, tok_ref,
        ) = near
        porter = Porter(refs[8 + len(large)], far, near)
        rest = list(refs[9 + len(large) :])
        recv_sems, send_sems = rest.pop(), rest.pop()
        stage, down_stage, back_src, halo_src, gq_ref, acc, gsel_ref, gates, gn_sel, gn_halo, own_vec = rest[-11:]
        room = rest[:-11]
        place.locate()
        mail = Mail(send_sems, recv_sems)
        rank, g = lax.axis_index("seq"), lax.axis_index("grp")
        after = (lax.rem(rank + 1, ranks), g)
        before = (lax.rem(rank + ranks - 1, ranks), g)
        barrier, answers = place.greet("cxpqg", [after, before])
        pl.semaphore_wait(barrier, answers)
        taken = {}
        for task, count in zip(tasks, counts):
            taken[id(task)] = room[:count]
            del room[:count]

        def column_writer(out, first):
            def write(offset, value):
                out[:, pl.ds(first + offset, value.shape[1])] = value

            return write

        def quad_writer(quad):
            def write(offset, value):
                wide = value.shape[1]
                low = offset
                while low < offset + wide:
                    kind = low // lanes
                    high = min(offset + wide, (kind + 1) * lanes)
                    at = kind * width + quad * lanes + low - kind * lanes
                    gqkv_ref[:, pl.ds(at, high - low)] = value[:, low - offset : high - offset]
                    low = high

            return write

        used = [0, 0]

        holders = [[None] * slots, [None] * down_slots]

        def bind(task, which, out):
            count = (slots, down_slots)[which]
            spot = used[which] % count
            used[which] += 1
            held = holders[which][spot]
            while held is not None and not held.freed:
                held.stages.pop(0)()
            holders[which][spot] = task
            src = (stage, down_stage)[which].at[spot]
            task.bind(mail, taken[id(task)], src, 0, out)
            return src

        def fill(src, left, right):
            value = dot(left, right, TN).astype(BF16)
            src[...] = value.reshape(src.shape)

        def down(i):
            porter.need(hid_ref, dy_ref)
            src = bind(downs[i], 1, column_writer(gdown_ref, i * down_wide))
            fill(src, hid_ref[...], dy_ref[:, i * down_wide : (i + 1) * down_wide])
            return downs[i]

        def up(i):
            porter.need(n2_ref, gpre_ref)
            src = bind(ups[i], 0, column_writer(gup_ref, i * width))
            fill(src, n2_ref[...], gpre_ref[:, i * width : (i + 1) * width])
            return ups[i]

        def out():
            porter.need(att_ref, branch_ref)
            src = bind(out_task, 0, column_writer(gout_ref, 0))
            fill(src, att_ref[...], branch_ref[...])
            return out_task

        def attend_back(quad, first, last):
            cols = pl.ds(quad * lanes, lanes)
            vals = pl.ds(width + quad * lanes, lanes)

            def step(i, _):
                seq, block = lax.div(i, blocks), lax.rem(i, blocks)
                at = pl.multiple_of(i * WIN, WIN)
                start = pl.multiple_of(block * WIN, WIN)
                keys = keys_of(ext_ref, sel_ref, seq, start, at, cols)
                values = keys_of(ext_ref, sel_ref, seq, start, at, vals)
                wide_q = spread_heads(q_ref[pl.ds(at, WIN), cols], head_size)
                wide_g = spread_heads(gatt_ref[pl.ds(at, WIN), cols], head_size)
                low_probs = prob_ref[i, quad]
                full = low_probs.astype(F32)
                weighed = full * dot(values, wide_g, NT)
                delta = jnp.sum(weighed, axis=0, keepdims=True)
                low = (weighed - full * delta).astype(BF16)
                grad_values = dot(low_probs, wide_g)
                grad_keys = dot(low, wide_q)
                gq = merge_heads(dot(low, keys, TN), head_size) * scale
                gq_ref[pl.ds(at, WIN), :] = gq.astype(BF16)
                acc[seq, pl.ds(start, 2 * WIN), :lanes] += grad_keys[: 2 * WIN]
                acc[seq, pl.ds(start, 2 * WIN), lanes:] += grad_values[: 2 * WIN]
                gsel_ref[pl.ds(at, WIN), :lanes] = grad_keys[2 * WIN :].astype(BF16)
                gsel_ref[pl.ds(at, WIN), lanes:] = grad_values[2 * WIN :].astype(BF16)
                head = lax.broadcasted_iota(jnp.int32, (lanes, 128), 0) // head_size + quad * QUAD
                pick = jnp.where(head == lax.broadcasted_iota(jnp.int32, (lanes, 128), 1), 1.0, 0.0)
                gates[pl.ds(at, WIN), :] += dot(low[2 * WIN :], pick.astype(BF16))
                return 0

            porter.need(q_ref, ext_ref, sel_ref, prob_ref, gatt_ref)
            if first == 0:
                acc[...] = jnp.zeros_like(acc)
            lax.fori_loop(first, last, step, 0)

        def finish_quad(quad):
            porter.need(normed_ref, halo_ref, nsel_ref, w_ref)
            src = bind(qkvs[quad], 0, quad_writer(quad))
            gq = gq_ref[...]
            gown = jnp.concatenate([acc[seq, WIN:, :] for seq in range(seq_count)], axis=0).astype(BF16)
            ghalo = jnp.concatenate([acc[seq, :WIN, :] for seq in range(seq_count)], axis=0).astype(BF16)
            gsel = gsel_ref[...]
            src[:, :, :, :, :, :lanes] = (
                dot(normed_ref[...], gq, TN).astype(BF16).reshape(lead + (share, lanes))
            )
            both = dot(normed_ref[...], gown, TN) + dot(halo_ref[...], ghalo, TN) + dot(nsel_ref[...], gsel, TN)
            src[:, :, :, :, :, lanes:] = both.astype(BF16).reshape(lead + (share, 2 * lanes))
            spots = [pl.ds(kind * width + quad * lanes, lanes) for kind in range(3)]
            own = dot(gq, w_ref[:, spots[0]], NT)
            own = own + dot(gown[:, :lanes], w_ref[:, spots[1]], NT)
            own = own + dot(gown[:, lanes:], w_ref[:, spots[2]], NT)
            near = dot(ghalo[:, :lanes], w_ref[:, spots[1]], NT) + dot(ghalo[:, lanes:], w_ref[:, spots[2]], NT)
            chosen = dot(gsel[:, :lanes], w_ref[:, spots[1]], NT) + dot(gsel[:, lanes:], w_ref[:, spots[2]], NT)
            if quad == 0:
                gn_ref[...], gn_halo[...], gn_sel[...] = own, near, chosen
            else:
                gn_ref[...] += own
                gn_halo[...] += near
                gn_sel[...] += chosen
            cols = pl.ds(quad * lanes, lanes)
            own_vec[0:1, cols] = jnp.sum(gq.astype(F32), axis=0, keepdims=True)
            own_vec[1:2, cols] = (
                jnp.sum(gown[:, lanes:].astype(F32), axis=0, keepdims=True)
                + jnp.sum(ghalo[:, lanes:].astype(F32), axis=0, keepdims=True)
                + jnp.sum(gsel[:, lanes:].astype(F32), axis=0, keepdims=True)
            )
            return qkvs[quad]

        def give_back():
            porter.need(score_ref, tok_ref)
            score_now = score_ref[...].astype(F32)
            gscore = (gates[...] / (1.0 + jnp.exp(score_now))).astype(BF16)
            chosen = gn_sel[...] + dot(gscore[:, :heads], ws_ref[...])
            low = chosen.astype(BF16)
            for seq in range(seq_count):
                hot = hot_columns(selected_row(pick_ref, seq), ranks * cands)
                terms = dot(hot, low[seq * picks : (seq + 1) * picks]).astype(BF16)
                back_src[:, :, :, :, pl.ds(seq * cands, cands), :] = terms.reshape(lead + (cands, width))
                halo_src[seq] = gn_halo[pl.ds(seq * WIN, WIN), :].astype(BF16)
            for i, task in enumerate(backs):
                task.bind(mail, taken[id(task)], back_src, i * back_wide, column_writer(cand_ref, i * back_wide))

            def halo_write(value):
                back_ref[...] = value

            shift_task.bind(mail, taken[id(shift_task)], halo_src, before, halo_write)
            gain_row, shift_row = row(gain_ref), row(shift_ref)
            hat, _ = norm_parts(tok_ref[...].astype(F32))

            def hat_of(ref):
                return (ref[...].astype(F32) - shift_row) / gain_row

            own, near = gn_ref[...], gn_halo[...]
            own_vec[2:3, :] = (
                jnp.sum(own * hat, axis=0, keepdims=True)
                + jnp.sum(near * hat_of(halo_ref), axis=0, keepdims=True)
                + jnp.sum(chosen * hat_of(nsel_ref), axis=0, keepdims=True)
            )
            own_vec[3:4, :] = (
                jnp.sum(own, axis=0, keepdims=True)
                + jnp.sum(near, axis=0, keepdims=True)
                + jnp.sum(chosen, axis=0, keepdims=True)
            )
            own_vec[4 : vec_ref.shape[0], :] = vec_ref[4:, :]
            own_vec[vec_ref.shape[0] :, :] = dot(gscore, nsel_ref[...], TN)[:heads]

            def vec_write(value):
                total_ref[...] = value

            total.bind(mail, taken[id(total)], lambda: own_vec[...], vec_write)
            return [shift_task] + backs + [total]

        gates[...] = jnp.zeros_like(gates)
        half = steps // 2
        begun = {"s": shift_task, "t": total, "o": out_task}
        work_of = {"o": out, "give": give_back}
        for i, task in enumerate(downs):
            begun[f"d{i}"], work_of[f"d{i}"] = task, lambda i=i: down(i)
        for i, task in enumerate(ups):
            begun[f"u{i}"], work_of[f"u{i}"] = task, lambda i=i: up(i)
        for i, task in enumerate(qkvs):
            begun[f"q{i}"], work_of[f"fin{i}"] = task, lambda i=i: finish_quad(i)
            work_of[f"q{i}a"] = lambda i=i: attend_back(i, 0, half)
            work_of[f"q{i}b"] = lambda i=i: attend_back(i, half, steps)
        for i, task in enumerate(backs):
            begun[f"b{i}"] = task
        for entry in SCHEDULE:
            what, name = entry[0], entry[1:]
            if what == "c":
                work_of[name]()
            elif begun[name].stages:
                begun[name].stages.pop(0)()
        for task in tasks:
            while task.stages:
                task.stages.pop(0)()
        mail.finish()
        porter.finish()

    shapes = [
        ((share, 3 * width), F32),
        ((share, width), F32),
        ((share, hidden_size), F32),
        ((down_share, width), F32),
        ((every_row, width), F32),
        ((rows, width), F32),
        ((seq_count * cands, width), F32),
        ((seq_count, WIN, width), BF16),
    ]
    return pl.pallas_call(
        kernel,
        out_shape=[jax.ShapeDtypeStruct(*shape) for shape in shapes],
        in_specs=[WHOLE] * 5 + [FAR] * len(large),
        out_specs=[WHOLE] * len(shapes),
        scratch_shapes=like(large)
        + [pltpu.SemaphoreType.DMA((len(large),))]
        + boxes
        + work
        + [pltpu.SemaphoreType.DMA((copies,)), pltpu.SemaphoreType.DMA((copies,))],
        compiler_params=pltpu.CompilerParams(
            collective_id=3, has_side_effects=True, vmem_limit_bytes=LIMIT
        ),
    )(score_rows, selected, gain, shift, vec, *large)


def ending(tokens, candidates, gain, grad_middle, gn, cand_back, halo_back, total, sums, parts, heads, ranks):
    rows, width = tokens.shape
    seq_count, _, cands = candidates.shape
    tok = rows // seq_count
    share = width // ranks
    up_share = parts * share
    vec_rows = total.shape[0]

    def kernel(
        tok_ref, cand_ref, gain_ref, gmid_ref, gn_ref, back_ref, halo_ref, total_ref, *refs
    ):
        grad_ref, small_ref, up_ref, score_ref = refs[len(sums) : len(sums) + 4]
        for came, result in zip(refs[: len(sums)], refs[len(sums) + 4 :]):
            result[...] = came[...]
        rank = lax.axis_index("seq")
        gain_row = row(gain_ref)
        for seq in range(seq_count):
            here = pl.ds(seq * tok, tok)
            hot = hot_columns(cand_ref[seq, pl.ds(rank, 1), :], tok)
            came = back_ref[pl.ds(seq * cands, cands), :].astype(BF16)
            grad = gn_ref[here, :] + dot(hot, came)
            near = halo_ref[seq].astype(F32)
            grad = grad + jnp.concatenate([jnp.zeros((tok - WIN, width), F32), near], axis=0)
            hat, root = norm_parts(tok_ref[here, :].astype(F32))
            grad_ref[here, :] = gmid_ref[here, :] + norm_back(grad, hat, root, gain_row)
        from_row = lax.broadcasted_iota(jnp.int32, (width, share), 0)
        to_col = lax.broadcasted_iota(jnp.int32, (width, share), 1)
        pick = jnp.where(from_row == to_col + rank * share, 1.0, 0.0)
        values = total_ref[...]
        small = lax.dot_general(
            values, pick, (((1,), (0,)), ((), ())),
            precision=lax.Precision.HIGHEST, preferred_element_type=F32,
        )
        small_ref[...] = small[:8]
        score_ref[...] = small[8 + parts :]
        per_row = width // up_share
        from_row = lax.broadcasted_iota(jnp.int32, (width, up_share), 0)
        to_col = lax.broadcasted_iota(jnp.int32, (width, up_share), 1)
        pick = jnp.where(from_row == to_col + lax.rem(rank, per_row) * up_share, 1.0, 0.0)
        ups = lax.dot_general(
            values[8 : 8 + parts], pick, (((1,), (0,)), ((), ())),
            precision=lax.Precision.HIGHEST, preferred_element_type=F32,
        )
        which = lax.broadcasted_iota(jnp.int32, ups.shape, 0)
        up_ref[...] = jnp.sum(
            jnp.where(which == lax.div(rank, per_row), ups, 0.0), axis=0, keepdims=True
        )

    return pl.pallas_call(
        kernel,
        out_shape=[
            jax.ShapeDtypeStruct((rows, width), F32),
            jax.ShapeDtypeStruct((8, share), F32),
            jax.ShapeDtypeStruct((1, up_share), F32),
            jax.ShapeDtypeStruct((heads, share), F32),
        ]
        + [jax.ShapeDtypeStruct(array.shape, array.dtype) for array in sums],
        in_specs=[WHOLE] * (8 + len(sums)),
        out_specs=[WHOLE] * (4 + len(sums)),
        compiler_params=pltpu.CompilerParams(vmem_limit_bytes=LIMIT),
    )(tokens, candidates, gain, grad_middle, gn, cand_back, halo_back, total, *sums)


def per_device(
    tokens,
    weight_qkv,
    bias_query,
    bias_value,
    weight_score,
    weight_out,
    bias_out,
    gain_one,
    shift_one,
    gain_two,
    shift_two,
    weight_up,
    bias_up,
    weight_down,
    bias_down,
    cotangent,
    lengths,
    candidates,
    selected,
):
    seq_count, tok, width = tokens.shape
    heads = weight_score.shape[1]
    head_size = width // heads
    rows = seq_count * tok
    ranks = lax.axis_size("seq")
    place = Place(ranks, lax.axis_size("grp"))
    parts = bias_up.shape[0] // width
    flat = tokens.reshape(rows, width)
    dy = cotangent.reshape(rows, width)
    (
        normed, queries, ext, halo, nsel, ksel, score,
        attended, probs, mixed, hidden, gpre, n2, branch, grad_middle, gatt, vec,
    ) = front(
        place, lengths, flat, candidates, selected, (gain_one, shift_one), (gain_two, shift_two),
        (bias_query, bias_value, bias_out, bias_up, bias_down), weight_score.T,
        weight_qkv, dy, weight_down, weight_out, weight_up,
    )
    grad_qkv, grad_out, grad_up, grad_down, total, gn, cand_back, halo_back = closing(
        place,
        (hidden, dy, gpre, n2, branch, attended),
        (queries, ext, ksel, probs, score, gatt, normed, halo, nsel),
        weight_qkv, weight_score.T, selected, gain_one, shift_one, flat, vec, head_size,
    )
    grad_tokens, small, up_row, score_rows, *sums = ending(
        flat, candidates, gain_one, grad_middle, gn, cand_back, halo_back, total,
        (grad_qkv, grad_out, grad_up, grad_down), parts, heads, ranks,
    )
    grad_qkv, grad_out, grad_up, grad_down = sums
    return (
        mixed.reshape(tokens.shape),
        grad_tokens.reshape(tokens.shape),
        grad_qkv,
        small[0],
        small[1],
        score_rows.T,
        grad_out,
        small[4],
        small[2],
        small[3],
        small[5],
        small[6],
        grad_up,
        up_row[0],
        grad_down,
        small[7],
    )


def solution(mesh):
    return jax.shard_map(
        per_device,
        mesh=mesh,
        in_specs=(
            P("grp", "seq", None),
            P(),
            P(),
            P(),
            P(),
            P(),
            P(),
            P(),
            P(),
            P(),
            P(),
            P(),
            P(),
            P(),
            P(),
            P("grp", "seq", None),
            P("grp"),
            P("grp", None, None),
            P("grp", "seq", None),
        ),
        out_specs=(
            P("grp", "seq", None),
            P("grp", "seq", None),
            P("seq", None),
            P("seq"),
            P("seq"),
            P("seq", None),
            P("seq", None),
            P("seq"),
            P("seq"),
            P("seq"),
            P("seq"),
            P("seq"),
            P("seq", None),
            P("seq"),
            P("seq", None),
            P("seq"),
        ),
        check_vma=False,
    )
```

```python
import jax
import jax.numpy as jnp
from jax import lax
from jax.experimental import pallas as pl
from jax.experimental.pallas import tpu as pltpu
from jax.sharding import PartitionSpec as P

WIN = 64
MESH_ID = pl.DeviceIdType.MESH
BF16 = jnp.bfloat16
F32 = jnp.float32


class Place:
    def __init__(self, seq_count, grp_count):
        self.nc = 2
        self.np = 2 if seq_count % 8 == 0 else 1
        self.nq = self.np
        self.nz = self.nq * self.np
        self.nx = seq_count // (self.nc * self.nz)
        self.ng = grp_count
        self.lead = (self.nq, self.np, self.nx, self.nc)
        self.counts = {
            "q": self.nq, "p": self.np, "z": self.nz, "x": self.nx, "c": self.nc, "g": self.ng,
        }

    def locate(self):
        rank = lax.axis_index("seq")
        z = lax.div(rank, self.nc * self.nx)
        self.at = {
            "c": lax.rem(rank, self.nc),
            "x": lax.rem(lax.div(rank, self.nc), self.nx),
            "z": z,
            "p": lax.rem(z, self.np),
            "q": lax.div(z, self.np),
            "g": lax.axis_index("grp"),
        }
        return self

    def device(self, axis, where):
        at = dict(self.at)
        at[axis] = where
        z = at["z"] if axis == "z" else at["q"] * self.np + at["p"]
        return ((z * self.nx + at["x"]) * self.nc + at["c"], at["g"])

    def others(self, axis):
        count = self.counts[axis]
        return [lax.rem(self.at[axis] + step, count) for step in range(1, count)]

    def greet(self, axes, more):
        barrier = pltpu.get_barrier_semaphore()
        devices = list(more)
        for axis in axes:
            devices += [self.device(axis, where) for where in self.others(axis)]
        for device in devices:
            pl.semaphore_signal(barrier, inc=1, device_id=device, device_id_type=MESH_ID)
        return barrier, len(devices)


class Mail:
    def __init__(self, send_sems, recv_sems):
        self.send_sems, self.recv_sems, self.count, self.sent = send_sems, recv_sems, 0, []

    def send(self, src, dst, device):
        copy = pltpu.make_async_remote_copy(
            src_ref=src,
            dst_ref=dst,
            send_sem=self.send_sems.at[self.count],
            recv_sem=self.recv_sems.at[self.count],
            device_id=device,
            device_id_type=MESH_ID,
        )
        copy.start()
        self.count += 1
        self.sent.append(copy)
        return copy

    def settle(self, copies):
        for copy in copies:
            copy.wait_send()
        gone = {id(copy) for copy in copies}
        self.sent = [copy for copy in self.sent if id(copy) not in gone]

    def finish(self):
        self.settle(list(self.sent))


def each(dims, body):
    count = 1
    for dim in dims:
        count *= dim
    if count == 1:
        body((0,) * len(dims))
        return

    def turn(flat, _):
        index, rest = [], flat
        for dim in reversed(dims):
            index.insert(0, lax.rem(rest, dim))
            rest = lax.div(rest, dim)
        body(tuple(index))
        return 0

    lax.fori_loop(0, count, turn, 0)


class Reduction:
    def __init__(self, place, rows, wide, order, groups=True):
        self.place, self.rows, self.wide, self.order, self.groups = place, rows, wide, order, groups
        self.split = "g" in order
        axes = ["q", "p", "x"]
        self.part = wide
        if self.split:
            axes.insert(0, "g")
            self.part = wide // place.ng
        self.axes = axes
        lead = tuple(place.counts[axis] for axis in axes)
        self.boxes = [lead + (rows, self.part)]
        self.copies = place.ng if self.split else 1
        left = list(axes)
        for axis in order:
            left.remove(axis)
            others = place.counts[axis] - 1
            self.copies += others
            lead = tuple(place.counts[one] for one in left)
            self.boxes.append((max(others, 1),) + lead + (rows, self.part))
        if groups:
            self.boxes.append((place.ng, rows, self.part))
            self.copies += place.ng - 1

    def scratch(self):
        return [pltpu.VMEM(box, BF16) for box in self.boxes]

    def bind(self, mail, refs, src, first, out):
        place, part = self.place, self.part
        here = place.at
        pieces = place.ng if self.split else 1
        state = {}
        self.freed = False

        def start():
            far = place.others("c")[0]
            device = place.device("c", far)
            state["wait"] = []
            for i in range(pieces):
                view = src.at[:, :, :, far, :, pl.ds(first + i * part, part)]
                target = refs[0].at[i] if self.split else refs[0]
                state["wait"].append(mail.send(view, target, device))

        def send(level):
            axis = self.order[level]
            current, axes = state["current"], state["axes"]
            spot = axes.index(axis)
            state["spot"] = spot
            state["wait"] = [
                mail.send(
                    current.at[(slice(None),) * spot + (far,)],
                    refs[level + 1].at[i],
                    place.device(axis, far),
                )
                for i, far in enumerate(place.others(axis))
            ]

        def after_core():
            for copy in state["wait"]:
                copy.wait_recv()
            box = refs[0]

            def add(index):
                for i in range(pieces):
                    at = (i,) + index if self.split else index
                    mine = src[index + (here["c"], slice(None), pl.ds(first + i * part, part))]
                    box[at] = (mine.astype(F32) + box[at].astype(F32)).astype(BF16)

            each(place.lead[:3], add)
            mail.settle(state["wait"])
            self.freed = True
            state["current"], state["axes"] = box, list(self.axes)
            send(0)

        def after(level):
            def run():
                for copy in state["wait"]:
                    copy.wait_recv()
                axis, spot, current = self.order[level], state["spot"], state["current"]
                axes = [one for one in state["axes"] if one != axis]
                box = refs[level + 1]

                def total(index):
                    at = index[:spot] + (here[axis],) + index[spot:]
                    value = current[at].astype(F32)
                    for i in range(place.counts[axis] - 1):
                        value = value + box[(i,) + index].astype(F32)
                    return value

                if level + 1 < len(self.order):

                    def add(index):
                        box[(0,) + index] = total(index).astype(BF16)

                    each(tuple(place.counts[one] for one in axes), add)
                    state["current"], state["axes"] = box.at[0], axes
                    send(level + 1)
                    return
                value = total(())
                if not self.groups:
                    out(0, value)
                    return
                last = refs[-1]
                mine = here["g"]
                last[mine] = value.astype(BF16)
                state["wait"] = [
                    mail.send(last.at[mine], last.at[mine], place.device("g", far))
                    for far in place.others("g")
                ]

            return run

        def end():
            for copy in state["wait"]:
                copy.wait_recv()
            last = refs[-1]
            if self.split:
                for i in range(place.ng):
                    out(i * part, last[i].astype(F32))
                return
            value = last[0].astype(F32)
            for i in range(1, place.ng):
                value = value + last[i].astype(F32)
            out(0, value)

        self.stages = [start, after_core] + [after(level) for level in range(len(self.order))]
        if self.groups:
            self.stages.append(end)
        return self


class Total:
    axes = "cxpqg"

    def __init__(self, place, shape):
        self.place, self.shape = place, shape
        self.counts = [place.counts[axis] for axis in self.axes]
        self.copies = sum(count - 1 for count in self.counts)

    def scratch(self):
        return [
            pltpu.VMEM((count,) + self.shape, BF16 if level else F32)
            for level, count in enumerate(self.counts)
        ]

    def bind(self, mail, refs, src, out):
        pending = {}
        place = self.place

        def stage(level):
            def run():
                if level == 0:
                    value = src()
                else:
                    for copy in pending[level - 1]:
                        copy.wait_recv()
                    box = refs[level - 1]
                    value = box[0].astype(F32)
                    for i in range(1, self.counts[level - 1]):
                        value = value + box[i].astype(F32)
                if level == len(self.axes):
                    out(value)
                    return
                box, axis = refs[level], self.axes[level]
                here = place.at[axis]
                box[here] = value.astype(box.dtype)
                pending[level] = [
                    mail.send(box.at[here], box.at[here], place.device(axis, far))
                    for far in place.others(axis)
                ]

            return run

        self.stages = [stage(level) for level in range(len(self.axes) + 1)]
        return self

NT = (((1,), (1,)), ((), ()))
TN = (((0,), (0,)), ((), ()))
NEG_FILL = -1e30
QUAD = 4
WHOLE = pl.BlockSpec(memory_space=pltpu.VMEM)
FAR = pl.BlockSpec(memory_space=pl.ANY)
LIMIT = 63 * 2**20
CURVE = 0.7978845608028654
CUBE = 0.044715


def dot(a, b, dims=(((1,), (0,)), ((), ()))):
    return lax.dot_general(a, b, dims, preferred_element_type=F32)


class Porter:
    def __init__(self, sems, sources, places):
        self.sems, self.count, self.out = sems, 0, []
        self.coming = {}
        for source, place in zip(sources, places):
            copy = pltpu.make_async_copy(source, place, self.sems.at[self.count])
            copy.start()
            self.count += 1
            self.coming[id(place)] = copy

    def need(self, *places):
        for place in places:
            copy = self.coming.pop(id(place), None)
            if copy is not None:
                copy.wait()

    def ship(self, place, target):
        copy = pltpu.make_async_copy(place, target, self.sems.at[self.count])
        copy.start()
        self.count += 1
        self.out.append(copy)

    def finish(self):
        for copy in list(self.coming.values()) + self.out:
            copy.wait()


def like(arrays):
    return [pltpu.VMEM(array.shape, array.dtype) for array in arrays]


def row(ref):
    return ref[...].reshape(1, ref.shape[0])


def norm_parts(values):
    center = values - jnp.mean(values, axis=-1, keepdims=True)
    root = lax.rsqrt(jnp.mean(center * center, axis=-1, keepdims=True) + 1e-05)
    return center * root, root


def norm_back(grad, hat, root, gain):
    gx = grad * gain
    return root * (
        gx - jnp.mean(gx, axis=-1, keepdims=True) - hat * jnp.mean(gx * hat, axis=-1, keepdims=True)
    )


def hot_columns(index_row, count):
    rows = lax.broadcasted_iota(jnp.int32, (count, index_row.shape[1]), 0)
    return jnp.where(rows == index_row, 1.0, 0.0).astype(BF16)


def selected_row(sel_ref, seq):
    return jnp.concatenate([sel_ref[seq, b : b + 1, :] for b in range(sel_ref.shape[1])], axis=1)


def spread_heads(rows, size):
    lane_head = lax.broadcasted_iota(jnp.int32, rows.shape, 1) // size
    zero = jnp.zeros_like(rows)
    return jnp.concatenate([jnp.where(lane_head == h, rows, zero) for h in range(QUAD)], axis=0)


def merge_heads(wide, size):
    count = wide.shape[0] // QUAD
    lane_head = lax.broadcasted_iota(jnp.int32, (count, wide.shape[1]), 1) // size
    result = wide[:count]
    for h in range(1, QUAD):
        result = jnp.where(lane_head == h, wide[h * count : (h + 1) * count], result)
    return result


def window_bias(base, length):
    shape = (2 * WIN, QUAD * WIN)
    key = lax.broadcasted_iota(jnp.int32, shape, 0)
    query = lax.broadcasted_iota(jnp.int32, shape, 1) % WIN
    key_pos = key + (base - WIN)
    keep = (
        (key > query)
        & (key <= query + WIN)
        & (key_pos >= 0)
        & ((key_pos < length) | (key == query + WIN))
    )
    return jnp.where(keep, 0.0, NEG_FILL).astype(F32)


def keys_of(ext_ref, sel_ref, seq, start, rows_at, cols):
    return jnp.concatenate(
        [ext_ref[seq, pl.ds(start, 2 * WIN), cols], sel_ref[pl.ds(rows_at, WIN), cols]], axis=0
    )


def front(place, lengths, tokens, candidates, selected, norm_one, norm_two, biases, score_rows, weight_qkv, dy, weight_down, weight_out, weight_up):
    rows, width = tokens.shape
    seq_count, ranks, cands = candidates.shape
    tok = rows // seq_count
    blocks = tok // WIN
    every = ranks * cands
    heads = score_rows.shape[0]
    head_size = width // heads
    lanes = QUAD * head_size
    quads = width // lanes
    hidden_size = weight_up.shape[1]
    parts = hidden_size // width
    nz, nx, nc = place.nz, place.nx, place.nc
    copies = 1 + (nz - 1) + (nx - 1) * nz + nz * nx
    scale = head_size ** (-0.5)
    picks = blocks * WIN
    small = (tokens, candidates, selected, *norm_one, *norm_two, *biases, score_rows)
    large = (weight_qkv, dy, weight_down, weight_out, weight_up)
    shapes = [
        ((rows, width), BF16),
        ((rows, width), BF16),
        ((seq_count, tok + WIN, 2 * width), BF16),
        ((seq_count * WIN, width), BF16),
        ((seq_count * picks, width), BF16),
        ((seq_count * picks, 2 * width), BF16),
        ((seq_count * picks, 128), BF16),
        ((rows, width), BF16),
        ((seq_count * blocks, quads, 3 * WIN, QUAD * WIN), BF16),
        ((rows, width), BF16),
        ((rows, hidden_size), BF16),
        ((rows, hidden_size), BF16),
        ((rows, width), BF16),
        ((rows, width), BF16),
        ((rows, width), F32),
        ((rows, width), BF16),
        ((8 + parts, width), F32),
    ]

    def kernel(
        len_ref, tok_ref, cand_ref, pick_ref, gain_one, shift_one, gain_two, shift_two,
        bq_ref, bv_ref, bo_ref, bu_ref, bd_ref, ws_ref, *refs,
    ):
        far_in, refs = refs[: len(large)], refs[len(large) :]
        far_out, refs = refs[: len(shapes)], refs[len(shapes) :]
        near_in, refs = refs[: len(large)], refs[len(large) :]
        near_out, refs = refs[: len(shapes)], refs[len(shapes) :]
        bias_ref, gat, halo_out, halo_in, move_sems, send_sems, recv_sems = refs
        w_ref, dy_ref, wd_ref, wo_ref, wu_ref = near_in
        (
            normed_ref, q_ref, ext_ref, halo_ref, nsel_ref, ksel_ref, score_ref,
            att_ref, prob_ref, mixed_ref, hidden_ref, gpre_ref, n2_ref, branch_ref, gmid_ref, gatt_ref, vec_ref,
        ) = near_out
        porter = Porter(move_sems, far_in, near_in)

        def ship(ref):
            porter.ship(ref, far_out[[one is ref for one in near_out].index(True)])

        place.locate()
        mail = Mail(send_sems, recv_sems)
        z, x, c, g = (place.at[axis] for axis in "zxcg")
        rank = lax.axis_index("seq")
        after = (lax.rem(rank + 1, ranks), g)
        before = (lax.rem(rank + ranks - 1, ranks), g)
        barrier = pltpu.get_barrier_semaphore()
        greeted = [after, before]
        for axis in "czx":
            greeted += [place.device(axis, where) for where in place.others(axis)]
        for device in greeted:
            pl.semaphore_signal(barrier, inc=1, device_id=device, device_id_type=MESH_ID)
        gain_row, shift_row = row(gain_one), row(shift_one)

        def norm(values):
            return (norm_parts(values.astype(F32))[0] * gain_row + shift_row).astype(BF16)

        for seq in range(seq_count):
            hot = hot_columns(cand_ref[seq, pl.ds(rank, 1), :], tok)
            gat[seq, z, x, c] = norm(dot(hot, tok_ref[pl.ds(seq * tok, tok), :], TN))
            halo_out[seq] = norm(tok_ref[pl.ds((seq + 1) * tok - WIN, WIN), :])
        pl.semaphore_wait(barrier, len(greeted))

        def slot(zi, xi, ci):
            return gat.at[:, zi, xi, ci]

        by_z = [
            mail.send(slot(z, x, c), slot(z, x, c), place.device("z", far))
            for far in place.others("z")
        ]
        halo_copy = mail.send(halo_out, halo_in, after)
        core = place.device("c", place.others("c")[0])
        by_x, by_c = [], []

        def forward_x(zi):
            by_x.append(
                [
                    mail.send(slot(zi, x, c), slot(zi, x, c), place.device("x", far))
                    for far in place.others("x")
                ]
            )
            by_c.append(mail.send(slot(zi, x, c), slot(zi, x, c), core))

        def forward_c(zi, step):
            for i, copy in enumerate(by_x[step]):
                copy.wait_recv()
                come = lax.rem(x + nx - 1 - i, nx)
                by_c.append(mail.send(slot(zi, come, c), slot(zi, come, c), core))

        forward_x(z)
        for seq in range(seq_count):
            normed_ref[pl.ds(seq * tok, tok), :] = norm(tok_ref[pl.ds(seq * tok, tok), :])
        sources = [z] + [lax.rem(z + nz - 1 - i, nz) for i in range(nz - 1)]
        ship(normed_ref)
        porter.need(w_ref)
        queries = dot(normed_ref[...], w_ref[:, :width]) + row(bq_ref)
        q_ref[...] = (queries.astype(BF16).astype(F32) * scale).astype(BF16)
        ship(q_ref)
        value_bias = row(bv_ref)

        def project(values, half):
            part = dot(values, w_ref[:, pl.ds((1 + half) * width, width)])
            if half == 1:
                part = part + value_bias
            return part.astype(BF16)

        for i in range(nz - 1):
            by_z[i].wait_recv()
            forward_x(sources[i + 1])
        forward_c(sources[0], 0)
        for half in range(2):
            cols = pl.ds(half * width, width)
            for seq in range(seq_count):
                ext_ref[seq, pl.ds(WIN, tok), cols] = project(
                    normed_ref[pl.ds(seq * tok, tok), :], half
                )
        halo_copy.wait_recv()
        for seq in range(seq_count):
            halo_ref[pl.ds(seq * WIN, WIN), :] = halo_in[seq]
        for half in range(2):
            part = project(halo_ref[...], half)
            for seq in range(seq_count):
                ext_ref[seq, pl.ds(0, WIN), pl.ds(half * width, width)] = part[
                    seq * WIN : (seq + 1) * WIN
                ]
        ship(halo_ref)
        ship(ext_ref)
        porter.need(dy_ref, wd_ref)
        for part in range(parts):
            cols = pl.ds(part * width, width)
            gpre_ref[:, cols] = dot(dy_ref[...], wd_ref[cols, :], NT).astype(BF16)
        for i in range(1, nz):
            forward_c(sources[i], i)
        counted = []
        for seq in range(seq_count):
            index = selected_row(pick_ref, seq)
            inner = hot_columns(index % cands, cands)
            table = cand_ref[seq].astype(F32).astype(BF16)
            offset = dot(table, inner)
            block_of = lax.broadcasted_iota(jnp.int32, (ranks, picks), 0)
            chosen = jnp.where(block_of == index // cands, offset, 0.0)
            position = jnp.sum(chosen, axis=0, keepdims=True)
            position = position + ((index // cands) * tok).astype(F32)
            lane_block = lax.broadcasted_iota(jnp.int32, (1, picks), 1) // WIN
            limit = jnp.minimum((rank * blocks + lane_block) * WIN - WIN + 1, len_ref[seq])
            flag = jnp.where(position < limit.astype(F32), 1.0, 0.0)
            across = lax.broadcasted_iota(jnp.int32, (picks, picks), 0)
            down = lax.broadcasted_iota(jnp.int32, (picks, picks), 1)
            diagonal = jnp.where(across == down, flag, 0.0).astype(BF16)
            counted.append(dot(diagonal, jnp.ones((picks, width), BF16)))
        head_of = lax.broadcasted_iota(jnp.int32, (heads, width), 1) // head_size
        widen = jnp.where(head_of == lax.broadcasted_iota(jnp.int32, (heads, width), 0), 1.0, 0.0)
        score_ref[...] = jnp.zeros_like(score_ref)
        for copy in by_c:
            copy.wait_recv()
        for seq in range(seq_count):
            here = pl.ds(seq * picks, picks)
            hot = hot_columns(selected_row(pick_ref, seq), every)
            picked = dot(hot, gat[seq].reshape(every, width), TN).astype(BF16)
            nsel_ref[here, :] = picked
            for half in range(2):
                ksel_ref[here, pl.ds(half * width, width)] = project(picked, half)
            score = dot(picked, ws_ref[...], NT).astype(BF16)
            score_ref[here, pl.ds(0, heads)] = score
            wide = dot(score, widen.astype(BF16))
            gate = jnp.minimum(wide, 0.0) - jnp.log1p(jnp.exp(-jnp.abs(wide)))
            bias_ref[here, :] = jnp.where(counted[seq] > 0.5, gate, NEG_FILL)
        ship(nsel_ref)
        ship(ksel_ref)
        ship(score_ref)
        base = rank * tok

        def attend(block, seq):
            i = seq * blocks + block
            at = pl.multiple_of(i * WIN, WIN)
            start = pl.multiple_of(block * WIN, WIN)
            mask = window_bias(base + block * WIN, len_ref[seq])
            for quad in range(quads):
                cols = pl.ds(quad * lanes, lanes)
                vals = pl.ds(width + quad * lanes, lanes)
                keys = keys_of(ext_ref, ksel_ref, seq, start, at, cols)
                values = keys_of(ext_ref, ksel_ref, seq, start, at, vals)
                wide = spread_heads(q_ref[pl.ds(at, WIN), cols], head_size)
                logits = dot(keys, wide, NT)
                logits = logits + jnp.concatenate([mask, bias_ref[pl.ds(at, WIN), cols]], axis=0)
                grown = jnp.exp(logits - jnp.max(logits, axis=0, keepdims=True))
                probs = (grown / jnp.sum(grown, axis=0, keepdims=True)).astype(BF16)
                prob_ref[i, quad] = probs
                att_ref[pl.ds(at, WIN), cols] = merge_heads(
                    dot(probs, values, TN), head_size
                ).astype(BF16)

        def attend_all(block, _):
            for seq in range(seq_count):
                attend(block, seq)
            return 0

        lax.fori_loop(0, blocks, attend_all, 0)
        ship(att_ref)
        ship(prob_ref)
        porter.need(wo_ref)
        gain_row = row(gain_two)
        middle = tok_ref[...].astype(F32) + dot(att_ref[...], wo_ref[...]) + row(bo_ref)
        gmid_ref[...] = middle
        hat, _ = norm_parts(middle)
        n2_ref[...] = (hat * gain_row + row(shift_two)).astype(BF16)
        ship(n2_ref)
        porter.need(wu_ref)
        bias_row = row(bu_ref)
        mixed = middle + row(bd_ref)
        grad_normed = jnp.zeros((rows, width), F32)
        for part in range(parts):
            cols = pl.ds(part * width, width)
            pre = dot(n2_ref[...], wu_ref[:, cols]) + bias_row[:, part * width : (part + 1) * width]
            square = pre * pre
            tanh = jnp.tanh(CURVE * pre * (1.0 + CUBE * square))
            half = 0.5 + 0.5 * tanh
            hidden_ref[:, cols] = (pre * half).astype(BF16)
            slope = half + 0.5 * pre * (1.0 - tanh * tanh) * (CURVE + 3 * CUBE * CURVE * square)
            gpre = (gpre_ref[:, cols].astype(F32) * slope).astype(BF16)
            gpre_ref[:, cols] = gpre
            vec_ref[pl.ds(8 + part, 1), :] = jnp.sum(gpre.astype(F32), axis=0, keepdims=True)
            mixed = mixed + dot(hidden_ref[:, cols], wd_ref[cols, :])
            grad_normed = grad_normed + dot(gpre, wu_ref[:, cols], NT)
        ship(hidden_ref)
        ship(gpre_ref)
        mixed_ref[...] = mixed.astype(BF16)
        ship(mixed_ref)
        hat, root = norm_parts(gmid_ref[...])
        dy_wide = dy_ref[...].astype(F32)
        vec_ref[0:4, :] = jnp.zeros((4, width), F32)
        vec_ref[5:6, :] = jnp.sum(grad_normed * hat, axis=0, keepdims=True)
        vec_ref[6:7, :] = jnp.sum(grad_normed, axis=0, keepdims=True)
        vec_ref[7:8, :] = jnp.sum(dy_wide, axis=0, keepdims=True)
        grad_middle = dy_wide + norm_back(grad_normed, hat, root, gain_row)
        gmid_ref[...] = grad_middle
        ship(gmid_ref)
        branch = grad_middle.astype(BF16)
        branch_ref[...] = branch
        ship(branch_ref)
        vec_ref[4:5, :] = jnp.sum(branch.astype(F32), axis=0, keepdims=True)
        ship(vec_ref)
        gatt_ref[...] = dot(branch, wo_ref[...], NT).astype(BF16)
        ship(gatt_ref)
        mail.finish()
        porter.finish()

    return pl.pallas_call(
        kernel,
        out_shape=[jax.ShapeDtypeStruct(*shape) for shape in shapes],
        in_specs=[pl.BlockSpec(memory_space=pltpu.SMEM)] + [WHOLE] * len(small) + [FAR] * len(large),
        out_specs=[FAR] * len(shapes),
        scratch_shapes=like(large)
        + [pltpu.VMEM(*shape) for shape in shapes]
        + [
            pltpu.VMEM((seq_count * picks, width), F32),
            pltpu.VMEM((seq_count, nz, nx, nc, cands, width), BF16),
            pltpu.VMEM((seq_count, WIN, width), BF16),
            pltpu.VMEM((seq_count, WIN, width), BF16),
            pltpu.SemaphoreType.DMA((len(large) + len(shapes),)),
            pltpu.SemaphoreType.DMA((copies,)),
            pltpu.SemaphoreType.DMA((copies,)),
        ],
        compiler_params=pltpu.CompilerParams(
            collective_id=2, has_side_effects=True, vmem_limit_bytes=LIMIT
        ),
    )(lengths, *small, *large)


SCHEDULE = (
    "cd2", "bd2", "cd0", "bd0", "cu2", "ad2", "bu2", "cu1", "ad0", "bu1", "cd1", "au2",
    "bd1", "cu3", "au1", "bu3", "cq0a", "au3", "ad1", "cq0b", "co", "ad2", "bo", "cfin0",
    "ao", "bq0", "cu0", "au2", "bu0", "cq1a", "au0", "aq0", "cq1b", "au1", "cfin1", "bq1",
    "cq2a", "au3", "au2", "aq1", "cq2b", "ad2", "ad0", "au1", "ao", "ad1", "cfin2", "au0",
    "au2", "aq0", "bq2", "cgive", "aq2", "ad2", "au3", "au1", "au2", "bs", "ao", "bb0",
    "bb1", "aq0", "bt", "at", "ab1", "ad1", "ab0", "au2", "ad2", "au1", "au3", "ao",
    "ad0", "aq2", "at", "au1", "ad2", "au0", "au3", "ab0", "aq0", "aq1", "ao", "ad0",
    "at", "au3", "ad1", "aq1", "aq0", "au0", "aq2", "as", "ad0", "ab0", "ab1", "at",
    "ad1", "aq0", "aq2", "au0", "ad0", "at", "aq1", "ad1", "ab0", "ab1", "au0", "aq2",
    "aq1", "aq2", "ab1", "aq1",
)
ORDERS = {
    "b0": "pxq",
    "b1": "xpq",
    "d0": "qxgp",
    "d1": "gqxp",
    "d2": "xqgp",
    "o": "xpq",
    "q0": "pgxq",
    "q1": "xgqp",
    "q2": "gpxq",
    "u0": "gxqp",
    "u1": "pxgq",
    "u2": "gxqp",
    "u3": "gxpq",
}

class Shift:
    copies = 1

    def __init__(self, shape):
        self.shape = shape

    def scratch(self):
        return [pltpu.VMEM(self.shape, BF16)]

    def bind(self, mail, refs, src, device, out):
        held = []

        def start():
            held.append(mail.send(src, refs[0], device))

        def finish():
            held[0].wait_recv()
            out(refs[0][...])

        self.stages = [start, finish]
        return self


def closing(place, gradients, attention, weight_qkv, score_rows, selected, gain, shift, tokens, vec, head_size):
    hidden, dy, gpre, n2, branch, attended = gradients
    queries, ext, ksel, probs, score, gatt, normed, halo, nsel = attention
    rows, width = dy.shape
    seq_count, ext_rows, _ = ext.shape
    tok = ext_rows - WIN
    blocks = tok // WIN
    steps = seq_count * blocks
    lanes = QUAD * head_size
    quads = width // lanes
    heads = score_rows.shape[0]
    hidden_size = hidden.shape[1]
    parts = hidden_size // width
    large = tuple(gradients) + tuple(attention) + (weight_qkv, tokens)
    ng = place.ng
    lead = place.lead
    ranks = place.nz * place.nx * place.nc
    share = width // ranks
    down_share = hidden_size // ranks
    down_wide = 256
    every_row = vec.shape[0] + heads
    picks = blocks * WIN
    cands = 32
    scale = head_size ** (-0.5)
    can_split = width % (128 * ng) == 0 and down_wide % (128 * ng) == 0
    def order(name):
        given = ORDERS[name]
        return given if can_split else given.replace("g", "")

    def reduction(name, piece_rows, wide, groups=True):
        return Reduction(place, piece_rows, wide, order(name), groups)

    downs = [reduction(f"d{i}", down_share, down_wide) for i in range(width // down_wide)]
    ups = [reduction(f"u{i}", share, width) for i in range(parts)]
    out_task = reduction("o", share, width)
    qkvs = [reduction(f"q{i}", share, width) for i in range(quads)]
    back_wide = width // 2
    backs = [reduction(f"b{i}", seq_count * cands, back_wide, False) for i in range(2)]
    total = Total(place, (every_row, width))
    shift_task = Shift((seq_count, WIN, width))
    tasks = downs + ups + [out_task] + qkvs + backs + [total, shift_task]
    boxes, counts = [], []
    for task in tasks:
        mine = task.scratch()
        boxes.extend(mine)
        counts.append(len(mine))
    copies = sum(task.copies for task in tasks)
    slots, down_slots = 3, 2
    work = [
        pltpu.VMEM((slots,) + lead + (share, width), BF16),
        pltpu.VMEM((down_slots,) + lead + (down_share, down_wide), BF16),
        pltpu.VMEM(lead + (seq_count * cands, width), BF16),
        pltpu.VMEM((seq_count, WIN, width), BF16),
        pltpu.VMEM((rows, lanes), BF16),
        pltpu.VMEM((seq_count, ext_rows, 2 * lanes), F32),
        pltpu.VMEM((seq_count * picks, 2 * lanes), BF16),
        pltpu.VMEM((seq_count * picks, 128), F32),
        pltpu.VMEM((seq_count * picks, width), F32),
        pltpu.VMEM((seq_count * WIN, width), F32),
        pltpu.VMEM((every_row, width), F32),
    ]

    def kernel(*refs):
        ws_ref, pick_ref, gain_ref, shift_ref, vec_ref = refs[:5]
        far = refs[5 : 5 + len(large)]
        refs = refs[5 + len(large) :]
        gqkv_ref, gout_ref, gup_ref, gdown_ref, total_ref, gn_ref, cand_ref, back_ref = refs[:8]
        near = refs[8 : 8 + len(large)]
        (
            hid_ref, dy_ref, gpre_ref, n2_ref, branch_ref, att_ref,
            q_ref, ext_ref, sel_ref, prob_ref, score_ref, gatt_ref, normed_ref, halo_ref, nsel_ref,
            w_ref, tok_ref,
        ) = near
        porter = Porter(refs[8 + len(large)], far, near)
        rest = list(refs[9 + len(large) :])
        recv_sems, send_sems = rest.pop(), rest.pop()
        stage, down_stage, back_src, halo_src, gq_ref, acc, gsel_ref, gates, gn_sel, gn_halo, own_vec = rest[-11:]
        room = rest[:-11]
        place.locate()
        mail = Mail(send_sems, recv_sems)
        rank, g = lax.axis_index("seq"), lax.axis_index("grp")
        after = (lax.rem(rank + 1, ranks), g)
        before = (lax.rem(rank + ranks - 1, ranks), g)
        barrier, answers = place.greet("cxpqg", [after, before])
        pl.semaphore_wait(barrier, answers)
        taken = {}
        for task, count in zip(tasks, counts):
            taken[id(task)] = room[:count]
            del room[:count]

        def column_writer(out, first):
            def write(offset, value):
                out[:, pl.ds(first + offset, value.shape[1])] = value

            return write

        def quad_writer(quad):
            def write(offset, value):
                wide = value.shape[1]
                low = offset
                while low < offset + wide:
                    kind = low // lanes
                    high = min(offset + wide, (kind + 1) * lanes)
                    at = kind * width + quad * lanes + low - kind * lanes
                    gqkv_ref[:, pl.ds(at, high - low)] = value[:, low - offset : high - offset]
                    low = high

            return write

        used = [0, 0]

        holders = [[None] * slots, [None] * down_slots]

        def bind(task, which, out):
            count = (slots, down_slots)[which]
            spot = used[which] % count
            used[which] += 1
            held = holders[which][spot]
            while held is not None and not held.freed:
                held.stages.pop(0)()
            holders[which][spot] = task
            src = (stage, down_stage)[which].at[spot]
            task.bind(mail, taken[id(task)], src, 0, out)
            return src

        def fill(src, left, right):
            value = dot(left, right, TN).astype(BF16)
            src[...] = value.reshape(src.shape)

        def down(i):
            porter.need(hid_ref, dy_ref)
            src = bind(downs[i], 1, column_writer(gdown_ref, i * down_wide))
            fill(src, hid_ref[...], dy_ref[:, i * down_wide : (i + 1) * down_wide])
            return downs[i]

        def up(i):
            porter.need(n2_ref, gpre_ref)
            src = bind(ups[i], 0, column_writer(gup_ref, i * width))
            fill(src, n2_ref[...], gpre_ref[:, i * width : (i + 1) * width])
            return ups[i]

        def out():
            porter.need(att_ref, branch_ref)
            src = bind(out_task, 0, column_writer(gout_ref, 0))
            fill(src, att_ref[...], branch_ref[...])
            return out_task

        def attend_back(quad, first, last):
            cols = pl.ds(quad * lanes, lanes)
            vals = pl.ds(width + quad * lanes, lanes)

            def step(seq, block):
                i = seq * blocks + block
                at, start = i * WIN, block * WIN
                keys = keys_of(ext_ref, sel_ref, seq, start, at, cols)
                values = keys_of(ext_ref, sel_ref, seq, start, at, vals)
                wide_q = spread_heads(q_ref[pl.ds(at, WIN), cols], head_size)
                wide_g = spread_heads(gatt_ref[pl.ds(at, WIN), cols], head_size)
                low_probs = prob_ref[i, quad]
                full = low_probs.astype(F32)
                weighed = full * dot(values, wide_g, NT)
                delta = jnp.sum(weighed, axis=0, keepdims=True)
                low = (weighed - full * delta).astype(BF16)
                grad_values = dot(low_probs, wide_g)
                grad_keys = dot(low, wide_q)
                gq = merge_heads(dot(low, keys, TN), head_size) * scale
                gq_ref[pl.ds(at, WIN), :] = gq.astype(BF16)
                acc[seq, pl.ds(start, 2 * WIN), :lanes] += grad_keys[: 2 * WIN]
                acc[seq, pl.ds(start, 2 * WIN), lanes:] += grad_values[: 2 * WIN]
                gsel_ref[pl.ds(at, WIN), :lanes] = grad_keys[2 * WIN :].astype(BF16)
                gsel_ref[pl.ds(at, WIN), lanes:] = grad_values[2 * WIN :].astype(BF16)
                head = lax.broadcasted_iota(jnp.int32, (lanes, 128), 0) // head_size + quad * QUAD
                pick = jnp.where(head == lax.broadcasted_iota(jnp.int32, (lanes, 128), 1), 1.0, 0.0)
                gates[pl.ds(at, WIN), :] += dot(low[2 * WIN :], pick.astype(BF16))

            porter.need(q_ref, ext_ref, sel_ref, prob_ref, gatt_ref)
            if first == 0:
                acc[...] = jnp.zeros_like(acc)
            for block in range(first, last):
                for seq in range(seq_count):
                    step(seq, block)

        def finish_quad(quad):
            porter.need(normed_ref, halo_ref, nsel_ref, w_ref)
            src = bind(qkvs[quad], 0, quad_writer(quad))
            gq = gq_ref[...]
            gown = jnp.concatenate([acc[seq, WIN:, :] for seq in range(seq_count)], axis=0).astype(BF16)
            ghalo = jnp.concatenate([acc[seq, :WIN, :] for seq in range(seq_count)], axis=0).astype(BF16)
            gsel = gsel_ref[...]
            src[:, :, :, :, :, :lanes] = (
                dot(normed_ref[...], gq, TN).astype(BF16).reshape(lead + (share, lanes))
            )
            both = dot(normed_ref[...], gown, TN) + dot(halo_ref[...], ghalo, TN) + dot(nsel_ref[...], gsel, TN)
            src[:, :, :, :, :, lanes:] = both.astype(BF16).reshape(lead + (share, 2 * lanes))
            spots = [pl.ds(kind * width + quad * lanes, lanes) for kind in range(3)]
            own = dot(gq, w_ref[:, spots[0]], NT)
            own = own + dot(gown[:, :lanes], w_ref[:, spots[1]], NT)
            own = own + dot(gown[:, lanes:], w_ref[:, spots[2]], NT)
            near = dot(ghalo[:, :lanes], w_ref[:, spots[1]], NT) + dot(ghalo[:, lanes:], w_ref[:, spots[2]], NT)
            chosen = dot(gsel[:, :lanes], w_ref[:, spots[1]], NT) + dot(gsel[:, lanes:], w_ref[:, spots[2]], NT)
            if quad == 0:
                gn_ref[...], gn_halo[...], gn_sel[...] = own, near, chosen
            else:
                gn_ref[...] += own
                gn_halo[...] += near
                gn_sel[...] += chosen
            cols = pl.ds(quad * lanes, lanes)
            own_vec[0:1, cols] = jnp.sum(gq.astype(F32), axis=0, keepdims=True)
            own_vec[1:2, cols] = (
                jnp.sum(gown[:, lanes:].astype(F32), axis=0, keepdims=True)
                + jnp.sum(ghalo[:, lanes:].astype(F32), axis=0, keepdims=True)
                + jnp.sum(gsel[:, lanes:].astype(F32), axis=0, keepdims=True)
            )
            return qkvs[quad]

        def give_back():
            porter.need(score_ref, tok_ref)
            score_now = score_ref[...].astype(F32)
            gscore = (gates[...] / (1.0 + jnp.exp(score_now))).astype(BF16)
            chosen = gn_sel[...] + dot(gscore[:, :heads], ws_ref[...])
            low = chosen.astype(BF16)
            for seq in range(seq_count):
                hot = hot_columns(selected_row(pick_ref, seq), ranks * cands)
                terms = dot(hot, low[seq * picks : (seq + 1) * picks]).astype(BF16)
                back_src[:, :, :, :, pl.ds(seq * cands, cands), :] = terms.reshape(lead + (cands, width))
                halo_src[seq] = gn_halo[pl.ds(seq * WIN, WIN), :].astype(BF16)
            for i, task in enumerate(backs):
                task.bind(mail, taken[id(task)], back_src, i * back_wide, column_writer(cand_ref, i * back_wide))

            def halo_write(value):
                back_ref[...] = value

            shift_task.bind(mail, taken[id(shift_task)], halo_src, before, halo_write)
            gain_row, shift_row = row(gain_ref), row(shift_ref)
            hat, _ = norm_parts(tok_ref[...].astype(F32))

            def hat_of(ref):
                return (ref[...].astype(F32) - shift_row) / gain_row

            own, near = gn_ref[...], gn_halo[...]
            own_vec[2:3, :] = (
                jnp.sum(own * hat, axis=0, keepdims=True)
                + jnp.sum(near * hat_of(halo_ref), axis=0, keepdims=True)
                + jnp.sum(chosen * hat_of(nsel_ref), axis=0, keepdims=True)
            )
            own_vec[3:4, :] = (
                jnp.sum(own, axis=0, keepdims=True)
                + jnp.sum(near, axis=0, keepdims=True)
                + jnp.sum(chosen, axis=0, keepdims=True)
            )
            own_vec[4 : vec_ref.shape[0], :] = vec_ref[4:, :]
            own_vec[vec_ref.shape[0] :, :] = dot(gscore, nsel_ref[...], TN)[:heads]

            def vec_write(value):
                total_ref[...] = value

            total.bind(mail, taken[id(total)], lambda: own_vec[...], vec_write)
            return [shift_task] + backs + [total]

        gates[...] = jnp.zeros_like(gates)
        half = blocks // 2
        begun = {"s": shift_task, "t": total, "o": out_task}
        work_of = {"o": out, "give": give_back}
        for i, task in enumerate(downs):
            begun[f"d{i}"], work_of[f"d{i}"] = task, lambda i=i: down(i)
        for i, task in enumerate(ups):
            begun[f"u{i}"], work_of[f"u{i}"] = task, lambda i=i: up(i)
        for i, task in enumerate(qkvs):
            begun[f"q{i}"], work_of[f"fin{i}"] = task, lambda i=i: finish_quad(i)
            work_of[f"q{i}a"] = lambda i=i: attend_back(i, 0, half)
            work_of[f"q{i}b"] = lambda i=i: attend_back(i, half, blocks)
        for i, task in enumerate(backs):
            begun[f"b{i}"] = task
        for entry in SCHEDULE:
            what, name = entry[0], entry[1:]
            if what == "c":
                work_of[name]()
            elif begun[name].stages:
                begun[name].stages.pop(0)()
        for task in tasks:
            while task.stages:
                task.stages.pop(0)()
        mail.finish()
        porter.finish()

    shapes = [
        ((share, 3 * width), F32),
        ((share, width), F32),
        ((share, hidden_size), F32),
        ((down_share, width), F32),
        ((every_row, width), F32),
        ((rows, width), F32),
        ((seq_count * cands, width), F32),
        ((seq_count, WIN, width), BF16),
    ]
    return pl.pallas_call(
        kernel,
        out_shape=[jax.ShapeDtypeStruct(*shape) for shape in shapes],
        in_specs=[WHOLE] * 5 + [FAR] * len(large),
        out_specs=[WHOLE] * len(shapes),
        scratch_shapes=like(large)
        + [pltpu.SemaphoreType.DMA((len(large),))]
        + boxes
        + work
        + [pltpu.SemaphoreType.DMA((copies,)), pltpu.SemaphoreType.DMA((copies,))],
        compiler_params=pltpu.CompilerParams(
            collective_id=3, has_side_effects=True, vmem_limit_bytes=LIMIT
        ),
    )(score_rows, selected, gain, shift, vec, *large)


def ending(tokens, candidates, gain, grad_middle, gn, cand_back, halo_back, total, sums, parts, heads, ranks):
    rows, width = tokens.shape
    seq_count, _, cands = candidates.shape
    tok = rows // seq_count
    share = width // ranks
    up_share = parts * share

    large = (gn, tokens, grad_middle, *sums)
    alone = 8

    def kernel(cand_ref, gain_ref, back_ref, halo_ref, total_ref, *refs):
        far_in, refs = refs[: len(large)], refs[len(large) :]
        small_refs, refs = refs[:alone], refs[alone:]
        up_ref, score_ref, grad_far = refs[:3]
        far_out, refs = refs[3 : 3 + len(sums)], refs[3 + len(sums) :]
        near, grad_ref, sems = refs[: len(large)], refs[-2], refs[-1]
        gn_ref, tok_ref, gmid_ref = near[:3]
        porter = Porter(sems, far_in, near)
        rank = lax.axis_index("seq")
        gain_row = row(gain_ref)
        values = total_ref[...]

        def pick(values, count, first):
            from_row = lax.broadcasted_iota(jnp.int32, (width, count), 0)
            to_col = lax.broadcasted_iota(jnp.int32, (width, count), 1)
            hot = jnp.where(from_row == to_col + first, 1.0, 0.0)
            return lax.dot_general(
                values, hot, (((1,), (0,)), ((), ())),
                precision=lax.Precision.HIGHEST, preferred_element_type=F32,
            )

        small = pick(values, share, rank * share)
        for i in range(alone):
            small_refs[i][...] = small[i]
        score_ref[...] = small[alone + parts :]
        per_row = width // up_share
        ups = pick(values[alone : alone + parts], up_share, lax.rem(rank, per_row) * up_share)
        which = lax.broadcasted_iota(jnp.int32, ups.shape, 0)
        up_ref[...] = jnp.sum(jnp.where(which == lax.div(rank, per_row), ups, 0.0), axis=0)
        porter.need(gn_ref, tok_ref, gmid_ref)
        for seq in range(seq_count):
            here = pl.ds(seq * tok, tok)
            hot = hot_columns(cand_ref[seq, pl.ds(rank, 1), :], tok)
            came = back_ref[pl.ds(seq * cands, cands), :].astype(BF16)
            grad = gn_ref[here, :] + dot(hot, came)
            near_rows = halo_ref[seq].astype(F32)
            grad = grad + jnp.concatenate([jnp.zeros((tok - WIN, width), F32), near_rows], axis=0)
            hat, root = norm_parts(tok_ref[here, :].astype(F32))
            grad_ref[here, :] = gmid_ref[here, :] + norm_back(grad, hat, root, gain_row)
            porter.ship(grad_ref.at[here, :], grad_far.at[here, :])
            if seq == 0:
                for came, result in zip(near[3:], far_out):
                    porter.need(came)
                    porter.ship(came, result)
        porter.finish()

    results = [jax.ShapeDtypeStruct((share,), F32)] * alone + [
        jax.ShapeDtypeStruct((up_share,), F32),
        jax.ShapeDtypeStruct((heads, share), F32),
        jax.ShapeDtypeStruct((rows, width), F32),
    ]
    return pl.pallas_call(
        kernel,
        out_shape=results + [jax.ShapeDtypeStruct(array.shape, array.dtype) for array in sums],
        in_specs=[WHOLE] * 5 + [FAR] * len(large),
        out_specs=[WHOLE] * (alone + 2) + [FAR] * (1 + len(sums)),
        scratch_shapes=like(large)
        + [
            pltpu.VMEM((rows, width), F32),
            pltpu.SemaphoreType.DMA((len(large) + seq_count + len(sums),)),
        ],
        compiler_params=pltpu.CompilerParams(vmem_limit_bytes=LIMIT),
    )(candidates, gain, cand_back, halo_back, total, *large)


def per_device(
    tokens,
    weight_qkv,
    bias_query,
    bias_value,
    weight_score,
    weight_out,
    bias_out,
    gain_one,
    shift_one,
    gain_two,
    shift_two,
    weight_up,
    bias_up,
    weight_down,
    bias_down,
    cotangent,
    lengths,
    candidates,
    selected,
):
    seq_count, tok, width = tokens.shape
    heads = weight_score.shape[1]
    head_size = width // heads
    rows = seq_count * tok
    ranks = lax.axis_size("seq")
    place = Place(ranks, lax.axis_size("grp"))
    parts = bias_up.shape[0] // width
    flat = tokens.reshape(rows, width)
    dy = cotangent.reshape(rows, width)
    (
        normed, queries, ext, halo, nsel, ksel, score,
        attended, probs, mixed, hidden, gpre, n2, branch, grad_middle, gatt, vec,
    ) = front(
        place, lengths, flat, candidates, selected, (gain_one, shift_one), (gain_two, shift_two),
        (bias_query, bias_value, bias_out, bias_up, bias_down), weight_score.T,
        weight_qkv, dy, weight_down, weight_out, weight_up,
    )
    grad_qkv, grad_out, grad_up, grad_down, total, gn, cand_back, halo_back = closing(
        place,
        (hidden, dy, gpre, n2, branch, attended),
        (queries, ext, ksel, probs, score, gatt, normed, halo, nsel),
        weight_qkv, weight_score.T, selected, gain_one, shift_one, flat, vec, head_size,
    )
    results = ending(
        flat, candidates, gain_one, grad_middle, gn, cand_back, halo_back, total,
        (grad_qkv, grad_out, grad_up, grad_down), parts, heads, ranks,
    )
    small, (up_row, score_rows, grad_tokens), sums = results[:8], results[8:11], results[11:]
    grad_qkv, grad_out, grad_up, grad_down = sums
    return (
        mixed.reshape(tokens.shape),
        grad_tokens.reshape(tokens.shape),
        grad_qkv,
        small[0],
        small[1],
        score_rows.T,
        grad_out,
        small[4],
        small[2],
        small[3],
        small[5],
        small[6],
        grad_up,
        up_row,
        grad_down,
        small[7],
    )


def solution(mesh):
    return jax.shard_map(
        per_device,
        mesh=mesh,
        in_specs=(
            P("grp", "seq", None),
            P(),
            P(),
            P(),
            P(),
            P(),
            P(),
            P(),
            P(),
            P(),
            P(),
            P(),
            P(),
            P(),
            P(),
            P("grp", "seq", None),
            P("grp"),
            P("grp", None, None),
            P("grp", "seq", None),
        ),
        out_specs=(
            P("grp", "seq", None),
            P("grp", "seq", None),
            P("seq", None),
            P("seq"),
            P("seq"),
            P("seq", None),
            P("seq", None),
            P("seq"),
            P("seq"),
            P("seq"),
            P("seq"),
            P("seq"),
            P("seq", None),
            P("seq"),
            P("seq", None),
            P("seq"),
        ),
        check_vma=False,
    )
```

```python
import jax
import jax.numpy as jnp
from jax import lax
from jax.experimental import pallas as pl
from jax.experimental.pallas import tpu as pltpu
from jax.sharding import PartitionSpec as P

WIN = 64
MESH_ID = pl.DeviceIdType.MESH
BF16 = jnp.bfloat16
F32 = jnp.float32


class Place:
    def __init__(self, seq_count, grp_count):
        self.nc = 2
        self.np = 2 if seq_count % 8 == 0 else 1
        self.nq = self.np
        self.nz = self.nq * self.np
        self.nx = seq_count // (self.nc * self.nz)
        self.ng = grp_count
        self.lead = (self.nq, self.np, self.nx, self.nc)
        self.counts = {
            "q": self.nq, "p": self.np, "z": self.nz, "x": self.nx, "c": self.nc, "g": self.ng,
        }

    def locate(self):
        rank = lax.axis_index("seq")
        z = lax.div(rank, self.nc * self.nx)
        self.at = {
            "c": lax.rem(rank, self.nc),
            "x": lax.rem(lax.div(rank, self.nc), self.nx),
            "z": z,
            "p": lax.rem(z, self.np),
            "q": lax.div(z, self.np),
            "g": lax.axis_index("grp"),
        }
        return self

    def device(self, axis, where):
        at = dict(self.at)
        at[axis] = where
        z = at["z"] if axis == "z" else at["q"] * self.np + at["p"]
        return ((z * self.nx + at["x"]) * self.nc + at["c"], at["g"])

    def others(self, axis):
        count = self.counts[axis]
        return [lax.rem(self.at[axis] + step, count) for step in range(1, count)]

    def greet(self, axes, more):
        barrier = pltpu.get_barrier_semaphore()
        devices = list(more)
        for axis in axes:
            devices += [self.device(axis, where) for where in self.others(axis)]
        for device in devices:
            pl.semaphore_signal(barrier, inc=1, device_id=device, device_id_type=MESH_ID)
        return barrier, len(devices)


class Mail:
    def __init__(self, send_sems, recv_sems):
        self.send_sems, self.recv_sems, self.count, self.sent = send_sems, recv_sems, 0, []

    def send(self, src, dst, device):
        copy = pltpu.make_async_remote_copy(
            src_ref=src,
            dst_ref=dst,
            send_sem=self.send_sems.at[self.count],
            recv_sem=self.recv_sems.at[self.count],
            device_id=device,
            device_id_type=MESH_ID,
        )
        copy.start()
        self.count += 1
        self.sent.append(copy)
        return copy

    def settle(self, copies):
        for copy in copies:
            copy.wait_send()
        gone = {id(copy) for copy in copies}
        self.sent = [copy for copy in self.sent if id(copy) not in gone]

    def finish(self):
        self.settle(list(self.sent))


def each(dims, body):
    count = 1
    for dim in dims:
        count *= dim
    if count == 1:
        body((0,) * len(dims))
        return

    def turn(flat, _):
        index, rest = [], flat
        for dim in reversed(dims):
            index.insert(0, lax.rem(rest, dim))
            rest = lax.div(rest, dim)
        body(tuple(index))
        return 0

    lax.fori_loop(0, count, turn, 0)


class Reduction:
    def __init__(self, place, rows, wide, order, groups=True):
        self.place, self.rows, self.wide, self.order, self.groups = place, rows, wide, order, groups
        self.split = "g" in order
        axes = ["q", "p", "x"]
        self.part = wide
        if self.split:
            axes.insert(0, "g")
            self.part = wide // place.ng
        self.axes = axes
        lead = tuple(place.counts[axis] for axis in axes)
        self.boxes = [lead + (rows, self.part)]
        self.copies = place.ng if self.split else 1
        left = list(axes)
        for axis in order:
            left.remove(axis)
            others = place.counts[axis] - 1
            self.copies += others
            lead = tuple(place.counts[one] for one in left)
            self.boxes.append((max(others, 1),) + lead + (rows, self.part))
        if groups:
            self.boxes.append((place.ng, rows, self.part))
            self.copies += place.ng - 1

    def scratch(self):
        return [pltpu.VMEM(box, BF16) for box in self.boxes]

    def bind(self, mail, refs, src, first, out):
        place, part = self.place, self.part
        here = place.at
        pieces = place.ng if self.split else 1
        state = {}
        self.freed = False

        def start():
            far = place.others("c")[0]
            device = place.device("c", far)
            state["wait"] = []
            for i in range(pieces):
                view = src.at[:, :, :, far, :, pl.ds(first + i * part, part)]
                target = refs[0].at[i] if self.split else refs[0]
                state["wait"].append(mail.send(view, target, device))

        def send(level):
            axis = self.order[level]
            current, axes = state["current"], state["axes"]
            spot = axes.index(axis)
            state["spot"] = spot
            state["wait"] = [
                mail.send(
                    current.at[(slice(None),) * spot + (far,)],
                    refs[level + 1].at[i],
                    place.device(axis, far),
                )
                for i, far in enumerate(place.others(axis))
            ]

        def after_core():
            for copy in state["wait"]:
                copy.wait_recv()
            box = refs[0]

            def add(index):
                for i in range(pieces):
                    at = (i,) + index if self.split else index
                    mine = src[index + (here["c"], slice(None), pl.ds(first + i * part, part))]
                    box[at] = (mine.astype(F32) + box[at].astype(F32)).astype(BF16)

            each(place.lead[:3], add)
            mail.settle(state["wait"])
            self.freed = True
            state["current"], state["axes"] = box, list(self.axes)
            send(0)

        def after(level):
            def run():
                for copy in state["wait"]:
                    copy.wait_recv()
                axis, spot, current = self.order[level], state["spot"], state["current"]
                axes = [one for one in state["axes"] if one != axis]
                box = refs[level + 1]

                def total(index):
                    at = index[:spot] + (here[axis],) + index[spot:]
                    value = current[at].astype(F32)
                    for i in range(place.counts[axis] - 1):
                        value = value + box[(i,) + index].astype(F32)
                    return value

                if level + 1 < len(self.order):

                    def add(index):
                        box[(0,) + index] = total(index).astype(BF16)

                    each(tuple(place.counts[one] for one in axes), add)
                    state["current"], state["axes"] = box.at[0], axes
                    send(level + 1)
                    return
                value = total(())
                if not self.groups:
                    out(0, value)
                    return
                last = refs[-1]
                mine = here["g"]
                last[mine] = value.astype(BF16)
                state["wait"] = [
                    mail.send(last.at[mine], last.at[mine], place.device("g", far))
                    for far in place.others("g")
                ]

            return run

        def end():
            for copy in state["wait"]:
                copy.wait_recv()
            last = refs[-1]
            if self.split:
                for i in range(place.ng):
                    out(i * part, last[i].astype(F32))
                return
            value = last[0].astype(F32)
            for i in range(1, place.ng):
                value = value + last[i].astype(F32)
            out(0, value)

        self.stages = [start, after_core] + [after(level) for level in range(len(self.order))]
        if self.groups:
            self.stages.append(end)
        return self


class Total:
    axes = "cxpqg"

    def __init__(self, place, shape):
        self.place, self.shape = place, shape
        self.counts = [place.counts[axis] for axis in self.axes]
        self.copies = sum(count - 1 for count in self.counts)

    def scratch(self):
        return [
            pltpu.VMEM((count,) + self.shape, BF16 if level else F32)
            for level, count in enumerate(self.counts)
        ]

    def bind(self, mail, refs, src, out):
        pending = {}
        place = self.place

        def stage(level):
            def run():
                if level == 0:
                    value = src()
                else:
                    for copy in pending[level - 1]:
                        copy.wait_recv()
                    box = refs[level - 1]
                    value = box[0].astype(F32)
                    for i in range(1, self.counts[level - 1]):
                        value = value + box[i].astype(F32)
                if level == len(self.axes):
                    out(value)
                    return
                box, axis = refs[level], self.axes[level]
                here = place.at[axis]
                box[here] = value.astype(box.dtype)
                pending[level] = [
                    mail.send(box.at[here], box.at[here], place.device(axis, far))
                    for far in place.others(axis)
                ]

            return run

        self.stages = [stage(level) for level in range(len(self.axes) + 1)]
        return self

NT = (((1,), (1,)), ((), ()))
TN = (((0,), (0,)), ((), ()))
NEG_FILL = -1e30
QUAD = 4
WHOLE = pl.BlockSpec(memory_space=pltpu.VMEM)
FAR = pl.BlockSpec(memory_space=pl.ANY)
LIMIT = 63 * 2**20
CURVE = 0.7978845608028654
CUBE = 0.044715


def dot(a, b, dims=(((1,), (0,)), ((), ()))):
    return lax.dot_general(a, b, dims, preferred_element_type=F32)


class Porter:
    def __init__(self, sems, sources, places):
        self.sems, self.count, self.out = sems, 0, []
        self.coming = {}
        for source, place in zip(sources, places):
            copy = pltpu.make_async_copy(source, place, self.sems.at[self.count])
            copy.start()
            self.count += 1
            self.coming[id(place)] = copy

    def need(self, *places):
        for place in places:
            copy = self.coming.pop(id(place), None)
            if copy is not None:
                copy.wait()

    def ship(self, place, target):
        copy = pltpu.make_async_copy(place, target, self.sems.at[self.count])
        copy.start()
        self.count += 1
        self.out.append(copy)

    def finish(self):
        for copy in list(self.coming.values()) + self.out:
            copy.wait()


def like(arrays):
    return [pltpu.VMEM(array.shape, array.dtype) for array in arrays]


def row(ref):
    return ref[...].reshape(1, ref.shape[0])


def norm_parts(values):
    center = values - jnp.mean(values, axis=-1, keepdims=True)
    root = lax.rsqrt(jnp.mean(center * center, axis=-1, keepdims=True) + 1e-05)
    return center * root, root


def norm_back(grad, hat, root, gain):
    gx = grad * gain
    return root * (
        gx - jnp.mean(gx, axis=-1, keepdims=True) - hat * jnp.mean(gx * hat, axis=-1, keepdims=True)
    )


def hot_columns(index_row, count):
    rows = lax.broadcasted_iota(jnp.int32, (count, index_row.shape[1]), 0)
    return jnp.where(rows == index_row, 1.0, 0.0).astype(BF16)


def selected_row(sel_ref, seq):
    return jnp.concatenate([sel_ref[seq, b : b + 1, :] for b in range(sel_ref.shape[1])], axis=1)


def spread_heads(rows, size):
    lane_head = lax.broadcasted_iota(jnp.int32, rows.shape, 1) // size
    zero = jnp.zeros_like(rows)
    return jnp.concatenate([jnp.where(lane_head == h, rows, zero) for h in range(QUAD)], axis=0)


def merge_heads(wide, size):
    count = wide.shape[0] // QUAD
    lane_head = lax.broadcasted_iota(jnp.int32, (count, wide.shape[1]), 1) // size
    result = wide[:count]
    for h in range(1, QUAD):
        result = jnp.where(lane_head == h, wide[h * count : (h + 1) * count], result)
    return result


def window_bias(base, length):
    shape = (2 * WIN, QUAD * WIN)
    key = lax.broadcasted_iota(jnp.int32, shape, 0)
    query = lax.broadcasted_iota(jnp.int32, shape, 1) % WIN
    key_pos = key + (base - WIN)
    keep = (
        (key > query)
        & (key <= query + WIN)
        & (key_pos >= 0)
        & ((key_pos < length) | (key == query + WIN))
    )
    return jnp.where(keep, 0.0, NEG_FILL).astype(F32)


def keys_of(ext_ref, sel_ref, seq, start, rows_at, cols):
    return jnp.concatenate(
        [ext_ref[seq, pl.ds(start, 2 * WIN), cols], sel_ref[pl.ds(rows_at, WIN), cols]], axis=0
    )


def front(place, lengths, tokens, candidates, selected, norm_one, norm_two, biases, score_rows, weight_qkv, dy, weight_down, weight_out, weight_up):
    rows, width = tokens.shape
    seq_count, ranks, cands = candidates.shape
    tok = rows // seq_count
    blocks = tok // WIN
    every = ranks * cands
    heads = score_rows.shape[0]
    head_size = width // heads
    lanes = QUAD * head_size
    quads = width // lanes
    hidden_size = weight_up.shape[1]
    parts = hidden_size // width
    nz, nx, nc = place.nz, place.nx, place.nc
    copies = 1 + (nz - 1) + (nx - 1) * nz + nz * nx
    scale = head_size ** (-0.5)
    picks = blocks * WIN
    small = (tokens, candidates, selected, *norm_one, *norm_two, *biases, score_rows)
    large = (weight_qkv, dy, weight_down, weight_out, weight_up)
    shapes = [
        ((rows, width), BF16),
        ((rows, width), BF16),
        ((seq_count, tok + WIN, 2 * width), BF16),
        ((seq_count * WIN, width), BF16),
        ((seq_count * picks, width), BF16),
        ((seq_count * picks, 2 * width), BF16),
        ((seq_count * picks, 128), BF16),
        ((rows, width), BF16),
        ((seq_count * blocks, quads, 3 * WIN, QUAD * WIN), BF16),
        ((rows, width), BF16),
        ((rows, hidden_size), BF16),
        ((rows, hidden_size), BF16),
        ((rows, width), BF16),
        ((rows, width), BF16),
        ((rows, width), F32),
        ((rows, width), BF16),
        ((8 + parts, width), F32),
    ]

    def kernel(
        len_ref, tok_ref, cand_ref, pick_ref, gain_one, shift_one, gain_two, shift_two,
        bq_ref, bv_ref, bo_ref, bu_ref, bd_ref, ws_ref, *refs,
    ):
        far_in, refs = refs[: len(large)], refs[len(large) :]
        far_out, refs = refs[: len(shapes)], refs[len(shapes) :]
        near_in, refs = refs[: len(large)], refs[len(large) :]
        near_out, refs = refs[: len(shapes)], refs[len(shapes) :]
        bias_ref, gat, halo_out, halo_in, move_sems, send_sems, recv_sems = refs
        w_ref, dy_ref, wd_ref, wo_ref, wu_ref = near_in
        (
            normed_ref, q_ref, ext_ref, halo_ref, nsel_ref, ksel_ref, score_ref,
            att_ref, prob_ref, mixed_ref, hidden_ref, gpre_ref, n2_ref, branch_ref, gmid_ref, gatt_ref, vec_ref,
        ) = near_out
        porter = Porter(move_sems, far_in, near_in)

        def ship(ref):
            porter.ship(ref, far_out[[one is ref for one in near_out].index(True)])

        place.locate()
        mail = Mail(send_sems, recv_sems)
        z, x, c, g = (place.at[axis] for axis in "zxcg")
        rank = lax.axis_index("seq")
        after = (lax.rem(rank + 1, ranks), g)
        before = (lax.rem(rank + ranks - 1, ranks), g)
        barrier = pltpu.get_barrier_semaphore()
        greeted = [after, before]
        for axis in "czx":
            greeted += [place.device(axis, where) for where in place.others(axis)]
        for device in greeted:
            pl.semaphore_signal(barrier, inc=1, device_id=device, device_id_type=MESH_ID)
        gain_row, shift_row = row(gain_one), row(shift_one)

        def norm(values):
            return (norm_parts(values.astype(F32))[0] * gain_row + shift_row).astype(BF16)

        for seq in range(seq_count):
            hot = hot_columns(cand_ref[seq, pl.ds(rank, 1), :], tok)
            gat[seq, z, x, c] = norm(dot(hot, tok_ref[pl.ds(seq * tok, tok), :], TN))
            halo_out[seq] = norm(tok_ref[pl.ds((seq + 1) * tok - WIN, WIN), :])
        pl.semaphore_wait(barrier, len(greeted))

        def slot(zi, xi, ci):
            return gat.at[:, zi, xi, ci]

        by_z = [
            mail.send(slot(z, x, c), slot(z, x, c), place.device("z", far))
            for far in place.others("z")
        ]
        halo_copy = mail.send(halo_out, halo_in, after)
        core = place.device("c", place.others("c")[0])
        by_x, by_c = [], []

        def forward_x(zi):
            by_x.append(
                [
                    mail.send(slot(zi, x, c), slot(zi, x, c), place.device("x", far))
                    for far in place.others("x")
                ]
            )
            by_c.append(mail.send(slot(zi, x, c), slot(zi, x, c), core))

        def forward_c(zi, step):
            for i, copy in enumerate(by_x[step]):
                copy.wait_recv()
                come = lax.rem(x + nx - 1 - i, nx)
                by_c.append(mail.send(slot(zi, come, c), slot(zi, come, c), core))

        forward_x(z)
        for seq in range(seq_count):
            normed_ref[pl.ds(seq * tok, tok), :] = norm(tok_ref[pl.ds(seq * tok, tok), :])
        sources = [z] + [lax.rem(z + nz - 1 - i, nz) for i in range(nz - 1)]
        ship(normed_ref)
        porter.need(w_ref)
        queries = dot(normed_ref[...], w_ref[:, :width]) + row(bq_ref)
        q_ref[...] = (queries.astype(BF16).astype(F32) * scale).astype(BF16)
        ship(q_ref)
        value_bias = row(bv_ref)

        def project(values, half):
            part = dot(values, w_ref[:, pl.ds((1 + half) * width, width)])
            if half == 1:
                part = part + value_bias
            return part.astype(BF16)

        for i in range(nz - 1):
            by_z[i].wait_recv()
            forward_x(sources[i + 1])
        forward_c(sources[0], 0)
        for half in range(2):
            cols = pl.ds(half * width, width)
            for seq in range(seq_count):
                ext_ref[seq, pl.ds(WIN, tok), cols] = project(
                    normed_ref[pl.ds(seq * tok, tok), :], half
                )
        halo_copy.wait_recv()
        for seq in range(seq_count):
            halo_ref[pl.ds(seq * WIN, WIN), :] = halo_in[seq]
        for half in range(2):
            part = project(halo_ref[...], half)
            for seq in range(seq_count):
                ext_ref[seq, pl.ds(0, WIN), pl.ds(half * width, width)] = part[
                    seq * WIN : (seq + 1) * WIN
                ]
        ship(halo_ref)
        ship(ext_ref)
        porter.need(dy_ref, wd_ref)
        for part in range(parts):
            cols = pl.ds(part * width, width)
            gpre_ref[:, cols] = dot(dy_ref[...], wd_ref[cols, :], NT).astype(BF16)
        for i in range(1, nz):
            forward_c(sources[i], i)
        counted = []
        for seq in range(seq_count):
            index = selected_row(pick_ref, seq)
            inner = hot_columns(index % cands, cands)
            table = cand_ref[seq].astype(F32).astype(BF16)
            offset = dot(table, inner)
            block_of = lax.broadcasted_iota(jnp.int32, (ranks, picks), 0)
            chosen = jnp.where(block_of == index // cands, offset, 0.0)
            position = jnp.sum(chosen, axis=0, keepdims=True)
            position = position + ((index // cands) * tok).astype(F32)
            lane_block = lax.broadcasted_iota(jnp.int32, (1, picks), 1) // WIN
            limit = jnp.minimum((rank * blocks + lane_block) * WIN - WIN + 1, len_ref[seq])
            flag = jnp.where(position < limit.astype(F32), 1.0, 0.0)
            across = lax.broadcasted_iota(jnp.int32, (picks, picks), 0)
            down = lax.broadcasted_iota(jnp.int32, (picks, picks), 1)
            diagonal = jnp.where(across == down, flag, 0.0).astype(BF16)
            counted.append(dot(diagonal, jnp.ones((picks, width), BF16)))
        head_of = lax.broadcasted_iota(jnp.int32, (heads, width), 1) // head_size
        widen = jnp.where(head_of == lax.broadcasted_iota(jnp.int32, (heads, width), 0), 1.0, 0.0)
        score_ref[...] = jnp.zeros_like(score_ref)
        for copy in by_c:
            copy.wait_recv()
        for seq in range(seq_count):
            here = pl.ds(seq * picks, picks)
            hot = hot_columns(selected_row(pick_ref, seq), every)
            picked = dot(hot, gat[seq].reshape(every, width), TN).astype(BF16)
            nsel_ref[here, :] = picked
            for half in range(2):
                ksel_ref[here, pl.ds(half * width, width)] = project(picked, half)
            score = dot(picked, ws_ref[...], NT).astype(BF16)
            score_ref[here, pl.ds(0, heads)] = score
            wide = dot(score, widen.astype(BF16))
            gate = jnp.minimum(wide, 0.0) - jnp.log1p(jnp.exp(-jnp.abs(wide)))
            bias_ref[here, :] = jnp.where(counted[seq] > 0.5, gate, NEG_FILL)
        ship(nsel_ref)
        ship(ksel_ref)
        ship(score_ref)
        base = rank * tok

        def attend(block, seq):
            i = seq * blocks + block
            at = pl.multiple_of(i * WIN, WIN)
            start = pl.multiple_of(block * WIN, WIN)
            mask = window_bias(base + block * WIN, len_ref[seq])
            for quad in range(quads):
                cols = pl.ds(quad * lanes, lanes)
                vals = pl.ds(width + quad * lanes, lanes)
                keys = keys_of(ext_ref, ksel_ref, seq, start, at, cols)
                values = keys_of(ext_ref, ksel_ref, seq, start, at, vals)
                wide = spread_heads(q_ref[pl.ds(at, WIN), cols], head_size)
                logits = dot(keys, wide, NT)
                logits = logits + jnp.concatenate([mask, bias_ref[pl.ds(at, WIN), cols]], axis=0)
                grown = jnp.exp(logits - jnp.max(logits, axis=0, keepdims=True))
                probs = (grown / jnp.sum(grown, axis=0, keepdims=True)).astype(BF16)
                prob_ref[i, quad] = probs
                att_ref[pl.ds(at, WIN), cols] = merge_heads(
                    dot(probs, values, TN), head_size
                ).astype(BF16)

        def attend_all(pair, _):
            for seq in range(seq_count):
                attend(pair, seq)
                attend(pair + blocks // 2, seq)
            return 0

        lax.fori_loop(0, blocks // 2, attend_all, 0)
        ship(att_ref)
        ship(prob_ref)
        porter.need(wo_ref)
        gain_row = row(gain_two)
        middle = tok_ref[...].astype(F32) + dot(att_ref[...], wo_ref[...]) + row(bo_ref)
        gmid_ref[...] = middle
        hat, _ = norm_parts(middle)
        n2_ref[...] = (hat * gain_row + row(shift_two)).astype(BF16)
        ship(n2_ref)
        porter.need(wu_ref)
        bias_row = row(bu_ref)
        mixed = middle + row(bd_ref)
        grad_normed = jnp.zeros((rows, width), F32)
        for part in range(parts):
            cols = pl.ds(part * width, width)
            pre = dot(n2_ref[...], wu_ref[:, cols]) + bias_row[:, part * width : (part + 1) * width]
            square = pre * pre
            tanh = jnp.tanh(CURVE * pre * (1.0 + CUBE * square))
            half = 0.5 + 0.5 * tanh
            hidden_ref[:, cols] = (pre * half).astype(BF16)
            slope = half + 0.5 * pre * (1.0 - tanh * tanh) * (CURVE + 3 * CUBE * CURVE * square)
            gpre = (gpre_ref[:, cols].astype(F32) * slope).astype(BF16)
            gpre_ref[:, cols] = gpre
            vec_ref[pl.ds(8 + part, 1), :] = jnp.sum(gpre.astype(F32), axis=0, keepdims=True)
            mixed = mixed + dot(hidden_ref[:, cols], wd_ref[cols, :])
            grad_normed = grad_normed + dot(gpre, wu_ref[:, cols], NT)
        ship(hidden_ref)
        ship(gpre_ref)
        mixed_ref[...] = mixed.astype(BF16)
        ship(mixed_ref)
        hat, root = norm_parts(gmid_ref[...])
        dy_wide = dy_ref[...].astype(F32)
        vec_ref[0:4, :] = jnp.zeros((4, width), F32)
        vec_ref[5:6, :] = jnp.sum(grad_normed * hat, axis=0, keepdims=True)
        vec_ref[6:7, :] = jnp.sum(grad_normed, axis=0, keepdims=True)
        vec_ref[7:8, :] = jnp.sum(dy_wide, axis=0, keepdims=True)
        grad_middle = dy_wide + norm_back(grad_normed, hat, root, gain_row)
        gmid_ref[...] = grad_middle
        ship(gmid_ref)
        branch = grad_middle.astype(BF16)
        branch_ref[...] = branch
        ship(branch_ref)
        vec_ref[4:5, :] = jnp.sum(branch.astype(F32), axis=0, keepdims=True)
        ship(vec_ref)
        gatt_ref[...] = dot(branch, wo_ref[...], NT).astype(BF16)
        ship(gatt_ref)
        mail.finish()
        porter.finish()

    return pl.pallas_call(
        kernel,
        out_shape=[jax.ShapeDtypeStruct(*shape) for shape in shapes],
        in_specs=[pl.BlockSpec(memory_space=pltpu.SMEM)] + [WHOLE] * len(small) + [FAR] * len(large),
        out_specs=[FAR] * len(shapes),
        scratch_shapes=like(large)
        + [pltpu.VMEM(*shape) for shape in shapes]
        + [
            pltpu.VMEM((seq_count * picks, width), F32),
            pltpu.VMEM((seq_count, nz, nx, nc, cands, width), BF16),
            pltpu.VMEM((seq_count, WIN, width), BF16),
            pltpu.VMEM((seq_count, WIN, width), BF16),
            pltpu.SemaphoreType.DMA((len(large) + len(shapes),)),
            pltpu.SemaphoreType.DMA((copies,)),
            pltpu.SemaphoreType.DMA((copies,)),
        ],
        compiler_params=pltpu.CompilerParams(
            collective_id=2, has_side_effects=True, vmem_limit_bytes=LIMIT
        ),
    )(lengths, *small, *large)


SCHEDULE = (
    "cd2", "bd2", "cd0", "bd0", "cu2", "ad2", "bu2", "cu1", "ad0", "bu1", "cd1", "au2",
    "bd1", "cu3", "au1", "bu3", "cq0a", "au3", "ad1", "cq0b", "co", "ad2", "bo", "cfin0",
    "ao", "bq0", "cu0", "au2", "bu0", "cq1a", "au0", "aq0", "cq1b", "au1", "cfin1", "bq1",
    "cq2a", "au3", "au2", "aq1", "cq2b", "ad2", "ad0", "au1", "ao", "ad1", "cfin2", "au0",
    "au2", "aq0", "bq2", "cgive", "aq2", "ad2", "au3", "au1", "au2", "bs", "ao", "bb0",
    "bb1", "aq0", "bt", "at", "ab1", "ad1", "ab0", "au2", "ad2", "au1", "au3", "ao",
    "ad0", "aq2", "at", "au1", "ad2", "au0", "au3", "ab0", "aq0", "aq1", "ao", "ad0",
    "at", "au3", "ad1", "aq1", "aq0", "au0", "aq2", "as", "ad0", "ab0", "ab1", "at",
    "ad1", "aq0", "aq2", "au0", "ad0", "at", "aq1", "ad1", "ab0", "ab1", "au0", "aq2",
    "aq1", "aq2", "ab1", "aq1",
)
ORDERS = {
    "b0": "pxq",
    "b1": "xpq",
    "d0": "qxgp",
    "d1": "gqxp",
    "d2": "xqgp",
    "o": "xpq",
    "q0": "pgxq",
    "q1": "xgqp",
    "q2": "gpxq",
    "u0": "gxqp",
    "u1": "pxgq",
    "u2": "gxqp",
    "u3": "gxpq",
}

class Shift:
    copies = 1

    def __init__(self, shape):
        self.shape = shape

    def scratch(self):
        return [pltpu.VMEM(self.shape, BF16)]

    def bind(self, mail, refs, src, device, out):
        held = []

        def start():
            held.append(mail.send(src, refs[0], device))

        def finish():
            held[0].wait_recv()
            out(refs[0][...])

        self.stages = [start, finish]
        return self


def closing(place, gradients, attention, weight_qkv, score_rows, selected, gain, shift, tokens, grad_middle, vec, head_size):
    hidden, dy, gpre, n2, branch, attended = gradients
    queries, ext, ksel, probs, score, gatt, normed, halo, nsel = attention
    rows, width = dy.shape
    seq_count, ext_rows, _ = ext.shape
    tok = ext_rows - WIN
    blocks = tok // WIN
    steps = seq_count * blocks
    lanes = QUAD * head_size
    quads = width // lanes
    heads = score_rows.shape[0]
    hidden_size = hidden.shape[1]
    parts = hidden_size // width
    large = tuple(gradients) + tuple(attention) + (weight_qkv, tokens, grad_middle)
    ng = place.ng
    lead = place.lead
    ranks = place.nz * place.nx * place.nc
    share = width // ranks
    down_share = hidden_size // ranks
    down_wide = 256
    every_row = vec.shape[0] + heads
    picks = blocks * WIN
    cands = 32
    scale = head_size ** (-0.5)
    can_split = width % (128 * ng) == 0 and down_wide % (128 * ng) == 0
    def order(name):
        given = ORDERS[name]
        return given if can_split else given.replace("g", "")

    def reduction(name, piece_rows, wide, groups=True):
        return Reduction(place, piece_rows, wide, order(name), groups)

    downs = [reduction(f"d{i}", down_share, down_wide) for i in range(width // down_wide)]
    ups = [reduction(f"u{i}", share, width) for i in range(parts)]
    out_task = reduction("o", share, width)
    qkvs = [reduction(f"q{i}", share, width) for i in range(quads)]
    back_wide = width // 2
    backs = [reduction(f"b{i}", seq_count * cands, back_wide, False) for i in range(2)]
    total = Total(place, (every_row, width))
    shift_task = Shift((seq_count, WIN, width))
    tasks = downs + ups + [out_task] + qkvs + backs + [total, shift_task]
    boxes, counts = [], []
    for task in tasks:
        mine = task.scratch()
        boxes.extend(mine)
        counts.append(len(mine))
    copies = sum(task.copies for task in tasks)
    slots, down_slots = (3, 2) if can_split else (2, 1)
    work = [
        pltpu.VMEM((slots,) + lead + (share, width), BF16),
        pltpu.VMEM((down_slots,) + lead + (down_share, down_wide), BF16),
        pltpu.VMEM(lead + (seq_count * cands, width), BF16),
        pltpu.VMEM((seq_count, WIN, width), BF16),
        pltpu.VMEM((rows, lanes), BF16),
        pltpu.VMEM((seq_count, ext_rows, 2 * lanes), F32),
        pltpu.VMEM((seq_count * picks, 2 * lanes), BF16),
        pltpu.VMEM((seq_count * picks, 128), F32),
        pltpu.VMEM((seq_count * picks, width), F32),
        pltpu.VMEM((seq_count * WIN, width), F32),
        pltpu.VMEM((every_row, width), F32),
        pltpu.VMEM((rows, width), F32),
    ]

    def kernel(*refs):
        ws_ref, pick_ref, gain_ref, shift_ref, vec_ref = refs[:5]
        far = refs[5 : 5 + len(large)]
        refs = refs[5 + len(large) :]
        gqkv_ref, gout_ref, gup_ref, gdown_ref, total_ref, gn_far, cand_ref, back_ref = refs[:8]
        near = refs[8 : 8 + len(large)]
        (
            hid_ref, dy_ref, gpre_ref, n2_ref, branch_ref, att_ref,
            q_ref, ext_ref, sel_ref, prob_ref, score_ref, gatt_ref, normed_ref, halo_ref, nsel_ref,
            w_ref, tok_ref, gmid_ref,
        ) = near
        porter = Porter(refs[8 + len(large)], far, near)
        rest = list(refs[9 + len(large) :])
        recv_sems, send_sems = rest.pop(), rest.pop()
        stage, down_stage, back_src, halo_src, gq_ref, acc, gsel_ref, gates, gn_sel, gn_halo, own_vec, gn_ref = rest[-12:]
        room = rest[:-12]
        place.locate()
        mail = Mail(send_sems, recv_sems)
        rank, g = lax.axis_index("seq"), lax.axis_index("grp")
        after = (lax.rem(rank + 1, ranks), g)
        before = (lax.rem(rank + ranks - 1, ranks), g)
        barrier, answers = place.greet("cxpqg", [after, before])
        pl.semaphore_wait(barrier, answers)
        taken = {}
        for task, count in zip(tasks, counts):
            taken[id(task)] = room[:count]
            del room[:count]

        def column_writer(out, first):
            def write(offset, value):
                out[:, pl.ds(first + offset, value.shape[1])] = value

            return write

        def quad_writer(quad):
            def write(offset, value):
                wide = value.shape[1]
                low = offset
                while low < offset + wide:
                    kind = low // lanes
                    high = min(offset + wide, (kind + 1) * lanes)
                    at = kind * width + quad * lanes + low - kind * lanes
                    gqkv_ref[:, pl.ds(at, high - low)] = value[:, low - offset : high - offset]
                    low = high

            return write

        used = [0, 0]

        holders = [[None] * slots, [None] * down_slots]

        def bind(task, which, out):
            count = (slots, down_slots)[which]
            spot = used[which] % count
            used[which] += 1
            held = holders[which][spot]
            while held is not None and not held.freed:
                held.stages.pop(0)()
            holders[which][spot] = task
            src = (stage, down_stage)[which].at[spot]
            task.bind(mail, taken[id(task)], src, 0, out)
            return src

        def fill(src, left, right):
            value = dot(left, right, TN).astype(BF16)
            src[...] = value.reshape(src.shape)

        def down(i):
            porter.need(hid_ref, dy_ref)
            src = bind(downs[i], 1, column_writer(gdown_ref, i * down_wide))
            fill(src, hid_ref[...], dy_ref[:, i * down_wide : (i + 1) * down_wide])
            return downs[i]

        def up(i):
            porter.need(n2_ref, gpre_ref)
            src = bind(ups[i], 0, column_writer(gup_ref, i * width))
            fill(src, n2_ref[...], gpre_ref[:, i * width : (i + 1) * width])
            return ups[i]

        def out():
            porter.need(att_ref, branch_ref)
            src = bind(out_task, 0, column_writer(gout_ref, 0))
            fill(src, att_ref[...], branch_ref[...])
            return out_task

        def attend_back(quad, first, last):
            cols = pl.ds(quad * lanes, lanes)
            vals = pl.ds(width + quad * lanes, lanes)

            def step(seq, block):
                i = seq * blocks + block
                at, start = i * WIN, block * WIN
                keys = keys_of(ext_ref, sel_ref, seq, start, at, cols)
                values = keys_of(ext_ref, sel_ref, seq, start, at, vals)
                wide_q = spread_heads(q_ref[pl.ds(at, WIN), cols], head_size)
                wide_g = spread_heads(gatt_ref[pl.ds(at, WIN), cols], head_size)
                low_probs = prob_ref[i, quad]
                full = low_probs.astype(F32)
                weighed = full * dot(values, wide_g, NT)
                delta = jnp.sum(weighed, axis=0, keepdims=True)
                low = (weighed - full * delta).astype(BF16)
                grad_values = dot(low_probs, wide_g)
                grad_keys = dot(low, wide_q)
                gq = merge_heads(dot(low, keys, TN), head_size) * scale
                gq_ref[pl.ds(at, WIN), :] = gq.astype(BF16)
                acc[seq, pl.ds(start, 2 * WIN), :lanes] += grad_keys[: 2 * WIN]
                acc[seq, pl.ds(start, 2 * WIN), lanes:] += grad_values[: 2 * WIN]
                gsel_ref[pl.ds(at, WIN), :lanes] = grad_keys[2 * WIN :].astype(BF16)
                gsel_ref[pl.ds(at, WIN), lanes:] = grad_values[2 * WIN :].astype(BF16)
                head = lax.broadcasted_iota(jnp.int32, (lanes, 128), 0) // head_size + quad * QUAD
                pick = jnp.where(head == lax.broadcasted_iota(jnp.int32, (lanes, 128), 1), 1.0, 0.0)
                gates[pl.ds(at, WIN), :] += dot(low[2 * WIN :], pick.astype(BF16))

            porter.need(q_ref, ext_ref, sel_ref, prob_ref, gatt_ref)
            if first == 0:
                acc[...] = jnp.zeros_like(acc)
            for block in range(first, last):
                for seq in range(seq_count):
                    step(seq, block)

        def finish_quad(quad):
            porter.need(normed_ref, halo_ref, nsel_ref, w_ref)
            src = bind(qkvs[quad], 0, quad_writer(quad))
            gq = gq_ref[...]
            gown = jnp.concatenate([acc[seq, WIN:, :] for seq in range(seq_count)], axis=0).astype(BF16)
            ghalo = jnp.concatenate([acc[seq, :WIN, :] for seq in range(seq_count)], axis=0).astype(BF16)
            gsel = gsel_ref[...]
            src[:, :, :, :, :, :lanes] = (
                dot(normed_ref[...], gq, TN).astype(BF16).reshape(lead + (share, lanes))
            )
            both = dot(normed_ref[...], gown, TN) + dot(halo_ref[...], ghalo, TN) + dot(nsel_ref[...], gsel, TN)
            src[:, :, :, :, :, lanes:] = both.astype(BF16).reshape(lead + (share, 2 * lanes))
            spots = [pl.ds(kind * width + quad * lanes, lanes) for kind in range(3)]
            own = dot(gq, w_ref[:, spots[0]], NT)
            own = own + dot(gown[:, :lanes], w_ref[:, spots[1]], NT)
            own = own + dot(gown[:, lanes:], w_ref[:, spots[2]], NT)
            near = dot(ghalo[:, :lanes], w_ref[:, spots[1]], NT) + dot(ghalo[:, lanes:], w_ref[:, spots[2]], NT)
            chosen = dot(gsel[:, :lanes], w_ref[:, spots[1]], NT) + dot(gsel[:, lanes:], w_ref[:, spots[2]], NT)
            if quad == 0:
                gn_ref[...], gn_halo[...], gn_sel[...] = own, near, chosen
            else:
                gn_ref[...] += own
                gn_halo[...] += near
                gn_sel[...] += chosen
            cols = pl.ds(quad * lanes, lanes)
            own_vec[0:1, cols] = jnp.sum(gq.astype(F32), axis=0, keepdims=True)
            own_vec[1:2, cols] = (
                jnp.sum(gown[:, lanes:].astype(F32), axis=0, keepdims=True)
                + jnp.sum(ghalo[:, lanes:].astype(F32), axis=0, keepdims=True)
                + jnp.sum(gsel[:, lanes:].astype(F32), axis=0, keepdims=True)
            )
            return qkvs[quad]

        def give_back():
            porter.need(score_ref, tok_ref)
            score_now = score_ref[...].astype(F32)
            gscore = (gates[...] / (1.0 + jnp.exp(score_now))).astype(BF16)
            chosen = gn_sel[...] + dot(gscore[:, :heads], ws_ref[...])
            low = chosen.astype(BF16)
            for seq in range(seq_count):
                hot = hot_columns(selected_row(pick_ref, seq), ranks * cands)
                terms = dot(hot, low[seq * picks : (seq + 1) * picks]).astype(BF16)
                back_src[:, :, :, :, pl.ds(seq * cands, cands), :] = terms.reshape(lead + (cands, width))
                halo_src[seq] = gn_halo[pl.ds(seq * WIN, WIN), :].astype(BF16)
            for i, task in enumerate(backs):
                task.bind(mail, taken[id(task)], back_src, i * back_wide, column_writer(cand_ref, i * back_wide))

            def halo_write(value):
                back_ref[...] = value

            shift_task.bind(mail, taken[id(shift_task)], halo_src, before, halo_write)
            gain_row, shift_row = row(gain_ref), row(shift_ref)
            hat, root = norm_parts(tok_ref[...].astype(F32))

            def hat_of(ref):
                return (ref[...].astype(F32) - shift_row) / gain_row

            own, near = gn_ref[...], gn_halo[...]
            own_vec[2:3, :] = (
                jnp.sum(own * hat, axis=0, keepdims=True)
                + jnp.sum(near * hat_of(halo_ref), axis=0, keepdims=True)
                + jnp.sum(chosen * hat_of(nsel_ref), axis=0, keepdims=True)
            )
            own_vec[3:4, :] = (
                jnp.sum(own, axis=0, keepdims=True)
                + jnp.sum(near, axis=0, keepdims=True)
                + jnp.sum(chosen, axis=0, keepdims=True)
            )
            porter.need(gmid_ref)
            gn_ref[...] = gmid_ref[...] + norm_back(own, hat, root, gain_row)
            porter.ship(gn_ref, gn_far)
            own_vec[4 : vec_ref.shape[0], :] = vec_ref[4:, :]
            own_vec[vec_ref.shape[0] :, :] = dot(gscore, nsel_ref[...], TN)[:heads]

            def vec_write(value):
                total_ref[...] = value

            total.bind(mail, taken[id(total)], lambda: own_vec[...], vec_write)
            return [shift_task] + backs + [total]

        gates[...] = jnp.zeros_like(gates)
        half = blocks // 2
        begun = {"s": shift_task, "t": total, "o": out_task}
        work_of = {"o": out, "give": give_back}
        for i, task in enumerate(downs):
            begun[f"d{i}"], work_of[f"d{i}"] = task, lambda i=i: down(i)
        for i, task in enumerate(ups):
            begun[f"u{i}"], work_of[f"u{i}"] = task, lambda i=i: up(i)
        for i, task in enumerate(qkvs):
            begun[f"q{i}"], work_of[f"fin{i}"] = task, lambda i=i: finish_quad(i)
            work_of[f"q{i}a"] = lambda i=i: attend_back(i, 0, half)
            work_of[f"q{i}b"] = lambda i=i: attend_back(i, half, blocks)
        for i, task in enumerate(backs):
            begun[f"b{i}"] = task
        for entry in SCHEDULE:
            what, name = entry[0], entry[1:]
            if what == "c":
                work_of[name]()
            elif begun[name].stages:
                begun[name].stages.pop(0)()
        for task in tasks:
            while task.stages:
                task.stages.pop(0)()
        mail.finish()
        porter.finish()

    shapes = [
        ((share, 3 * width), F32),
        ((share, width), F32),
        ((share, hidden_size), F32),
        ((down_share, width), F32),
        ((every_row, width), F32),
        ((rows, width), F32),
        ((seq_count * cands, width), F32),
        ((seq_count, WIN, width), BF16),
    ]
    return pl.pallas_call(
        kernel,
        out_shape=[jax.ShapeDtypeStruct(*shape) for shape in shapes],
        in_specs=[WHOLE] * 5 + [FAR] * len(large),
        out_specs=[WHOLE] * 5 + [FAR] + [WHOLE] * 2,
        scratch_shapes=like(large)
        + [pltpu.SemaphoreType.DMA((len(large) + 1,))]
        + boxes
        + work
        + [pltpu.SemaphoreType.DMA((copies,)), pltpu.SemaphoreType.DMA((copies,))],
        compiler_params=pltpu.CompilerParams(
            collective_id=3, has_side_effects=True, vmem_limit_bytes=LIMIT
        ),
    )(score_rows, selected, gain, shift, vec, *large)


def ending(tokens, candidates, gain, base, cand_back, halo_back, total, sums, parts, heads, ranks):
    rows, width = tokens.shape
    seq_count, _, cands = candidates.shape
    tok = rows // seq_count
    share = width // ranks
    up_share = parts * share

    large = (tokens, base, *sums)
    alone = 8

    def kernel(cand_ref, gain_ref, back_ref, halo_ref, total_ref, *refs):
        far_in, refs = refs[: len(large)], refs[len(large) :]
        small_refs, refs = refs[:alone], refs[alone:]
        up_ref, score_ref, grad_far = refs[:3]
        far_out, refs = refs[3 : 3 + len(sums)], refs[3 + len(sums) :]
        near, sems = refs[: len(large)], refs[-1]
        tok_ref, grad_ref = near[:2]
        porter = Porter(sems, far_in, near)
        rank = lax.axis_index("seq")
        gain_row = row(gain_ref)
        values = total_ref[...]

        def pick(values, count, first):
            from_row = lax.broadcasted_iota(jnp.int32, (width, count), 0)
            to_col = lax.broadcasted_iota(jnp.int32, (width, count), 1)
            hot = jnp.where(from_row == to_col + first, 1.0, 0.0)
            return lax.dot_general(
                values, hot, (((1,), (0,)), ((), ())),
                precision=lax.Precision.HIGHEST, preferred_element_type=F32,
            )

        small = pick(values, share, rank * share)
        for i in range(alone):
            small_refs[i][...] = small[i]
        score_ref[...] = small[alone + parts :]
        per_row = width // up_share
        ups = pick(values[alone : alone + parts], up_share, lax.rem(rank, per_row) * up_share)
        which = lax.broadcasted_iota(jnp.int32, ups.shape, 0)
        up_ref[...] = jnp.sum(jnp.where(which == lax.div(rank, per_row), ups, 0.0), axis=0)
        porter.need(tok_ref)

        def returned(rows_in, grad):
            hat, root = norm_parts(rows_in)
            return norm_back(grad, hat, root, gain_row)

        for seq in range(seq_count):
            here = pl.ds(seq * tok, tok)
            hot = hot_columns(cand_ref[seq, pl.ds(rank, 1), :], tok)
            chosen = dot(hot, tok_ref[here, :], TN)
            came = returned(chosen, back_ref[pl.ds(seq * cands, cands), :]).astype(BF16)
            edge = pl.ds((seq + 1) * tok - WIN, WIN)
            near_rows = returned(tok_ref[edge, :].astype(F32), halo_ref[seq].astype(F32))
            if seq == 0:
                porter.need(grad_ref)
            grad_ref[here, :] += dot(hot, came)
            grad_ref[edge, :] += near_rows
            porter.ship(grad_ref.at[here, :], grad_far.at[here, :])
            if seq == 0:
                for came, result in zip(near[2:], far_out):
                    porter.need(came)
                    porter.ship(came, result)
        porter.finish()

    results = [jax.ShapeDtypeStruct((share,), F32)] * alone + [
        jax.ShapeDtypeStruct((up_share,), F32),
        jax.ShapeDtypeStruct((heads, share), F32),
        jax.ShapeDtypeStruct((rows, width), F32),
    ]
    return pl.pallas_call(
        kernel,
        out_shape=results + [jax.ShapeDtypeStruct(array.shape, array.dtype) for array in sums],
        in_specs=[WHOLE] * 5 + [FAR] * len(large),
        out_specs=[WHOLE] * (alone + 2) + [FAR] * (1 + len(sums)),
        scratch_shapes=like(large)
        + [pltpu.SemaphoreType.DMA((len(large) + seq_count + len(sums),))],
        compiler_params=pltpu.CompilerParams(vmem_limit_bytes=LIMIT),
    )(candidates, gain, cand_back, halo_back, total, *large)


def per_device(
    tokens,
    weight_qkv,
    bias_query,
    bias_value,
    weight_score,
    weight_out,
    bias_out,
    gain_one,
    shift_one,
    gain_two,
    shift_two,
    weight_up,
    bias_up,
    weight_down,
    bias_down,
    cotangent,
    lengths,
    candidates,
    selected,
):
    seq_count, tok, width = tokens.shape
    heads = weight_score.shape[1]
    head_size = width // heads
    rows = seq_count * tok
    ranks = lax.axis_size("seq")
    place = Place(ranks, lax.axis_size("grp"))
    parts = bias_up.shape[0] // width
    flat = tokens.reshape(rows, width)
    dy = cotangent.reshape(rows, width)
    (
        normed, queries, ext, halo, nsel, ksel, score,
        attended, probs, mixed, hidden, gpre, n2, branch, grad_middle, gatt, vec,
    ) = front(
        place, lengths, flat, candidates, selected, (gain_one, shift_one), (gain_two, shift_two),
        (bias_query, bias_value, bias_out, bias_up, bias_down), weight_score.T,
        weight_qkv, dy, weight_down, weight_out, weight_up,
    )
    grad_qkv, grad_out, grad_up, grad_down, total, base, cand_back, halo_back = closing(
        place,
        (hidden, dy, gpre, n2, branch, attended),
        (queries, ext, ksel, probs, score, gatt, normed, halo, nsel),
        weight_qkv, weight_score.T, selected, gain_one, shift_one, flat, grad_middle, vec, head_size,
    )
    results = ending(
        flat, candidates, gain_one, base, cand_back, halo_back, total,
        (grad_qkv, grad_out, grad_up, grad_down), parts, heads, ranks,
    )
    small, (up_row, score_rows, grad_tokens), sums = results[:8], results[8:11], results[11:]
    grad_qkv, grad_out, grad_up, grad_down = sums
    return (
        mixed.reshape(tokens.shape),
        grad_tokens.reshape(tokens.shape),
        grad_qkv,
        small[0],
        small[1],
        score_rows.T,
        grad_out,
        small[4],
        small[2],
        small[3],
        small[5],
        small[6],
        grad_up,
        up_row,
        grad_down,
        small[7],
    )


def solution(mesh):
    return jax.shard_map(
        per_device,
        mesh=mesh,
        in_specs=(
            P("grp", "seq", None),
            P(),
            P(),
            P(),
            P(),
            P(),
            P(),
            P(),
            P(),
            P(),
            P(),
            P(),
            P(),
            P(),
            P(),
            P("grp", "seq", None),
            P("grp"),
            P("grp", None, None),
            P("grp", "seq", None),
        ),
        out_specs=(
            P("grp", "seq", None),
            P("grp", "seq", None),
            P("seq", None),
            P("seq"),
            P("seq"),
            P("seq", None),
            P("seq", None),
            P("seq"),
            P("seq"),
            P("seq"),
            P("seq"),
            P("seq"),
            P("seq", None),
            P("seq"),
            P("seq", None),
            P("seq"),
        ),
        check_vma=False,
    )
```

```python
import jax
import jax.numpy as jnp
from jax import lax
from jax.experimental import pallas as pl
from jax.experimental.pallas import tpu as pltpu
from jax.sharding import PartitionSpec as P

WIN = 64
MESH_ID = pl.DeviceIdType.MESH
BF16 = jnp.bfloat16
F32 = jnp.float32


class Place:
    def __init__(self, seq_count, grp_count):
        self.nc = 2
        self.np = 2 if seq_count % 8 == 0 else 1
        self.nq = self.np
        self.nz = self.nq * self.np
        self.nx = seq_count // (self.nc * self.nz)
        self.ng = grp_count
        self.lead = (self.nq, self.np, self.nx, self.nc)
        self.counts = {
            "q": self.nq, "p": self.np, "z": self.nz, "x": self.nx, "c": self.nc, "g": self.ng,
        }

    def locate(self):
        rank = lax.axis_index("seq")
        z = lax.div(rank, self.nc * self.nx)
        self.at = {
            "c": lax.rem(rank, self.nc),
            "x": lax.rem(lax.div(rank, self.nc), self.nx),
            "z": z,
            "p": lax.rem(z, self.np),
            "q": lax.div(z, self.np),
            "g": lax.axis_index("grp"),
        }
        return self

    def device(self, axis, where):
        at = dict(self.at)
        at[axis] = where
        z = at["z"] if axis == "z" else at["q"] * self.np + at["p"]
        return ((z * self.nx + at["x"]) * self.nc + at["c"], at["g"])

    def others(self, axis):
        count = self.counts[axis]
        return [lax.rem(self.at[axis] + step, count) for step in range(1, count)]

    def greet(self, axes, more):
        barrier = pltpu.get_barrier_semaphore()
        devices = list(more)
        for axis in axes:
            devices += [self.device(axis, where) for where in self.others(axis)]
        for device in devices:
            pl.semaphore_signal(barrier, inc=1, device_id=device, device_id_type=MESH_ID)
        return barrier, len(devices)


class Mail:
    def __init__(self, send_sems, recv_sems):
        self.send_sems, self.recv_sems, self.count, self.sent = send_sems, recv_sems, 0, []

    def send(self, src, dst, device):
        copy = pltpu.make_async_remote_copy(
            src_ref=src,
            dst_ref=dst,
            send_sem=self.send_sems.at[self.count],
            recv_sem=self.recv_sems.at[self.count],
            device_id=device,
            device_id_type=MESH_ID,
        )
        copy.start()
        self.count += 1
        self.sent.append(copy)
        return copy

    def settle(self, copies):
        for copy in copies:
            copy.wait_send()
        gone = {id(copy) for copy in copies}
        self.sent = [copy for copy in self.sent if id(copy) not in gone]

    def finish(self):
        self.settle(list(self.sent))


def each(dims, body):
    count = 1
    for dim in dims:
        count *= dim
    if count == 1:
        body((0,) * len(dims))
        return

    def turn(flat, _):
        index, rest = [], flat
        for dim in reversed(dims):
            index.insert(0, lax.rem(rest, dim))
            rest = lax.div(rest, dim)
        body(tuple(index))
        return 0

    lax.fori_loop(0, count, turn, 0)


class Reduction:
    def __init__(self, place, rows, wide, order, groups=True):
        self.place, self.rows, self.wide, self.order, self.groups = place, rows, wide, order, groups
        self.split = "g" in order
        axes = ["q", "p", "x"]
        self.part = wide
        if self.split:
            axes.insert(0, "g")
            self.part = wide // place.ng
        self.axes = axes
        lead = tuple(place.counts[axis] for axis in axes)
        self.boxes = [lead + (rows, self.part)]
        self.copies = place.ng if self.split else 1
        left = list(axes)
        for axis in order:
            left.remove(axis)
            others = place.counts[axis] - 1
            self.copies += others
            lead = tuple(place.counts[one] for one in left)
            self.boxes.append((max(others, 1),) + lead + (rows, self.part))
        if groups:
            self.boxes.append((place.ng, rows, self.part))
            self.copies += place.ng - 1

    def scratch(self):
        return [pltpu.VMEM(box, BF16) for box in self.boxes]

    def bind(self, mail, refs, src, first, out):
        place, part = self.place, self.part
        here = place.at
        pieces = place.ng if self.split else 1
        state = {}
        self.freed = False

        def start():
            far = place.others("c")[0]
            device = place.device("c", far)
            state["wait"] = []
            for i in range(pieces):
                view = src.at[:, :, :, far, :, pl.ds(first + i * part, part)]
                target = refs[0].at[i] if self.split else refs[0]
                state["wait"].append(mail.send(view, target, device))

        def send(level):
            axis = self.order[level]
            current, axes = state["current"], state["axes"]
            spot = axes.index(axis)
            state["spot"] = spot
            state["wait"] = [
                mail.send(
                    current.at[(slice(None),) * spot + (far,)],
                    refs[level + 1].at[i],
                    place.device(axis, far),
                )
                for i, far in enumerate(place.others(axis))
            ]

        def after_core():
            for copy in state["wait"]:
                copy.wait_recv()
            box = refs[0]

            def add(index):
                for i in range(pieces):
                    at = (i,) + index if self.split else index
                    mine = src[index + (here["c"], slice(None), pl.ds(first + i * part, part))]
                    box[at] = (mine.astype(F32) + box[at].astype(F32)).astype(BF16)

            each(place.lead[:3], add)
            mail.settle(state["wait"])
            self.freed = True
            state["current"], state["axes"] = box, list(self.axes)
            send(0)

        def after(level):
            def run():
                for copy in state["wait"]:
                    copy.wait_recv()
                axis, spot, current = self.order[level], state["spot"], state["current"]
                axes = [one for one in state["axes"] if one != axis]
                box = refs[level + 1]

                def total(index):
                    at = index[:spot] + (here[axis],) + index[spot:]
                    value = current[at].astype(F32)
                    for i in range(place.counts[axis] - 1):
                        value = value + box[(i,) + index].astype(F32)
                    return value

                if level + 1 < len(self.order):

                    def add(index):
                        box[(0,) + index] = total(index).astype(BF16)

                    each(tuple(place.counts[one] for one in axes), add)
                    state["current"], state["axes"] = box.at[0], axes
                    send(level + 1)
                    return
                value = total(())
                if not self.groups:
                    out(0, value)
                    return
                last = refs[-1]
                mine = here["g"]
                last[mine] = value.astype(BF16)
                state["wait"] = [
                    mail.send(last.at[mine], last.at[mine], place.device("g", far))
                    for far in place.others("g")
                ]

            return run

        def end():
            for copy in state["wait"]:
                copy.wait_recv()
            last = refs[-1]
            if self.split:
                for i in range(place.ng):
                    out(i * part, last[i].astype(F32))
                return
            value = last[0].astype(F32)
            for i in range(1, place.ng):
                value = value + last[i].astype(F32)
            out(0, value)

        self.stages = [start, after_core] + [after(level) for level in range(len(self.order))]
        if self.groups:
            self.stages.append(end)
        return self


class Total:
    axes = "cxpqg"

    def __init__(self, place, shape):
        self.place, self.shape = place, shape
        self.counts = [place.counts[axis] for axis in self.axes]
        self.copies = sum(count - 1 for count in self.counts)

    def scratch(self):
        return [
            pltpu.VMEM((count,) + self.shape, BF16 if level else F32)
            for level, count in enumerate(self.counts)
        ]

    def bind(self, mail, refs, src, out):
        pending = {}
        place = self.place

        def stage(level):
            def run():
                if level == 0:
                    value = src()
                else:
                    for copy in pending[level - 1]:
                        copy.wait_recv()
                    box = refs[level - 1]
                    value = box[0].astype(F32)
                    for i in range(1, self.counts[level - 1]):
                        value = value + box[i].astype(F32)
                if level == len(self.axes):
                    out(value)
                    return
                box, axis = refs[level], self.axes[level]
                here = place.at[axis]
                box[here] = value.astype(box.dtype)
                pending[level] = [
                    mail.send(box.at[here], box.at[here], place.device(axis, far))
                    for far in place.others(axis)
                ]

            return run

        self.stages = [stage(level) for level in range(len(self.axes) + 1)]
        return self

NT = (((1,), (1,)), ((), ()))
TN = (((0,), (0,)), ((), ()))
NEG_FILL = -1e30
QUAD = 4
WHOLE = pl.BlockSpec(memory_space=pltpu.VMEM)
FAR = pl.BlockSpec(memory_space=pl.ANY)
LIMIT = 63 * 2**20
CURVE = 0.7978845608028654
CUBE = 0.044715


def dot(a, b, dims=(((1,), (0,)), ((), ()))):
    return lax.dot_general(a, b, dims, preferred_element_type=F32)


class Porter:
    def __init__(self, sems, sources, places):
        self.sems, self.count, self.out = sems, 0, []
        self.coming = {}
        for source, place in zip(sources, places):
            copy = pltpu.make_async_copy(source, place, self.sems.at[self.count])
            copy.start()
            self.count += 1
            self.coming[id(place)] = copy

    def need(self, *places):
        for place in places:
            copy = self.coming.pop(id(place), None)
            if copy is not None:
                copy.wait()

    def ship(self, place, target):
        copy = pltpu.make_async_copy(place, target, self.sems.at[self.count])
        copy.start()
        self.count += 1
        self.out.append(copy)

    def finish(self):
        for copy in list(self.coming.values()) + self.out:
            copy.wait()


def like(arrays):
    return [pltpu.VMEM(array.shape, array.dtype) for array in arrays]


def row(ref):
    return ref[...].reshape(1, ref.shape[0])


def norm_parts(values):
    center = values - jnp.mean(values, axis=-1, keepdims=True)
    root = lax.rsqrt(jnp.mean(center * center, axis=-1, keepdims=True) + 1e-05)
    return center * root, root


def norm_back(grad, hat, root, gain):
    gx = grad * gain
    return root * (
        gx - jnp.mean(gx, axis=-1, keepdims=True) - hat * jnp.mean(gx * hat, axis=-1, keepdims=True)
    )


def hot_columns(index_row, count):
    rows = lax.broadcasted_iota(jnp.int32, (count, index_row.shape[1]), 0)
    return jnp.where(rows == index_row, 1.0, 0.0).astype(BF16)


def selected_row(sel_ref, seq):
    return jnp.concatenate([sel_ref[seq, b : b + 1, :] for b in range(sel_ref.shape[1])], axis=1)


def spread_heads(rows, size):
    lane_head = lax.broadcasted_iota(jnp.int32, rows.shape, 1) // size
    zero = jnp.zeros_like(rows)
    return jnp.concatenate([jnp.where(lane_head == h, rows, zero) for h in range(QUAD)], axis=0)


def merge_heads(wide, size):
    count = wide.shape[0] // QUAD
    lane_head = lax.broadcasted_iota(jnp.int32, (count, wide.shape[1]), 1) // size
    result = wide[:count]
    for h in range(1, QUAD):
        result = jnp.where(lane_head == h, wide[h * count : (h + 1) * count], result)
    return result


def window_bias(base, length):
    shape = (2 * WIN, QUAD * WIN)
    key = lax.broadcasted_iota(jnp.int32, shape, 0)
    query = lax.broadcasted_iota(jnp.int32, shape, 1) % WIN
    key_pos = key + (base - WIN)
    keep = (
        (key > query)
        & (key <= query + WIN)
        & (key_pos >= 0)
        & ((key_pos < length) | (key == query + WIN))
    )
    return jnp.where(keep, 0.0, NEG_FILL).astype(F32)


def keys_of(ext_ref, sel_ref, seq, start, rows_at, cols):
    return jnp.concatenate(
        [ext_ref[seq, pl.ds(start, 2 * WIN), cols], sel_ref[pl.ds(rows_at, WIN), cols]], axis=0
    )


def front(place, lengths, tokens, candidates, selected, norm_one, norm_two, biases, score_rows, weight_qkv, dy, weight_down, weight_out, weight_up):
    rows, width = tokens.shape
    seq_count, ranks, cands = candidates.shape
    tok = rows // seq_count
    blocks = tok // WIN
    every = ranks * cands
    heads = score_rows.shape[0]
    head_size = width // heads
    lanes = QUAD * head_size
    quads = width // lanes
    hidden_size = weight_up.shape[1]
    parts = hidden_size // width
    nz, nx, nc = place.nz, place.nx, place.nc
    copies = 1 + (nz - 1) + (nx - 1) * nz + nz * nx
    scale = head_size ** (-0.5)
    picks = blocks * WIN
    small = (tokens, candidates, selected, *norm_one, *norm_two, *biases, score_rows)
    large = (weight_qkv, dy, weight_down, weight_out, weight_up)
    shapes = [
        ((rows, width), BF16),
        ((rows, width), BF16),
        ((seq_count, tok + WIN, 2 * width), BF16),
        ((seq_count * WIN, width), BF16),
        ((seq_count * picks, width), BF16),
        ((seq_count * picks, 2 * width), BF16),
        ((seq_count * picks, 128), BF16),
        ((rows, width), BF16),
        ((seq_count * blocks, quads, 3 * WIN, QUAD * WIN), BF16),
        ((rows, width), BF16),
        ((rows, hidden_size), BF16),
        ((rows, hidden_size), BF16),
        ((rows, width), BF16),
        ((rows, width), BF16),
        ((rows, width), F32),
        ((rows, width), BF16),
        ((8 + parts, width), F32),
    ]

    def kernel(
        len_ref, tok_ref, cand_ref, pick_ref, gain_one, shift_one, gain_two, shift_two,
        bq_ref, bv_ref, bo_ref, bu_ref, bd_ref, ws_ref, *refs,
    ):
        far_in, refs = refs[: len(large)], refs[len(large) :]
        far_out, refs = refs[: len(shapes)], refs[len(shapes) :]
        near_in, refs = refs[: len(large)], refs[len(large) :]
        near_out, refs = refs[: len(shapes)], refs[len(shapes) :]
        bias_ref, gat, halo_out, halo_in, move_sems, send_sems, recv_sems = refs
        w_ref, dy_ref, wd_ref, wo_ref, wu_ref = near_in
        (
            normed_ref, q_ref, ext_ref, halo_ref, nsel_ref, ksel_ref, score_ref,
            att_ref, prob_ref, mixed_ref, hidden_ref, gpre_ref, n2_ref, branch_ref, gmid_ref, gatt_ref, vec_ref,
        ) = near_out
        porter = Porter(move_sems, far_in, near_in)

        def ship(ref):
            porter.ship(ref, far_out[[one is ref for one in near_out].index(True)])

        place.locate()
        mail = Mail(send_sems, recv_sems)
        z, x, c, g = (place.at[axis] for axis in "zxcg")
        rank = lax.axis_index("seq")
        after = (lax.rem(rank + 1, ranks), g)
        before = (lax.rem(rank + ranks - 1, ranks), g)
        barrier = pltpu.get_barrier_semaphore()
        greeted = [after, before]
        for axis in "czx":
            greeted += [place.device(axis, where) for where in place.others(axis)]
        for device in greeted:
            pl.semaphore_signal(barrier, inc=1, device_id=device, device_id_type=MESH_ID)
        gain_row, shift_row = row(gain_one), row(shift_one)

        def norm(values):
            return (norm_parts(values.astype(F32))[0] * gain_row + shift_row).astype(BF16)

        for seq in range(seq_count):
            hot = hot_columns(cand_ref[seq, pl.ds(rank, 1), :], tok)
            gat[seq, z, x, c] = norm(dot(hot, tok_ref[pl.ds(seq * tok, tok), :], TN))
            halo_out[seq] = norm(tok_ref[pl.ds((seq + 1) * tok - WIN, WIN), :])
        pl.semaphore_wait(barrier, len(greeted))

        def slot(zi, xi, ci):
            return gat.at[:, zi, xi, ci]

        by_z = [
            mail.send(slot(z, x, c), slot(z, x, c), place.device("z", far))
            for far in place.others("z")
        ]
        halo_copy = mail.send(halo_out, halo_in, after)
        core = place.device("c", place.others("c")[0])
        by_x, by_c = [], []

        def forward_x(zi):
            by_x.append(
                [
                    mail.send(slot(zi, x, c), slot(zi, x, c), place.device("x", far))
                    for far in place.others("x")
                ]
            )
            by_c.append(mail.send(slot(zi, x, c), slot(zi, x, c), core))

        def forward_c(zi, step):
            for i, copy in enumerate(by_x[step]):
                copy.wait_recv()
                come = lax.rem(x + nx - 1 - i, nx)
                by_c.append(mail.send(slot(zi, come, c), slot(zi, come, c), core))

        forward_x(z)
        for seq in range(seq_count):
            normed_ref[pl.ds(seq * tok, tok), :] = norm(tok_ref[pl.ds(seq * tok, tok), :])
        sources = [z] + [lax.rem(z + nz - 1 - i, nz) for i in range(nz - 1)]
        ship(normed_ref)
        porter.need(w_ref)
        queries = dot(normed_ref[...], w_ref[:, :width]) + row(bq_ref)
        q_ref[...] = (queries.astype(BF16).astype(F32) * scale).astype(BF16)
        ship(q_ref)
        value_bias = row(bv_ref)

        def project(values, half):
            part = dot(values, w_ref[:, pl.ds((1 + half) * width, width)])
            if half == 1:
                part = part + value_bias
            return part.astype(BF16)

        for i in range(nz - 1):
            by_z[i].wait_recv()
            forward_x(sources[i + 1])
        forward_c(sources[0], 0)
        for half in range(2):
            cols = pl.ds(half * width, width)
            for seq in range(seq_count):
                ext_ref[seq, pl.ds(WIN, tok), cols] = project(
                    normed_ref[pl.ds(seq * tok, tok), :], half
                )
        halo_copy.wait_recv()
        for seq in range(seq_count):
            halo_ref[pl.ds(seq * WIN, WIN), :] = halo_in[seq]
        for half in range(2):
            part = project(halo_ref[...], half)
            for seq in range(seq_count):
                ext_ref[seq, pl.ds(0, WIN), pl.ds(half * width, width)] = part[
                    seq * WIN : (seq + 1) * WIN
                ]
        ship(halo_ref)
        ship(ext_ref)
        porter.need(dy_ref, wd_ref)
        for part in range(parts):
            cols = pl.ds(part * width, width)
            gpre_ref[:, cols] = dot(dy_ref[...], wd_ref[cols, :], NT).astype(BF16)
        for i in range(1, nz):
            forward_c(sources[i], i)
        counted = []
        for seq in range(seq_count):
            index = selected_row(pick_ref, seq)
            inner = hot_columns(index % cands, cands)
            table = cand_ref[seq].astype(F32).astype(BF16)
            offset = dot(table, inner)
            block_of = lax.broadcasted_iota(jnp.int32, (ranks, picks), 0)
            chosen = jnp.where(block_of == index // cands, offset, 0.0)
            position = jnp.sum(chosen, axis=0, keepdims=True)
            position = position + ((index // cands) * tok).astype(F32)
            lane_block = lax.broadcasted_iota(jnp.int32, (1, picks), 1) // WIN
            limit = jnp.minimum((rank * blocks + lane_block) * WIN - WIN + 1, len_ref[seq])
            flag = jnp.where(position < limit.astype(F32), 1.0, 0.0)
            across = lax.broadcasted_iota(jnp.int32, (picks, picks), 0)
            down = lax.broadcasted_iota(jnp.int32, (picks, picks), 1)
            diagonal = jnp.where(across == down, flag, 0.0).astype(BF16)
            counted.append(dot(diagonal, jnp.ones((picks, width), BF16)))
        head_of = lax.broadcasted_iota(jnp.int32, (heads, width), 1) // head_size
        widen = jnp.where(head_of == lax.broadcasted_iota(jnp.int32, (heads, width), 0), 1.0, 0.0)
        score_ref[...] = jnp.zeros_like(score_ref)
        for copy in by_c:
            copy.wait_recv()
        for seq in range(seq_count):
            here = pl.ds(seq * picks, picks)
            hot = hot_columns(selected_row(pick_ref, seq), every)
            picked = dot(hot, gat[seq].reshape(every, width), TN).astype(BF16)
            nsel_ref[here, :] = picked
            for half in range(2):
                ksel_ref[here, pl.ds(half * width, width)] = project(picked, half)
            score = dot(picked, ws_ref[...], NT).astype(BF16)
            score_ref[here, pl.ds(0, heads)] = score
            wide = dot(score, widen.astype(BF16))
            gate = jnp.minimum(wide, 0.0) - jnp.log1p(jnp.exp(-jnp.abs(wide)))
            bias_ref[here, :] = jnp.where(counted[seq] > 0.5, gate, NEG_FILL)
        ship(nsel_ref)
        ship(ksel_ref)
        ship(score_ref)
        base = rank * tok

        def attend(block, seq):
            i = seq * blocks + block
            at = pl.multiple_of(i * WIN, WIN)
            start = pl.multiple_of(block * WIN, WIN)
            mask = window_bias(base + block * WIN, len_ref[seq])
            for quad in range(quads):
                cols = pl.ds(quad * lanes, lanes)
                vals = pl.ds(width + quad * lanes, lanes)
                keys = keys_of(ext_ref, ksel_ref, seq, start, at, cols)
                values = keys_of(ext_ref, ksel_ref, seq, start, at, vals)
                wide = spread_heads(q_ref[pl.ds(at, WIN), cols], head_size)
                logits = dot(keys, wide, NT)
                logits = logits + jnp.concatenate([mask, bias_ref[pl.ds(at, WIN), cols]], axis=0)
                grown = jnp.exp(logits - jnp.max(logits, axis=0, keepdims=True))
                probs = (grown / jnp.sum(grown, axis=0, keepdims=True)).astype(BF16)
                prob_ref[i, quad] = probs
                att_ref[pl.ds(at, WIN), cols] = merge_heads(
                    dot(probs, values, TN), head_size
                ).astype(BF16)

        def attend_all(pair, _):
            for seq in range(seq_count):
                attend(pair, seq)
                attend(pair + blocks // 2, seq)
            return 0

        lax.fori_loop(0, blocks // 2, attend_all, 0)
        ship(att_ref)
        ship(prob_ref)
        porter.need(wo_ref)
        gain_row = row(gain_two)
        middle = tok_ref[...].astype(F32) + dot(att_ref[...], wo_ref[...]) + row(bo_ref)
        gmid_ref[...] = middle
        hat, _ = norm_parts(middle)
        n2_ref[...] = (hat * gain_row + row(shift_two)).astype(BF16)
        ship(n2_ref)
        porter.need(wu_ref)
        bias_row = row(bu_ref)
        mixed = middle + row(bd_ref)
        grad_normed = jnp.zeros((rows, width), F32)
        for part in range(parts):
            cols = pl.ds(part * width, width)
            pre = dot(n2_ref[...], wu_ref[:, cols]) + bias_row[:, part * width : (part + 1) * width]
            square = pre * pre
            tanh = jnp.tanh(CURVE * pre * (1.0 + CUBE * square))
            half = 0.5 + 0.5 * tanh
            hidden_ref[:, cols] = (pre * half).astype(BF16)
            slope = half + 0.5 * pre * (1.0 - tanh * tanh) * (CURVE + 3 * CUBE * CURVE * square)
            gpre = (gpre_ref[:, cols].astype(F32) * slope).astype(BF16)
            gpre_ref[:, cols] = gpre
            vec_ref[pl.ds(8 + part, 1), :] = jnp.sum(gpre.astype(F32), axis=0, keepdims=True)
            mixed = mixed + dot(hidden_ref[:, cols], wd_ref[cols, :])
            grad_normed = grad_normed + dot(gpre, wu_ref[:, cols], NT)
        ship(hidden_ref)
        ship(gpre_ref)
        mixed_ref[...] = mixed.astype(BF16)
        ship(mixed_ref)
        hat, root = norm_parts(gmid_ref[...])
        dy_wide = dy_ref[...].astype(F32)
        vec_ref[0:4, :] = jnp.zeros((4, width), F32)
        vec_ref[5:6, :] = jnp.sum(grad_normed * hat, axis=0, keepdims=True)
        vec_ref[6:7, :] = jnp.sum(grad_normed, axis=0, keepdims=True)
        vec_ref[7:8, :] = jnp.sum(dy_wide, axis=0, keepdims=True)
        grad_middle = dy_wide + norm_back(grad_normed, hat, root, gain_row)
        gmid_ref[...] = grad_middle
        ship(gmid_ref)
        branch = grad_middle.astype(BF16)
        branch_ref[...] = branch
        ship(branch_ref)
        vec_ref[4:5, :] = jnp.sum(branch.astype(F32), axis=0, keepdims=True)
        ship(vec_ref)
        gatt_ref[...] = dot(branch, wo_ref[...], NT).astype(BF16)
        ship(gatt_ref)
        mail.finish()
        porter.finish()

    return pl.pallas_call(
        kernel,
        out_shape=[jax.ShapeDtypeStruct(*shape) for shape in shapes],
        in_specs=[pl.BlockSpec(memory_space=pltpu.SMEM)] + [WHOLE] * len(small) + [FAR] * len(large),
        out_specs=[FAR] * len(shapes),
        scratch_shapes=like(large)
        + [pltpu.VMEM(*shape) for shape in shapes]
        + [
            pltpu.VMEM((seq_count * picks, width), F32),
            pltpu.VMEM((seq_count, nz, nx, nc, cands, width), BF16),
            pltpu.VMEM((seq_count, WIN, width), BF16),
            pltpu.VMEM((seq_count, WIN, width), BF16),
            pltpu.SemaphoreType.DMA((len(large) + len(shapes),)),
            pltpu.SemaphoreType.DMA((copies,)),
            pltpu.SemaphoreType.DMA((copies,)),
        ],
        compiler_params=pltpu.CompilerParams(
            collective_id=2, has_side_effects=True, vmem_limit_bytes=LIMIT
        ),
    )(lengths, *small, *large)


SCHEDULE = (
    "cd2", "bd2", "cd0", "bd0", "cu2", "ad2", "bu2", "cu1", "ad0", "bu1", "cd1", "au2",
    "bd1", "cu3", "au1", "bu3", "cq0a", "au3", "ad1", "cq0b", "co", "ad2", "bo", "cfin0",
    "ao", "bq0", "cu0", "au2", "bu0", "cq1a", "au0", "aq0", "cq1b", "au1", "cfin1", "bq1",
    "cq2a", "au3", "au2", "aq1", "cq2b", "ad2", "ad0", "au1", "ao", "ad1", "cfin2", "au0",
    "au2", "aq0", "bq2", "cgive", "aq2", "ad2", "au3", "au1", "au2", "bs", "ao", "bb0",
    "bb1", "aq0", "bt", "at", "ab1", "ad1", "ab0", "au2", "ad2", "au1", "au3", "ao",
    "ad0", "aq2", "at", "au1", "ad2", "au0", "au3", "ab0", "aq0", "aq1", "ao", "ad0",
    "at", "au3", "ad1", "aq1", "aq0", "au0", "aq2", "as", "ad0", "ab0", "ab1", "at",
    "ad1", "aq0", "aq2", "au0", "ad0", "at", "aq1", "ad1", "ab0", "ab1", "au0", "aq2",
    "aq1", "aq2", "ab1", "aq1",
)
ORDERS = {
    "b0": "pxq",
    "b1": "xpq",
    "d0": "qxgp",
    "d1": "gqxp",
    "d2": "xqgp",
    "o": "xpq",
    "q0": "pgxq",
    "q1": "xgqp",
    "q2": "gxpq",
    "u0": "gxqp",
    "u1": "pxgq",
    "u2": "gxqp",
    "u3": "gxpq",
}

class Shift:
    copies = 1

    def __init__(self, shape):
        self.shape = shape

    def scratch(self):
        return [pltpu.VMEM(self.shape, BF16)]

    def bind(self, mail, refs, src, device, out):
        held = []

        def start():
            held.append(mail.send(src, refs[0], device))

        def finish():
            held[0].wait_recv()
            out(refs[0][...])

        self.stages = [start, finish]
        return self


def closing(place, gradients, attention, weight_qkv, score_rows, selected, gain, shift, tokens, grad_middle, vec, head_size):
    hidden, dy, gpre, n2, branch, attended = gradients
    queries, ext, ksel, probs, score, gatt, normed, halo, nsel = attention
    rows, width = dy.shape
    seq_count, ext_rows, _ = ext.shape
    tok = ext_rows - WIN
    blocks = tok // WIN
    steps = seq_count * blocks
    lanes = QUAD * head_size
    quads = width // lanes
    heads = score_rows.shape[0]
    hidden_size = hidden.shape[1]
    parts = hidden_size // width
    large = tuple(gradients) + tuple(attention) + (weight_qkv, tokens, grad_middle)
    ng = place.ng
    lead = place.lead
    ranks = place.nz * place.nx * place.nc
    share = width // ranks
    down_share = hidden_size // ranks
    down_wide = 256
    every_row = vec.shape[0] + heads
    picks = blocks * WIN
    cands = 32
    scale = head_size ** (-0.5)
    can_split = width % (128 * ng) == 0 and down_wide % (128 * ng) == 0
    def order(name):
        given = ORDERS[name]
        return given if can_split else given.replace("g", "")

    def reduction(name, piece_rows, wide, groups=True):
        return Reduction(place, piece_rows, wide, order(name), groups)

    downs = [reduction(f"d{i}", down_share, down_wide) for i in range(width // down_wide)]
    ups = [reduction(f"u{i}", share, width) for i in range(parts)]
    out_task = reduction("o", share, width)
    qkvs = [reduction(f"q{i}", share, width) for i in range(quads)]
    back_wide = width // 2
    backs = [reduction(f"b{i}", seq_count * cands, back_wide, False) for i in range(2)]
    total = Total(place, (every_row, width))
    shift_task = Shift((seq_count, WIN, width))
    tasks = downs + ups + [out_task] + qkvs + backs + [total, shift_task]
    boxes, counts = [], []
    for task in tasks:
        mine = task.scratch()
        boxes.extend(mine)
        counts.append(len(mine))
    copies = sum(task.copies for task in tasks)
    slots, down_slots = (3, 2) if can_split else (2, 1)
    work = [
        pltpu.VMEM((slots,) + lead + (share, width), BF16),
        pltpu.VMEM((down_slots,) + lead + (down_share, down_wide), BF16),
        pltpu.VMEM(lead + (seq_count * cands, width), BF16),
        pltpu.VMEM((seq_count, WIN, width), BF16),
        pltpu.VMEM((rows, lanes), BF16),
        pltpu.VMEM((seq_count, ext_rows, 2 * lanes), F32),
        pltpu.VMEM((seq_count * picks, 2 * lanes), BF16),
        pltpu.VMEM((seq_count * picks, 128), F32),
        pltpu.VMEM((seq_count * picks, width), F32),
        pltpu.VMEM((seq_count * WIN, width), F32),
        pltpu.VMEM((every_row, width), F32),
        pltpu.VMEM((rows, width), F32),
    ]

    def kernel(*refs):
        ws_ref, pick_ref, gain_ref, shift_ref, vec_ref = refs[:5]
        far = refs[5 : 5 + len(large)]
        refs = refs[5 + len(large) :]
        gqkv_ref, gout_ref, gup_ref, gdown_ref, total_ref, gn_far, cand_ref, back_ref = refs[:8]
        near = refs[8 : 8 + len(large)]
        (
            hid_ref, dy_ref, gpre_ref, n2_ref, branch_ref, att_ref,
            q_ref, ext_ref, sel_ref, prob_ref, score_ref, gatt_ref, normed_ref, halo_ref, nsel_ref,
            w_ref, tok_ref, gmid_ref,
        ) = near
        porter = Porter(refs[8 + len(large)], far, near)
        rest = list(refs[9 + len(large) :])
        recv_sems, send_sems = rest.pop(), rest.pop()
        stage, down_stage, back_src, halo_src, gq_ref, acc, gsel_ref, gates, gn_sel, gn_halo, own_vec, gn_ref = rest[-12:]
        room = rest[:-12]
        place.locate()
        mail = Mail(send_sems, recv_sems)
        rank, g = lax.axis_index("seq"), lax.axis_index("grp")
        after = (lax.rem(rank + 1, ranks), g)
        before = (lax.rem(rank + ranks - 1, ranks), g)
        barrier, answers = place.greet("cxpqg", [after, before])
        pl.semaphore_wait(barrier, answers)
        taken = {}
        for task, count in zip(tasks, counts):
            taken[id(task)] = room[:count]
            del room[:count]

        def column_writer(out, first):
            def write(offset, value):
                out[:, pl.ds(first + offset, value.shape[1])] = value

            return write

        def quad_writer(quad):
            def write(offset, value):
                wide = value.shape[1]
                low = offset
                while low < offset + wide:
                    kind = low // lanes
                    high = min(offset + wide, (kind + 1) * lanes)
                    at = kind * width + quad * lanes + low - kind * lanes
                    gqkv_ref[:, pl.ds(at, high - low)] = value[:, low - offset : high - offset]
                    low = high

            return write

        used = [0, 0]

        holders = [[None] * slots, [None] * down_slots]

        def bind(task, which, out):
            count = (slots, down_slots)[which]
            spot = used[which] % count
            used[which] += 1
            held = holders[which][spot]
            while held is not None and not held.freed:
                held.stages.pop(0)()
            holders[which][spot] = task
            src = (stage, down_stage)[which].at[spot]
            task.bind(mail, taken[id(task)], src, 0, out)
            return src

        def fill(src, left, right):
            value = dot(left, right, TN).astype(BF16)
            src[...] = value.reshape(src.shape)

        def down(i):
            porter.need(hid_ref, dy_ref)
            src = bind(downs[i], 1, column_writer(gdown_ref, i * down_wide))
            fill(src, hid_ref[...], dy_ref[:, i * down_wide : (i + 1) * down_wide])
            return downs[i]

        def up(i):
            porter.need(n2_ref, gpre_ref)
            src = bind(ups[i], 0, column_writer(gup_ref, i * width))
            fill(src, n2_ref[...], gpre_ref[:, i * width : (i + 1) * width])
            return ups[i]

        def out():
            porter.need(att_ref, branch_ref)
            src = bind(out_task, 0, column_writer(gout_ref, 0))
            fill(src, att_ref[...], branch_ref[...])
            return out_task

        def attend_back(quad, first, last):
            cols = pl.ds(quad * lanes, lanes)
            vals = pl.ds(width + quad * lanes, lanes)

            def step(seq, block):
                i = seq * blocks + block
                at, start = i * WIN, block * WIN
                keys = keys_of(ext_ref, sel_ref, seq, start, at, cols)
                values = keys_of(ext_ref, sel_ref, seq, start, at, vals)
                wide_q = spread_heads(q_ref[pl.ds(at, WIN), cols], head_size)
                wide_g = spread_heads(gatt_ref[pl.ds(at, WIN), cols], head_size)
                low_probs = prob_ref[i, quad]
                full = low_probs.astype(F32)
                weighed = full * dot(values, wide_g, NT)
                delta = jnp.sum(weighed, axis=0, keepdims=True)
                low = (weighed - full * delta).astype(BF16)
                grad_values = dot(low_probs, wide_g)
                grad_keys = dot(low, wide_q)
                gq = merge_heads(dot(low, keys, TN), head_size) * scale
                gq_ref[pl.ds(at, WIN), :] = gq.astype(BF16)
                acc[seq, pl.ds(start, 2 * WIN), :lanes] += grad_keys[: 2 * WIN]
                acc[seq, pl.ds(start, 2 * WIN), lanes:] += grad_values[: 2 * WIN]
                gsel_ref[pl.ds(at, WIN), :lanes] = grad_keys[2 * WIN :].astype(BF16)
                gsel_ref[pl.ds(at, WIN), lanes:] = grad_values[2 * WIN :].astype(BF16)
                head = lax.broadcasted_iota(jnp.int32, (lanes, 128), 0) // head_size + quad * QUAD
                pick = jnp.where(head == lax.broadcasted_iota(jnp.int32, (lanes, 128), 1), 1.0, 0.0)
                gates[pl.ds(at, WIN), :] += dot(low[2 * WIN :], pick.astype(BF16))

            porter.need(q_ref, ext_ref, sel_ref, prob_ref, gatt_ref)
            if first == 0:
                acc[...] = jnp.zeros_like(acc)
            for block in range(first, last):
                for seq in range(seq_count):
                    step(seq, block)

        def finish_quad(quad):
            porter.need(normed_ref, halo_ref, nsel_ref, w_ref)
            src = bind(qkvs[quad], 0, quad_writer(quad))
            gq = gq_ref[...]
            gown = jnp.concatenate([acc[seq, WIN:, :] for seq in range(seq_count)], axis=0).astype(BF16)
            ghalo = jnp.concatenate([acc[seq, :WIN, :] for seq in range(seq_count)], axis=0).astype(BF16)
            gsel = gsel_ref[...]
            src[:, :, :, :, :, :lanes] = (
                dot(normed_ref[...], gq, TN).astype(BF16).reshape(lead + (share, lanes))
            )
            both = dot(normed_ref[...], gown, TN) + dot(halo_ref[...], ghalo, TN) + dot(nsel_ref[...], gsel, TN)
            src[:, :, :, :, :, lanes:] = both.astype(BF16).reshape(lead + (share, 2 * lanes))
            spots = [pl.ds(kind * width + quad * lanes, lanes) for kind in range(3)]
            own = dot(gq, w_ref[:, spots[0]], NT)
            own = own + dot(gown[:, :lanes], w_ref[:, spots[1]], NT)
            own = own + dot(gown[:, lanes:], w_ref[:, spots[2]], NT)
            near = dot(ghalo[:, :lanes], w_ref[:, spots[1]], NT) + dot(ghalo[:, lanes:], w_ref[:, spots[2]], NT)
            chosen = dot(gsel[:, :lanes], w_ref[:, spots[1]], NT) + dot(gsel[:, lanes:], w_ref[:, spots[2]], NT)
            if quad == 0:
                gn_ref[...], gn_halo[...], gn_sel[...] = own, near, chosen
            else:
                gn_ref[...] += own
                gn_halo[...] += near
                gn_sel[...] += chosen
            cols = pl.ds(quad * lanes, lanes)
            own_vec[0:1, cols] = jnp.sum(gq.astype(F32), axis=0, keepdims=True)
            own_vec[1:2, cols] = (
                jnp.sum(gown[:, lanes:].astype(F32), axis=0, keepdims=True)
                + jnp.sum(ghalo[:, lanes:].astype(F32), axis=0, keepdims=True)
                + jnp.sum(gsel[:, lanes:].astype(F32), axis=0, keepdims=True)
            )
            return qkvs[quad]

        def give_back():
            porter.need(score_ref, tok_ref)
            score_now = score_ref[...].astype(F32)
            gscore = (gates[...] / (1.0 + jnp.exp(score_now))).astype(BF16)
            chosen = gn_sel[...] + dot(gscore[:, :heads], ws_ref[...])
            low = chosen.astype(BF16)
            for seq in range(seq_count):
                hot = hot_columns(selected_row(pick_ref, seq), ranks * cands)
                terms = dot(hot, low[seq * picks : (seq + 1) * picks]).astype(BF16)
                back_src[:, :, :, :, pl.ds(seq * cands, cands), :] = terms.reshape(lead + (cands, width))
                halo_src[seq] = gn_halo[pl.ds(seq * WIN, WIN), :].astype(BF16)
            for i, task in enumerate(backs):
                task.bind(mail, taken[id(task)], back_src, i * back_wide, column_writer(cand_ref, i * back_wide))

            def halo_write(value):
                back_ref[...] = value

            shift_task.bind(mail, taken[id(shift_task)], halo_src, before, halo_write)
            gain_row, shift_row = row(gain_ref), row(shift_ref)
            hat, root = norm_parts(tok_ref[...].astype(F32))

            def hat_of(ref):
                return (ref[...].astype(F32) - shift_row) / gain_row

            own, near = gn_ref[...], gn_halo[...]
            own_vec[2:3, :] = (
                jnp.sum(own * hat, axis=0, keepdims=True)
                + jnp.sum(near * hat_of(halo_ref), axis=0, keepdims=True)
                + jnp.sum(chosen * hat_of(nsel_ref), axis=0, keepdims=True)
            )
            own_vec[3:4, :] = (
                jnp.sum(own, axis=0, keepdims=True)
                + jnp.sum(near, axis=0, keepdims=True)
                + jnp.sum(chosen, axis=0, keepdims=True)
            )
            porter.need(gmid_ref)
            gn_ref[...] = gmid_ref[...] + norm_back(own, hat, root, gain_row)
            porter.ship(gn_ref, gn_far)
            own_vec[4 : vec_ref.shape[0], :] = vec_ref[4:, :]
            own_vec[vec_ref.shape[0] :, :] = dot(gscore, nsel_ref[...], TN)[:heads]

            def vec_write(value):
                total_ref[...] = value

            total.bind(mail, taken[id(total)], lambda: own_vec[...], vec_write)
            return [shift_task] + backs + [total]

        gates[...] = jnp.zeros_like(gates)
        half = blocks // 2
        begun = {"s": shift_task, "t": total, "o": out_task}
        work_of = {"o": out, "give": give_back}
        for i, task in enumerate(downs):
            begun[f"d{i}"], work_of[f"d{i}"] = task, lambda i=i: down(i)
        for i, task in enumerate(ups):
            begun[f"u{i}"], work_of[f"u{i}"] = task, lambda i=i: up(i)
        for i, task in enumerate(qkvs):
            begun[f"q{i}"], work_of[f"fin{i}"] = task, lambda i=i: finish_quad(i)
            work_of[f"q{i}a"] = lambda i=i: attend_back(i, 0, half)
            work_of[f"q{i}b"] = lambda i=i: attend_back(i, half, blocks)
        for i, task in enumerate(backs):
            begun[f"b{i}"] = task
        for entry in SCHEDULE:
            what, name = entry[0], entry[1:]
            if what == "c":
                work_of[name]()
            elif begun[name].stages:
                begun[name].stages.pop(0)()
        for task in tasks:
            while task.stages:
                task.stages.pop(0)()
        mail.finish()
        porter.finish()

    shapes = [
        ((share, 3 * width), F32),
        ((share, width), F32),
        ((share, hidden_size), F32),
        ((down_share, width), F32),
        ((every_row, width), F32),
        ((rows, width), F32),
        ((seq_count * cands, width), F32),
        ((seq_count, WIN, width), BF16),
    ]
    return pl.pallas_call(
        kernel,
        out_shape=[jax.ShapeDtypeStruct(*shape) for shape in shapes],
        in_specs=[WHOLE] * 5 + [FAR] * len(large),
        out_specs=[WHOLE] * 5 + [FAR] + [WHOLE] * 2,
        scratch_shapes=like(large)
        + [pltpu.SemaphoreType.DMA((len(large) + 1,))]
        + boxes
        + work
        + [pltpu.SemaphoreType.DMA((copies,)), pltpu.SemaphoreType.DMA((copies,))],
        compiler_params=pltpu.CompilerParams(
            collective_id=3, has_side_effects=True, vmem_limit_bytes=LIMIT
        ),
    )(score_rows, selected, gain, shift, vec, *large)


def ending(tokens, candidates, gain, base, cand_back, halo_back, total, sums, parts, heads, ranks):
    rows, width = tokens.shape
    seq_count, _, cands = candidates.shape
    tok = rows // seq_count
    share = width // ranks
    up_share = parts * share

    large = (tokens, base, *sums)
    alone = 8

    def kernel(cand_ref, gain_ref, back_ref, halo_ref, total_ref, *refs):
        far_in, refs = refs[: len(large)], refs[len(large) :]
        small_refs, refs = refs[:alone], refs[alone:]
        up_ref, score_ref, grad_far = refs[:3]
        far_out, refs = refs[3 : 3 + len(sums)], refs[3 + len(sums) :]
        near, sems = refs[: len(large)], refs[-1]
        tok_ref, grad_ref = near[:2]
        porter = Porter(sems, far_in, near)
        rank = lax.axis_index("seq")
        gain_row = row(gain_ref)
        values = total_ref[...]

        def pick(values, count, first):
            from_row = lax.broadcasted_iota(jnp.int32, (width, count), 0)
            to_col = lax.broadcasted_iota(jnp.int32, (width, count), 1)
            hot = jnp.where(from_row == to_col + first, 1.0, 0.0)
            return lax.dot_general(
                values, hot, (((1,), (0,)), ((), ())),
                precision=lax.Precision.HIGHEST, preferred_element_type=F32,
            )

        small = pick(values, share, rank * share)
        for i in range(alone):
            small_refs[i][...] = small[i]
        score_ref[...] = small[alone + parts :]
        per_row = width // up_share
        ups = pick(values[alone : alone + parts], up_share, lax.rem(rank, per_row) * up_share)
        which = lax.broadcasted_iota(jnp.int32, ups.shape, 0)
        up_ref[...] = jnp.sum(jnp.where(which == lax.div(rank, per_row), ups, 0.0), axis=0)
        porter.need(tok_ref)

        def returned(rows_in, grad):
            hat, root = norm_parts(rows_in)
            return norm_back(grad, hat, root, gain_row)

        for seq in range(seq_count):
            here = pl.ds(seq * tok, tok)
            hot = hot_columns(cand_ref[seq, pl.ds(rank, 1), :], tok)
            chosen = dot(hot, tok_ref[here, :], TN)
            came = returned(chosen, back_ref[pl.ds(seq * cands, cands), :]).astype(BF16)
            edge = pl.ds((seq + 1) * tok - WIN, WIN)
            near_rows = returned(tok_ref[edge, :].astype(F32), halo_ref[seq].astype(F32))
            if seq == 0:
                porter.need(grad_ref)
            grad_ref[here, :] += dot(hot, came)
            grad_ref[edge, :] += near_rows
            porter.ship(grad_ref.at[here, :], grad_far.at[here, :])
            if seq == 0:
                for came, result in zip(near[2:], far_out):
                    porter.need(came)
                    porter.ship(came, result)
        porter.finish()

    results = [jax.ShapeDtypeStruct((share,), F32)] * alone + [
        jax.ShapeDtypeStruct((up_share,), F32),
        jax.ShapeDtypeStruct((heads, share), F32),
        jax.ShapeDtypeStruct((rows, width), F32),
    ]
    return pl.pallas_call(
        kernel,
        out_shape=results + [jax.ShapeDtypeStruct(array.shape, array.dtype) for array in sums],
        in_specs=[WHOLE] * 5 + [FAR] * len(large),
        out_specs=[WHOLE] * (alone + 2) + [FAR] * (1 + len(sums)),
        scratch_shapes=like(large)
        + [pltpu.SemaphoreType.DMA((len(large) + seq_count + len(sums),))],
        compiler_params=pltpu.CompilerParams(vmem_limit_bytes=LIMIT),
    )(candidates, gain, cand_back, halo_back, total, *large)


def per_device(
    tokens,
    weight_qkv,
    bias_query,
    bias_value,
    weight_score,
    weight_out,
    bias_out,
    gain_one,
    shift_one,
    gain_two,
    shift_two,
    weight_up,
    bias_up,
    weight_down,
    bias_down,
    cotangent,
    lengths,
    candidates,
    selected,
):
    seq_count, tok, width = tokens.shape
    heads = weight_score.shape[1]
    head_size = width // heads
    rows = seq_count * tok
    ranks = lax.axis_size("seq")
    place = Place(ranks, lax.axis_size("grp"))
    parts = bias_up.shape[0] // width
    flat = tokens.reshape(rows, width)
    dy = cotangent.reshape(rows, width)
    (
        normed, queries, ext, halo, nsel, ksel, score,
        attended, probs, mixed, hidden, gpre, n2, branch, grad_middle, gatt, vec,
    ) = front(
        place, lengths, flat, candidates, selected, (gain_one, shift_one), (gain_two, shift_two),
        (bias_query, bias_value, bias_out, bias_up, bias_down), weight_score.T,
        weight_qkv, dy, weight_down, weight_out, weight_up,
    )
    grad_qkv, grad_out, grad_up, grad_down, total, base, cand_back, halo_back = closing(
        place,
        (hidden, dy, gpre, n2, branch, attended),
        (queries, ext, ksel, probs, score, gatt, normed, halo, nsel),
        weight_qkv, weight_score.T, selected, gain_one, shift_one, flat, grad_middle, vec, head_size,
    )
    results = ending(
        flat, candidates, gain_one, base, cand_back, halo_back, total,
        (grad_qkv, grad_out, grad_up, grad_down), parts, heads, ranks,
    )
    small, (up_row, score_rows, grad_tokens), sums = results[:8], results[8:11], results[11:]
    grad_qkv, grad_out, grad_up, grad_down = sums
    return (
        mixed.reshape(tokens.shape),
        grad_tokens.reshape(tokens.shape),
        grad_qkv,
        small[0],
        small[1],
        score_rows.T,
        grad_out,
        small[4],
        small[2],
        small[3],
        small[5],
        small[6],
        grad_up,
        up_row,
        grad_down,
        small[7],
    )


def solution(mesh):
    return jax.shard_map(
        per_device,
        mesh=mesh,
        in_specs=(
            P("grp", "seq", None),
            P(),
            P(),
            P(),
            P(),
            P(),
            P(),
            P(),
            P(),
            P(),
            P(),
            P(),
            P(),
            P(),
            P(),
            P("grp", "seq", None),
            P("grp"),
            P("grp", None, None),
            P("grp", "seq", None),
        ),
        out_specs=(
            P("grp", "seq", None),
            P("grp", "seq", None),
            P("seq", None),
            P("seq"),
            P("seq"),
            P("seq", None),
            P("seq", None),
            P("seq"),
            P("seq"),
            P("seq"),
            P("seq"),
            P("seq"),
            P("seq", None),
            P("seq"),
            P("seq", None),
            P("seq"),
        ),
        check_vma=False,
    )
```
